32 devices in a mesh: cond: 4 (over x, core), slab: 8 (over z, y).
Axes of the slice: x: 2, y: 2, z: 4, core: 2. Of those that a mesh axis runs over, the one named last changes fastest.
Arguments:
- adjoint: float32 [4, 32, 512, 128], P('cond', 'slab'), may hold values from -6 to 6
- phase: bfloat16 [4, 32, 512, 128], P('cond', 'slab'), may hold values from -1.09375 to 1.09375
- targets: bfloat16 [4, 256, 128], P('cond', 'slab'), may hold values from -1 to 1
- owners: int32 [4, 256, 1], P('cond', 'slab'), may hold values from 0 to 7; in each aligned block of 32 rows (0 to 31, 32 to 63, ..., all dimensions but the last counted through in order) at most 8 rows name the same one
- target_cell: int32 [4, 256], P('cond', 'slab'), may hold values from 0 to 2047
- rate_index: int32 [4], P('cond'), may hold values from 0 to 7
- inflow_rates: float32 [8], replicated, may hold values from 0.5 to 2
- wall_mask: int32 [2, 32, 512], P(None, 'slab'), may hold values 0 or 1
Outputs:
- adjoint_out: float32 [4, 32, 512, 128], P('cond', 'slab')
- wall_gradient: float32 [2, 32, 512], P(None, 'slab')
The draws below stay inside these ranges and needn't reach their ends.
Inputs may be any that keep to these rules, and one draw needn't show every extreme that they name: `owners`: within each aligned block of 32 rows, no slab is named by more than 8 rows.
All inputs are finite; a program needn't handle non-finite values. No bound on the sum of `wall_mask` on one device may be relied on, other than what follows from the above.
Results may differ from the reference program's by a relative error of at most 0.0003.
Values may be sent and summed in bfloat16 or wider, within the bound.
No kernel may reach another device: no remote copies, remote signals or barrier semaphores. Data moves between devices by JAX's collectives and lax.ppermute only.
A program may use at most 64 MiB of HBM per device.

```python
import math
import jax
import jax.numpy as jnp
import numpy as np
from jax import lax

CX = 4
NY = 512
NZ = 128
R_DEV = 32
NRATES = 8
NX = 32
NCOND = 4
NTGT = 256
CAP = 8
N_SLAB = 8


def with_ends(entries, own_key, smallest, high):
    place = [jax.random.randint(jax.random.fold_in(own_key, axis), (), 0, length) for axis, length in enumerate(entries.shape)]
    longest = entries.shape.index(max(entries.shape))
    next_to = place[:longest] + [(place[longest] + 1) % entries.shape[longest]] + place[longest + 1:]
    return entries.at[tuple(place)].set(smallest).at[tuple(next_to)].set(high)


def block_levels(rng, extent, shards, least, largest):
    factor_of = 1.0
    for position, parts in shards:
        heights = jax.random.uniform(jax.random.fold_in(jax.random.fold_in(rng, 6), position), (parts,), jnp.float32, least / len(shards), largest / len(shards))
        factor_of = factor_of * jnp.repeat(jnp.exp(heights), extent[position] // parts).reshape((-1,) + (1,) * (len(extent) - 1 - position))
    return factor_of


def routed_block(key, own, number, rows, number_of, top, bound, slope):
    order = jax.random.permutation(key, number_of)
    crowded, ordinary = shares(number_of, rows * top, bound, slope, True), shares(number_of, rows * top, bound, slope, False)
    places = jnp.arange(number_of)

    def named(tallies, rotation):
        used = int((tallies > 0).sum())
        fixed = max(1, used // 4)
        passed = fixed + (places - fixed + rotation * (used - fixed)) % max(1, number_of - fixed)
        return jnp.zeros((number_of,), jnp.int32).at[order[jnp.where(places < fixed, places, passed)]].set(jnp.asarray(tallies, jnp.int32))

    tallies = jnp.where(number % 4 == 0, named(crowded, number // 4), named(ordinary, number - number // 4 - 1))
    mixed = jax.random.permutation(jax.random.fold_in(own, 3), number_of)
    donor, receiver = mixed[0:number_of // 2 * 2:2], mixed[1:number_of // 2 * 2:2]
    margin = jnp.minimum(tallies[donor] - 1, bound - tallies[receiver]) // 2
    margin = jnp.where((donor == order[0]) | (receiver == order[0]) | (tallies[receiver] == 0), 0, jnp.maximum(margin, 0))
    passed = jax.random.randint(jax.random.fold_in(own, 4), (number_of // 2,), 0, 1 << 20) % (margin + 1)
    tallies = tallies.at[donor].add(-passed).at[receiver].add(passed)
    items = jnp.searchsorted(jnp.cumsum(tallies), jnp.arange(rows * top), side="right").astype(jnp.int32)
    listing = items.reshape(top, rows).T
    listing = listing[jax.random.permutation(jax.random.fold_in(own, 1), rows)]
    rotation = jax.random.randint(jax.random.fold_in(own, 2), (rows, 1), 0, top)
    return jnp.take_along_axis(listing, (jnp.arange(top)[None, :] + rotation) % top, axis=1)


def shares(amount, total, limit, lean, full):
    portions = [(1 << 20) // math.isqrt(grade ** lean) + 1 for grade in range(1, amount + 1)]
    largest = limit if full else min(limit, max(-(-total // amount), total * portions[0] // sum(portions)))
    least = 1 if total - largest >= amount - 1 else 0
    holding, rest = [largest] + [least] * (amount - 1), total - largest - least * (amount - 1)
    while rest > 0:
        candidates = [i for i in range(1, amount) if holding[i] < largest] or [i for i in range(1, amount) if holding[i] < limit]
        mass, remaining = sum([portions[i] for i in candidates]), rest
        for i in candidates:
            extra = min(limit - holding[i], max(1, remaining * portions[i] // mass), rest)
            holding[i] = holding[i] + extra
            rest = rest - extra
    return np.array(holding)


def bell_draw(rng, dims, spread, most, split=(), dtype=jnp.bfloat16):
    drawn = jax.random.normal(rng, dims, jnp.float32) * spread
    if len(split) > 0:
        drawn = block_levels(rng, dims, split, -0.22, 0.18) * drawn
    return jnp.clip(drawn, min=-most, max=most).astype(dtype)


def setup_inputs(seed: int = 0) -> dict:
    arg_keys = jax.random.split(jax.random.key(seed), 9)
    adjoint = bell_draw(arg_keys[0], (NCOND, NX, NY, NZ), 1.0, 6.0, ((0, 4), (1, 8)), jnp.float32)
    phase = jnp.clip(jax.random.uniform(arg_keys[1], (NCOND, NX, NY, NZ), jnp.float32, -1.09375, 1.09375) * block_levels(arg_keys[1], (NCOND, NX, NY, NZ), ((0, 4), (1, 8)), -0.4, 0.0), -1.09375, 1.09375).astype(jnp.bfloat16)
    targets = jnp.clip(jax.random.uniform(arg_keys[2], (NCOND, NTGT, NZ), jnp.float32, -1.0, 1.0) * block_levels(arg_keys[2], (NCOND, NTGT, NZ), ((0, 4), (1, 8)), -0.4, 0.0), -1.0, 1.0).astype(jnp.bfloat16)
    owners_keys = jax.random.split(jax.random.fold_in(arg_keys[3], 1), NCOND * NTGT // R_DEV)
    owners_turns = jax.random.permutation(jax.random.fold_in(arg_keys[3], 3), NCOND * NTGT // R_DEV)
    owners = jax.vmap(lambda own, number: routed_block(jax.random.fold_in(arg_keys[3], 2), own, number, R_DEV, N_SLAB, 1, CAP, 2))(owners_keys, owners_turns).reshape((NCOND, NTGT, 1))
    target_cell = with_ends(jax.random.randint(arg_keys[4], (NCOND, NTGT), 0, CX * NY), jax.random.fold_in(arg_keys[4], 1), 0, (CX * NY) - 1).astype(jnp.int32)
    rate_index = with_ends(jax.random.randint(arg_keys[5], (NCOND,), 0, NRATES), jax.random.fold_in(arg_keys[5], 1), 0, NRATES - 1).astype(jnp.int32)
    inflow_rates = jnp.clip(jnp.exp(jax.random.uniform(arg_keys[6], (NRATES,), jnp.float32, math.log(0.5), math.log(2.0))), 0.5, 2.0)
    wall_mask = with_ends((jax.random.randint(arg_keys[7], (2, NX, NY), 0, 2) < 1).astype(jnp.int32), jax.random.fold_in(arg_keys[7], 1), 0, 1)
    return dict(adjoint=adjoint, phase=phase, targets=targets, owners=owners, target_cell=target_cell, rate_index=rate_index, inflow_rates=inflow_rates, wall_mask=wall_mask)


mobility_step = 0.02
stiffness_step = 0.01
transport_step = 0.125
wall_weight = 0.25


def inner_laplacian(field):
    center = field[1:-1]
    along_y = jnp.pad(center, ((0, 0), (1, 1), (0, 0)))
    along_z = jnp.pad(center, ((0, 0), (0, 0), (1, 1)))
    return (field[2:] + field[:-2] + along_y[:, 2:] + along_y[:, :-2]
            + along_z[:, :, 2:] + along_z[:, :, :-2] - 6.0 * center)


def within_grid(length, first_row, grid_rows):
    placed = first_row + jnp.arange(length)
    within = (placed >= 0) & (placed < grid_rows)
    return within.astype(jnp.float32)[:, None, None]


def adjoint_step(extended, curvature, inflow, first_row, grid_rows):
    length = extended.shape[0]
    first_lap = inner_laplacian(extended) * within_grid(length - 2, first_row + 1, grid_rows)
    second_lap = inner_laplacian(first_lap)
    center = extended[2:-2]
    column_depth = extended.shape[2]
    height = (jnp.arange(column_depth).astype(jnp.float32) + 0.5) / column_depth
    profile = 4.0 * height * (1.0 - height)
    padded = jnp.pad(center, ((0, 0), (1, 1), (0, 0)))
    transport = (padded[:, 2:] - padded[:, :-2]) * profile
    updated = (center + mobility_step * curvature * first_lap[1:-1]
               - stiffness_step * second_lap + transport_step * inflow * transport)
    return updated * within_grid(length - 4, first_row + 2, grid_rows)


def wall_term(state, phase32, wall_mask):
    lower_wall = (1.0 - phase32[:, :, 0] ** 2) * state[:, :, 0]
    upper_wall = (1.0 - phase32[:, :, -1] ** 2) * state[:, :, -1]
    return wall_weight * wall_mask.astype(jnp.float32) * jnp.stack([lower_wall, upper_wall])


def one_condition(adjoint_now, phase_now, target_rows, owner_rows, cell_rows, inflow, wall_mask):
    phase32 = phase_now.astype(jnp.float32)
    curvature = 3.0 * phase32 * phase32 - 1.0
    grid_rows = adjoint_now.shape[0]
    state = adjoint_now
    gradient = jnp.zeros(wall_mask.shape, jnp.float32)
    for sweep in range(2):
        extended = jnp.pad(state, ((2, 2), (0, 0), (0, 0)))
        state = adjoint_step(extended, curvature, inflow, -2, grid_rows)
        gradient = gradient + wall_term(state, phase32, wall_mask)
    row_index = (owner_rows[:, 0].astype(jnp.int32) * (CX * NY) + cell_rows.astype(jnp.int32)).astype(jnp.int32)
    flat_phase = phase32.reshape(-1, NZ)
    source = flat_phase[row_index] - target_rows.astype(jnp.float32)
    state = state.reshape(-1, NZ).at[row_index].add(source).reshape(state.shape)
    return state, gradient


def reference(adjoint, phase, targets, owners, target_cell, rate_index, inflow_rates, wall_mask):
    def per_condition(running, members):
        adjoint_now, phase_now, target_rows, owner_rows, cell_rows, chosen = members
        inflow = inflow_rates[chosen]
        state, gradient = one_condition(adjoint_now, phase_now, target_rows, owner_rows, cell_rows, inflow, wall_mask)
        return running + gradient, state
    initial = jnp.zeros(wall_mask.shape, jnp.float32)
    gradient, states = lax.scan(per_condition, initial, (adjoint, phase, targets, owners, target_cell, rate_index))
    return states, gradient
```

```python
import jax
import jax.numpy as jnp
from jax import lax
from jax.experimental import pallas as pl
from jax.experimental.pallas import tpu as pltpu
from jax.sharding import PartitionSpec as P

mobility_step = 0.02
stiffness_step = 0.01
transport_step = 0.125
wall_weight = 0.25

f32 = jnp.float32
bf16 = jnp.bfloat16
CHUNK = 64
PAD = 8
ANY = pl.BlockSpec(memory_space=pl.ANY)
VMEM = pl.BlockSpec(memory_space=pltpu.VMEM)
SMEM = pl.BlockSpec(memory_space=pltpu.SMEM)


def cost(flops, nbytes):
    return pl.CostEstimate(flops=flops, bytes_accessed=nbytes, transcendentals=0)


def call(kernel, outs, out_specs, in_specs, scratch, estimate, aliases=None):
    return pl.pallas_call(
        kernel,
        out_shape=outs,
        out_specs=out_specs,
        in_specs=in_specs,
        scratch_shapes=scratch,
        input_output_aliases=aliases or {},
        cost_estimate=estimate,
        compiler_params=pltpu.CompilerParams(vmem_limit_bytes=24 * 1024 * 1024),
    )


def starts(rows):
    return range(0, rows, CHUNK)


def read(ref, lead, y, shift=0):
    return ref[(*lead, pl.ds(PAD + y + shift, CHUNK), slice(None))]


def z_sum(v):
    depth = v.shape[1]
    lane = lax.broadcasted_iota(jnp.int32, v.shape, 1)
    below = jnp.where(lane == 0, 0.0, pltpu.roll(v, 1, 1))
    above = jnp.where(lane == depth - 1, 0.0, pltpu.roll(v, depth - 1, 1))
    return below + above


def plane_part(ref, lead, y):
    v = read(ref, lead, y)
    return read(ref, lead, y, 1) + read(ref, lead, y, -1) + z_sum(v) - 6.0 * v


def clear_margins(ref, lead, rows):
    zero = jnp.zeros((PAD, ref.shape[-1]), f32)
    ref[(*lead, pl.ds(0, PAD), slice(None))] = zero
    ref[(*lead, pl.ds(PAD + rows, PAD), slice(None))] = zero


def oriented(depth_from_a, layers):
    odd = lax.rem(lax.axis_index("slab"), 2)
    return jnp.where(odd == 1, depth_from_a, layers - 1 - depth_from_a)


def fetch(pairs, sems):
    copies = [pltpu.make_async_copy(s, d, sems.at[i]) for i, (s, d) in enumerate(pairs)]
    for c in copies:
        c.start()
    for c in copies:
        c.wait()


def write_message(near, far, missing, out):
    rows = far.shape[0] - 2 * PAD
    clear_margins(missing, (), rows)
    for y in starts(rows):
        v = read(near, (), y)
        rounded = v.astype(bf16)
        out[pl.ds(y, CHUNK), :] = rounded
        missing[pl.ds(PAD + y, CHUNK), :] = v - rounded.astype(f32)
    for y in starts(rows):
        out[pl.ds(rows + y, CHUNK), :] = (read(far, (), y) + 2.0 * plane_part(missing, (), y)).astype(bf16)


def first_message(side, adjoint, out, near, far, missing, sems):
    layers = adjoint.shape[0]
    rows = adjoint.shape[1]
    one, two = (0, 1) if side == 0 else (layers - 1, layers - 2)
    fetch(
        [
            (adjoint.at[oriented(one, layers)], near.at[pl.ds(PAD, rows)]),
            (adjoint.at[oriented(two, layers)], far.at[pl.ds(PAD, rows)]),
        ],
        sems,
    )
    write_message(near, far, missing, out)


def make_first_message(adjoint, side):
    layers, rows, depth = adjoint.shape
    padded = pltpu.VMEM((rows + 2 * PAD, depth), f32)
    return call(
        lambda *refs: first_message(side, *refs),
        jax.ShapeDtypeStruct((2 * rows, depth), bf16),
        VMEM,
        [ANY],
        [padded, padded, padded, pltpu.SemaphoreType.DMA((2,))],
        cost(20 * rows * depth, 12 * rows * depth),
    )(adjoint)


def local_step(state, first, phase, inflow, count, emit):
    layers = state.shape[0]
    rows = state.shape[1] - 2 * PAD
    depth = state.shape[2]
    position = lax.axis_index("slab")
    low = jnp.where(position > 0, 1.0, 0.0).astype(f32)
    high = jnp.where(position < count - 1, 1.0, 0.0).astype(f32)
    lane = lax.broadcasted_iota(jnp.int32, (1, depth), 1)
    height = (lane.astype(f32) + 0.5) / depth
    transport = (transport_step * inflow) * (4.0 * height * (1.0 - height))
    for l in range(layers):
        for y in starts(rows):
            lap = plane_part(state, (l,), y)
            if l > 0:
                lap = lap + read(state, (l - 1,), y)
            if l < layers - 1:
                lap = lap + read(state, (l + 1,), y)
            first[l, pl.ds(PAD + y, CHUNK), :] = lap
    for l in range(layers):
        for y in starts(rows):
            v = read(state, (l,), y)
            lap = read(first, (l,), y)
            second = plane_part(first, (l,), y)
            second = second + (read(first, (l - 1,), y) if l > 0 else low * v)
            second = second + (read(first, (l + 1,), y) if l < layers - 1 else high * v)
            p = phase[l, pl.ds(y, CHUNK), :].astype(f32)
            curvature = 3.0 * p * p - 1.0
            moved = read(state, (l,), y, 1) - read(state, (l,), y, -1)
            emit(l, y, v, v + mobility_step * curvature * lap - stiffness_step * second + transport * moved, p)


def load_state(source, state, first, sems):
    layers, rows, _ = source.shape
    copies = [
        pltpu.make_async_copy(source.at[l], state.at[l, pl.ds(PAD, rows)], sems.at[l]) for l in range(layers)
    ]
    for c in copies:
        c.start()
    for l in range(layers):
        clear_margins(state, (l,), rows)
        clear_margins(first, (l,), rows)
    for c in copies:
        c.wait()


def first_local(count, adjoint, phase, rates, choice, out, state, first, sems):
    load_state(adjoint, state, first, sems)

    def emit(l, y, v, stepped, p):
        out[l, pl.ds(y, CHUNK), :] = stepped

    local_step(state, first, phase, rates[choice[0]], count, emit)


def make_first_local(adjoint, phase, rates, choice, count):
    layers, rows, depth = adjoint.shape
    padded = pltpu.VMEM((layers, rows + 2 * PAD, depth), f32)
    return call(
        lambda *refs: first_local(count, *refs),
        jax.ShapeDtypeStruct(adjoint.shape, f32),
        VMEM,
        [ANY, VMEM, SMEM, SMEM],
        [padded, padded, pltpu.SemaphoreType.DMA((layers,))],
        cost(60 * layers * rows * depth, 10 * layers * rows * depth),
    )(adjoint, phase, rates, choice)


def add_halo(message, edge, inner, halo, phase, rows, put_edge, put_inner):
    clear_margins(halo, (), rows)
    for y in starts(rows):
        halo[pl.ds(PAD + y, CHUNK), :] = message[pl.ds(y, CHUNK), :].astype(f32)
    for y in starts(rows):
        near = read(halo, (), y)
        far = message[pl.ds(rows + y, CHUNK), :].astype(f32)
        p = phase[pl.ds(y, CHUNK), :].astype(f32)
        curvature = 3.0 * p * p - 1.0
        both = far + 2.0 * plane_part(halo, (), y)
        put_edge(y, edge(y) + mobility_step * curvature * near - stiffness_step * both)
        put_inner(y, inner(y) - stiffness_step * near)


def wall_rows(v, first_row):
    depth = v.shape[1]
    row = lax.broadcasted_iota(jnp.int32, (8, depth), 0) - first_row
    lane = lax.broadcasted_iota(jnp.int32, (8, depth), 1)
    pick = ((row == 0) & (lane == 0)) | ((row == 1) & (lane == depth - 1))
    pick = jnp.where(pick, 1.0, 0.0).astype(bf16)

    def part(w):
        return lax.dot_general(pick, w, (((1,), (1,)), ((), ())), preferred_element_type=f32)

    if v.dtype == bf16:
        return part(v)
    high = v.astype(bf16)
    rest = v - high.astype(f32)
    middle = rest.astype(bf16)
    low = (rest - middle.astype(f32)).astype(bf16)
    return part(high) + part(middle) + part(low)


def middle(side, message, pre, phase, out, sent, wall, edge, inner, halo, curved, missing, sems):
    layers, rows, depth = pre.shape
    one, two = (0, 1) if side == 0 else (layers - 1, layers - 2)
    fetch(
        [
            (pre.at[oriented(one, layers)], edge.at[pl.ds(PAD, rows)]),
            (pre.at[oriented(two, layers)], inner.at[pl.ds(PAD, rows)]),
            (phase.at[oriented(one, layers)], curved),
        ],
        sems,
    )
    clear_margins(edge, (), rows)

    def put_edge(y, v):
        edge[pl.ds(PAD + y, CHUNK), :] = v
        out[0, pl.ds(y, CHUNK), :] = v

    def put_inner(y, v):
        inner[pl.ds(PAD + y, CHUNK), :] = v
        out[1, pl.ds(y, CHUNK), :] = v

    add_halo(
        message, lambda y: read(edge, (), y), lambda y: read(inner, (), y), halo, curved, rows, put_edge, put_inner
    )
    write_message(edge, inner, missing, sent)
    for y in range(0, rows, 128):
        both = [read(inner, (), y + k) + 2.0 * plane_part(edge, (), y + k) for k in range(0, 128, CHUNK)]
        near = [read(edge, (), y + k) for k in range(0, 128, CHUNK)]
        wall[:, pl.ds(y, 128)] = wall_rows(jnp.concatenate(near), 0) + wall_rows(jnp.concatenate(both), 2)


def make_middle(message, pre, phase, side):
    layers, rows, depth = pre.shape
    padded = pltpu.VMEM((rows + 2 * PAD, depth), f32)
    return call(
        lambda *refs: middle(side, *refs),
        (
            jax.ShapeDtypeStruct((2, rows, depth), f32),
            jax.ShapeDtypeStruct((2 * rows, depth), bf16),
            jax.ShapeDtypeStruct((8, rows), f32),
        ),
        (VMEM, VMEM, VMEM),
        [VMEM, ANY, ANY],
        [padded, padded, padded, pltpu.VMEM((rows, depth), bf16), padded, pltpu.SemaphoreType.DMA((3,))],
        cost(60 * rows * depth, 30 * rows * depth),
    )(message, pre, phase)


def second_local(count, side_a, side_b, phase, rates, choice, index, listed, out, wall, phase_wall, state, first, sems):
    layers, rows, depth = out.shape
    pairs = []
    for i, ref in enumerate((side_a, side_b)):
        for j in range(2):
            depth_from_a = j if i == 0 else layers - 1 - j
            pairs.append((ref.at[j], state.at[oriented(depth_from_a, layers), pl.ds(PAD, rows)]))
    copies = [pltpu.make_async_copy(s, d, sems.at[i]) for i, (s, d) in enumerate(pairs)]
    for c in copies:
        c.start()
    for l in range(layers):
        clear_margins(state, (l,), rows)
        clear_margins(first, (l,), rows)
    total = index.shape[1]
    rhs = jnp.concatenate([jnp.ones((total, depth), bf16), listed[...]], axis=1)
    for l in range(layers):
        for y in range(0, rows, 128):
            cell = lax.broadcasted_iota(jnp.int32, (128, total), 0) + (l * rows + y)
            here = jnp.where(cell == index[...], 1.0, 0.0).astype(bf16)
            added = jnp.dot(here, rhs, preferred_element_type=f32)
            p = phase[l, pl.ds(y, 128), :].astype(f32)
            out[l, pl.ds(y, 128), :] = added[:, :depth] * p - added[:, depth:]
            phase_wall[l, :, pl.ds(y, 128)] = wall_rows(phase[l, pl.ds(y, 128), :], 0)
    for c in copies:
        c.wait()
    held = []

    def emit(l, y, v, stepped, p):
        out[l, pl.ds(y, CHUNK), :] += stepped
        held.append(v + stepped)
        if len(held) * CHUNK == 128:
            wall[l, :, pl.ds(y + CHUNK - 128, 128)] = wall_rows(jnp.concatenate(held), 0)
            held.clear()

    local_step(state, first, phase, rates[choice[0]], count, emit)


def make_second_local(side_a, side_b, phase, rates, choice, index, listed, count):
    layers, rows, depth = phase.shape
    padded = pltpu.VMEM((layers, rows + 2 * PAD, depth), f32)
    return call(
        lambda *refs: second_local(count, *refs),
        (
            jax.ShapeDtypeStruct((layers, rows, depth), f32),
            jax.ShapeDtypeStruct((layers, 8, rows), f32),
            jax.ShapeDtypeStruct((layers, 8, rows), f32),
        ),
        (VMEM, VMEM, VMEM),
        [ANY, ANY, VMEM, SMEM, SMEM, VMEM, VMEM],
        [padded, padded, pltpu.SemaphoreType.DMA((4,))],
        cost(120 * layers * rows * depth, 10 * layers * rows * depth),
    )(side_a, side_b, phase, rates, choice, index, listed)


def wall_kernel(wall, phase_wall, from_a, from_b, mask, out):
    layers = wall.shape[0]
    odd = lax.rem(lax.axis_index("slab"), 2) == 1
    low = jnp.where(odd, from_a[...], from_b[...])
    high = jnp.where(odd, from_b[...], from_a[...])
    for l in range(layers):
        p = phase_wall[l, :2, :]
        w = wall[l, :2, :]
        curvature = 3.0 * p * p - 1.0
        for halo, far_off in ((low, l), (high, layers - 1 - l)):
            if far_off == 0:
                w = w + mobility_step * curvature * halo[:2] - stiffness_step * halo[2:4]
            elif far_off == 1:
                w = w - stiffness_step * halo[:2]
        m = mask[:, l, :].astype(f32)
        out[:, l, :] = wall_weight * m * (1.0 - p * p) * w


def make_walls(wall, phase_wall, from_a, from_b, mask):
    return call(
        wall_kernel,
        jax.ShapeDtypeStruct(mask.shape, f32),
        VMEM,
        [VMEM] * 5,
        [],
        cost(40 * mask.size, 20 * mask.size),
    )(wall, phase_wall, from_a, from_b, mask)


def final(side, message, pre, phase, out, edge, inner, halo, curved, sems, out_sems):
    layers, rows, depth = pre.shape
    one, two = (0, 1) if side == 0 else (layers - 1, layers - 2)
    one, two = oriented(one, layers), oriented(two, layers)
    fetch([(pre.at[one], edge), (pre.at[two], inner), (phase.at[one], curved)], sems)

    def put_edge(y, v):
        edge[pl.ds(y, CHUNK), :] = v

    def put_inner(y, v):
        inner[pl.ds(y, CHUNK), :] = v

    add_halo(
        message,
        lambda y: edge[pl.ds(y, CHUNK), :],
        lambda y: inner[pl.ds(y, CHUNK), :],
        halo,
        curved,
        rows,
        put_edge,
        put_inner,
    )
    fetch([(edge, out.at[one]), (inner, out.at[two])], out_sems)


def make_final(message, pre, phase, side):
    layers, rows, depth = pre.shape
    plane = pltpu.VMEM((rows, depth), f32)
    return call(
        lambda *refs: final(side, *refs),
        jax.ShapeDtypeStruct(pre.shape, f32),
        ANY,
        [VMEM, ANY, ANY],
        [
            plane,
            plane,
            pltpu.VMEM((rows + 2 * PAD, depth), f32),
            pltpu.VMEM((rows, depth), bf16),
            pltpu.SemaphoreType.DMA((3,)),
            pltpu.SemaphoreType.DMA((2,)),
        ],
        cost(30 * rows * depth, 20 * rows * depth),
        aliases={1: 0},
    )(message, pre, phase)


def gather_rows(block, count):
    if count != 8:
        return lax.all_gather(block, "slab", axis=0)
    parts = block[None]
    for k in (1, 2, 4):
        parts = jnp.concatenate([parts, lax.ppermute(parts, "slab", [(i, i ^ k) for i in range(count)])])
    return parts


def total_over(g, axis):
    if lax.axis_size(axis) != 4:
        return lax.psum(g, axis)
    others = [lax.ppermute(g, axis, [(i, i ^ k) for i in range(4)]) for k in (1, 2, 3)]
    return (g + others[0]) + (others[1] + others[2])


def on_device(adjoint, phase, targets, owners, target_cell, rate_index, inflow_rates, wall_mask):
    state, phase = adjoint[0], phase[0]
    rows, depth = state.shape[1:]
    count = lax.axis_size("slab")
    position = lax.axis_index("slab")
    pairs = (
        [(i, i ^ 1) for i in range(count)],
        [(i, i + 1) for i in range(1, count - 1, 2)] + [(i + 1, i) for i in range(1, count - 1, 2)],
    )

    def send(v, side):
        return lax.ppermute(v, "slab", pairs[side])

    arrived = [send(make_first_message(state, side), side) for side in (0, 1)]

    cells = target_cell[0]
    digits = jnp.stack([owners[0, :, 0], cells // 256, cells % 256])
    digits = jnp.pad(digits, ((0, 13), (0, depth - digits.shape[1]))).astype(bf16)
    gathered = gather_rows(jnp.concatenate([targets[0], digits], axis=0), count)
    n = targets.shape[1]
    listed = gathered[:, :n].reshape(-1, depth)
    codes = gathered[:, n : n + 3, :n].astype(jnp.int32)
    index = jnp.where(codes[:, 0] == position, codes[:, 1] * 256 + codes[:, 2], -1).reshape(1, -1)

    pre = make_first_local(state, phase, inflow_rates, rate_index, count)
    halves, walls, later = [], [], []
    for side in (0, 1):
        half, message, wall = make_middle(arrived[side], pre, phase, side)
        halves.append(half)
        walls.append(send(wall, side))
        later.append(send(message, side))
    pre, wall, phase_wall = make_second_local(*halves, phase, inflow_rates, rate_index, index, listed, count)
    wall_gradient = total_over(make_walls(wall, phase_wall, *walls, wall_mask), "cond")
    for side in (0, 1):
        pre = make_final(later[side], pre, phase, side)
    return pre[None], wall_gradient


def solution(mesh):
    in_specs = (
        P("cond", "slab", None, None),
        P("cond", "slab", None, None),
        P("cond", "slab", None),
        P("cond", "slab", None),
        P("cond", "slab"),
        P("cond"),
        P(),
        P(None, "slab", None),
    )
    out_specs = (P("cond", "slab", None, None), P(None, "slab", None))
    return jax.shard_map(
        on_device, mesh=mesh, in_specs=in_specs, out_specs=out_specs, check_vma=False
    )
```

```python
import jax
import jax.numpy as jnp
from jax import lax
from jax.experimental import pallas as pl
from jax.experimental.pallas import tpu as pltpu
from jax.sharding import PartitionSpec as P

mobility_step = 0.02
stiffness_step = 0.01
transport_step = 0.125
wall_weight = 0.25

f32 = jnp.float32
bf16 = jnp.bfloat16
CHUNK = 64
LARGE = 56
PAD = 8
ANY = pl.BlockSpec(memory_space=pl.ANY)
HBM = pl.BlockSpec(memory_space=pltpu.HBM)
VMEM = pl.BlockSpec(memory_space=pltpu.VMEM)
SMEM = pl.BlockSpec(memory_space=pltpu.SMEM)


def cost(flops, nbytes):
    return pl.CostEstimate(flops=10**10, bytes_accessed=10**8, transcendentals=0)


def call(kernel, outs, out_specs, in_specs, scratch, estimate, aliases=None, limit=12):
    return pl.pallas_call(
        kernel,
        out_shape=outs,
        out_specs=out_specs,
        in_specs=in_specs,
        scratch_shapes=scratch,
        input_output_aliases=aliases or {},
        cost_estimate=estimate,
        compiler_params=pltpu.CompilerParams(vmem_limit_bytes=limit * 1024 * 1024),
    )


def starts(rows):
    return range(0, rows, CHUNK)


def read(layer, y, shift=0):
    ref, lead = layer
    return ref[(*lead, pl.ds(PAD + y + shift, CHUNK), slice(None))]


def write(layer, y, v):
    ref, lead = layer
    ref[(*lead, pl.ds(PAD + y, CHUNK), slice(None))] = v


def z_sum(v):
    depth = v.shape[1]
    lane = lax.broadcasted_iota(jnp.int32, v.shape, 1)
    below = jnp.where(lane == 0, 0.0, pltpu.roll(v, 1, 1))
    above = jnp.where(lane == depth - 1, 0.0, pltpu.roll(v, depth - 1, 1))
    return below + above


def plane_part(layer, y):
    v = read(layer, y)
    return read(layer, y, 1) + read(layer, y, -1) + z_sum(v) - 6.0 * v


def clear_margins(layer):
    ref, lead = layer
    zero = jnp.zeros((PAD, ref.shape[-1]), f32)
    ref[(*lead, pl.ds(0, PAD), slice(None))] = zero
    ref[(*lead, pl.ds(ref.shape[-2] - PAD, PAD), slice(None))] = zero


def is_odd():
    return lax.rem(lax.axis_index("slab"), 2) == 1


def stored(d, layers):
    return jnp.where(is_odd(), d, layers - 1 - d)


def has_partner(count):
    position = lax.axis_index("slab")
    above = position < count - 1
    below = position > 0
    odd = is_odd()
    flags = jnp.where(odd, below, above), jnp.where(odd, above, below)
    return [jnp.where(f, 1.0, 0.0).astype(f32) for f in flags]


def copy_all(pairs, sems):
    copies = [pltpu.make_async_copy(s, d, sems.at[i]) for i, (s, d) in enumerate(pairs)]
    for c in copies:
        c.start()
    return copies


def write_message(near, far, missing, out, rows):
    clear_margins(missing)
    for y in starts(rows):
        v = read(near, y)
        rounded = v.astype(bf16)
        out[pl.ds(y, CHUNK), :] = rounded
        write(missing, y, v - rounded.astype(f32))
    for y in starts(rows):
        out[pl.ds(rows + y, CHUNK), :] = (read(far, y) + 2.0 * plane_part(missing, y)).astype(bf16)


def curvature_of(p):
    return 3.0 * p * p - 1.0


def local_step(state, first, phase, row, count, emit):
    layers = len(state)
    rows = phase.shape[1]
    depth = phase.shape[2]
    side_a, side_b = has_partner(count)
    transport = row[0:1, :]
    for d in range(layers):
        for y in starts(rows):
            lap = plane_part(state[d], y)
            if d > 0:
                lap = lap + read(state[d - 1], y)
            if d < layers - 1:
                lap = lap + read(state[d + 1], y)
            write(first[d], y, lap)
    for d in range(layers):
        at = stored(d, layers)
        for y in starts(rows):
            v = read(state[d], y)
            second = plane_part(first[d], y)
            second = second + (read(first[d - 1], y) if d > 0 else side_a * v)
            second = second + (read(first[d + 1], y) if d < layers - 1 else side_b * v)
            p = phase[at, pl.ds(y, CHUNK), :].astype(f32)
            moved = read(state[d], y, 1) - read(state[d], y, -1)
            stepped = (
                v
                + mobility_step * curvature_of(p) * read(first[d], y)
                - stiffness_step * second
                + transport * moved
            )
            emit(d, y, v, stepped)


def padded(rows, depth, layers=None):
    lead = () if layers is None else (layers,)
    return pltpu.VMEM((*lead, rows + 2 * PAD, depth), f32)


def layers_of(ref):
    return [(ref, (d,)) for d in range(ref.shape[0])]


def first_message(adjoint, targets, owners, cells, out, near, far, missing, digits, owner, cell, sems):
    layers, rows, depth = adjoint.shape
    n = targets.shape[0]
    pairs = [(adjoint.at[stored(d, layers)], ref.at[pl.ds(PAD, rows)]) for d, ref in ((0, near), (1, far))]
    if out.shape[0] > 2 * rows:
        pairs += [(targets, out.at[pl.ds(2 * rows, n)]), (owners, owner), (cells, cell)]
    copies = copy_all(pairs, sems)
    if out.shape[0] > 2 * rows:
        digits[...] = jnp.zeros(digits.shape, f32)
        for c in copies[3:]:
            c.wait()
        digits[0:1, 0:n] = owner[...].astype(f32)
        digits[1:2, 0:n] = (cell[...] >> 8).astype(f32)
        digits[2:3, 0:n] = (cell[...] & 255).astype(f32)
        out[pl.ds(2 * rows + n, 16), :] = digits[...].astype(bf16)
    for c in copies[:3]:
        c.wait()
    write_message((near, ()), (far, ()), (missing, ()), out, rows)


def make_first_message(adjoint, targets, owners, cells, extra):
    layers, rows, depth = adjoint.shape
    row = pltpu.VMEM(owners.shape, jnp.int32)
    return call(
        first_message,
        jax.ShapeDtypeStruct((2 * rows + extra, depth), bf16),
        VMEM,
        [ANY] * 4,
        [padded(rows, depth)] * 3 + [pltpu.VMEM((16, depth), f32), row, row, pltpu.SemaphoreType.DMA((5,))],
        cost(20 * rows * depth, 12 * rows * depth),
        limit=LARGE,
    )(adjoint, targets, owners, cells)


def transport_row(inflow, depth):
    lane = lax.broadcasted_iota(jnp.int32, (8, depth), 1)
    height = (lane.astype(f32) + 0.5) / depth
    return (transport_step * inflow) * (4.0 * height * (1.0 - height))


def first_local(count, adjoint, phase, rates, choice, mask, after, out, message, row, masked, state, first, missing, sems):
    layers, rows, depth = adjoint.shape
    copies = copy_all(
        [(adjoint.at[stored(d, layers)], state.at[d, pl.ds(PAD, rows)]) for d in range(layers)], sems
    )
    row[...] = transport_row(rates[choice[0]], depth)
    masked[...] = wall_weight * mask[...].astype(f32)
    for d in range(layers):
        clear_margins((state, (d,)))
        clear_margins((first, (d,)))
    own = layers_of(state)
    for c in copies:
        c.wait()
    write_message(own[-1], own[-2], (missing, ()), message, rows)

    def emit(d, y, v, stepped):
        out[d, pl.ds(y, CHUNK), :] = stepped

    local_step(own, layers_of(first), phase, row, count, emit)


def make_first_local(adjoint, phase, rates, choice, mask, after, count):
    layers, rows, depth = adjoint.shape
    return call(
        lambda *refs: first_local(count, *refs),
        (
            jax.ShapeDtypeStruct(adjoint.shape, f32),
            jax.ShapeDtypeStruct((2 * rows, depth), bf16),
            jax.ShapeDtypeStruct((8, depth), f32),
            jax.ShapeDtypeStruct(mask.shape, f32),
        ),
        (VMEM,) * 4,
        [ANY, VMEM, SMEM, SMEM, VMEM, ANY],
        [padded(rows, depth, layers)] * 2 + [padded(rows, depth), pltpu.SemaphoreType.DMA((layers,))],
        cost(80 * layers * rows * depth, 12 * layers * rows * depth),
    )(adjoint, phase, rates, choice, mask, after)


def add_halo(message, edge, inner, halo, phase, at, rows, put_edge, put_inner):
    clear_margins(halo)
    for y in starts(rows):
        near = message[pl.ds(y, CHUNK), :].astype(f32)
        write(halo, y, near)
        put_inner(y, inner(y) - stiffness_step * near)
    for y in starts(rows):
        near = read(halo, y)
        far = message[pl.ds(rows + y, CHUNK), :].astype(f32)
        curvature = curvature_of(phase[at, pl.ds(y, CHUNK), :].astype(f32))
        both = far + 2.0 * plane_part(halo, y)
        put_edge(y, edge(y) + mobility_step * curvature * near - stiffness_step * both)


def wall_rows(v, first_row):
    depth = v.shape[1]
    row = lax.broadcasted_iota(jnp.int32, (8, depth), 0) - first_row
    lane = lax.broadcasted_iota(jnp.int32, (8, depth), 1)
    pick = ((row == 0) & (lane == 0)) | ((row == 1) & (lane == depth - 1))
    pick = jnp.where(pick, 1.0, 0.0).astype(bf16)

    def part(w):
        return lax.dot_general(pick, w, (((1,), (1,)), ((), ())), preferred_element_type=f32)

    if v.dtype == bf16:
        return part(v)
    high = v.astype(bf16)
    rest = v - high.astype(f32)
    middle = rest.astype(bf16)
    low = (rest - middle.astype(f32)).astype(bf16)
    return part(high) + part(middle) + part(low)


def middle(side, message, pre, phase, *refs):
    blocks, refs = refs[: 1 + 2 * side], refs[1 + 2 * side :]
    layers, rows, depth = pre.shape
    one, two = (0, 1) if side == 0 else (layers - 1, layers - 2)
    if side == 0:
        out, sent, block, halo, missing = refs
        if message.shape[0] > 2 * rows:
            block[0] = blocks[0][pl.ds(2 * rows, block.shape[1]), :]
            block[1] = message[pl.ds(2 * rows, block.shape[1]), :]
    else:
        out, wall, block, halo = refs
        for i in range(4):
            block[i] = blocks[i // 2][i % 2]
    edge, inner = layers_of(out)
    clear_margins(edge)
    clear_margins(inner)
    add_halo(
        message,
        lambda y: pre[one, pl.ds(y, CHUNK), :],
        lambda y: pre[two, pl.ds(y, CHUNK), :],
        (halo, ()),
        phase,
        stored(one, layers),
        rows,
        lambda y, v: write(edge, y, v),
        lambda y, v: write(inner, y, v),
    )
    if side == 0:
        write_message(edge, inner, (missing, ()), sent, rows)
    for y in range(0, rows, 128):
        both = [read(inner, y + k) + 2.0 * plane_part(edge, y + k) for k in range(0, 128, CHUNK)]
        near = [read(edge, y + k) for k in range(0, 128, CHUNK)]
        wall_part = wall_rows(jnp.concatenate(near), 0) + wall_rows(jnp.concatenate(both), 2)
        if side == 0:
            high = wall_part.astype(bf16)
            low = (wall_part - high.astype(f32)).astype(bf16)
            sent[pl.ds(2 * rows + y // 8, 16), :] = jnp.concatenate([high.astype(f32), low.astype(f32)]).astype(bf16)
        else:
            wall[:, pl.ds(y, 128)] = wall_part


def make_middle(message, pre, phase, side, extra, *more):
    layers, rows, depth = pre.shape
    outs = [jax.ShapeDtypeStruct((2, rows + 2 * PAD, depth), f32)]
    scratch = [padded(rows, depth)]
    if side == 1:
        outs.append(jax.ShapeDtypeStruct((8, rows), f32))
        outs.append(jax.ShapeDtypeStruct((4, extra, depth), bf16))
    else:
        outs.append(jax.ShapeDtypeStruct((2 * rows + rows // 8, depth), bf16))
        outs.append(jax.ShapeDtypeStruct((2, extra, depth), bf16))
        scratch.append(padded(rows, depth))
    return call(
        lambda *refs: middle(side, *refs),
        tuple(outs),
        (VMEM,) * len(outs),
        [VMEM, VMEM, VMEM] + ([VMEM, VMEM, ANY] if side else [VMEM]),
        scratch,
        cost(60 * rows * depth, 30 * rows * depth),
    )(message, pre, phase, *more)


def second_local(count, side_a, side_b, phase, row, out, wall, phase_wall, message, first, missing):
    layers, rows, depth = out.shape
    own = layers_of(side_a) + layers_of(side_b)[::-1]
    for d in range(layers):
        clear_margins((first, (d,)))
    write_message(own[-1], own[-2], (missing, ()), message, rows)
    held = []

    def emit(d, y, v, stepped):
        out[d, pl.ds(y, CHUNK), :] = stepped
        held.append(v + stepped)
        if len(held) * CHUNK == 128:
            start = y + CHUNK - 128
            wall[d, :, pl.ds(start, 128)] = wall_rows(jnp.concatenate(held), 0)
            phase_wall[d, :, pl.ds(start, 128)] = wall_rows(phase[stored(d, layers), pl.ds(start, 128), :], 0)
            held.clear()

    local_step(own, layers_of(first), phase, row, count, emit)


def make_second_local(side_a, side_b, phase, row, count):
    layers, rows, depth = phase.shape
    return call(
        lambda *refs: second_local(count, *refs),
        (
            jax.ShapeDtypeStruct((layers, rows, depth), f32),
            jax.ShapeDtypeStruct((layers, 8, rows), f32),
            jax.ShapeDtypeStruct((layers, 8, rows), f32),
            jax.ShapeDtypeStruct((2 * rows, depth), bf16),
        ),
        (VMEM,) * 4,
        [VMEM] * 4,
        [padded(rows, depth, layers), padded(rows, depth)],
        cost(80 * layers * rows * depth, 12 * layers * rows * depth),
    )(side_a, side_b, phase, row)


def injection(phase, *refs):
    blocks, (out, index, rhs) = refs[:-3], refs[-3:]
    layers, rows, depth = out.shape
    n = blocks[0].shape[1] - 16
    position = lax.axis_index("slab").astype(f32)
    rhs[:, :depth] = jnp.ones((rhs.shape[0], depth), bf16)
    at = 0
    for block in blocks:
        for i in range(block.shape[0]):
            rhs[pl.ds(at, n), depth:] = block[i, pl.ds(0, n), :]
            digits = block[i, pl.ds(n, 16), :].astype(f32)
            cell = jnp.where(digits[0:1] == position, digits[1:2] * 256.0 + digits[2:3], -1.0)
            index[0:1, pl.ds(at, n)] = cell[:, :n].astype(jnp.int32)
            at += n
    for d in range(layers):
        at = stored(d, layers)
        for y in range(0, rows, 128):
            cell = lax.broadcasted_iota(jnp.int32, (128, index.shape[1]), 0) + (at * rows + y)
            here = jnp.where(cell == index[0:1, :], 1.0, 0.0).astype(bf16)
            added = jnp.dot(here, rhs[...], preferred_element_type=f32)
            p = phase[at, pl.ds(y, 128), :].astype(f32)
            out[d, pl.ds(y, 128), :] = added[:, :depth] * p - added[:, depth:]


def make_injection(phase, *blocks):
    layers, rows, depth = phase.shape
    total = sum(b.shape[0] * (b.shape[1] - 16) for b in blocks)
    return call(
        injection,
        jax.ShapeDtypeStruct((layers, rows, depth), f32),
        VMEM,
        [VMEM] * (1 + len(blocks)),
        [pltpu.VMEM((8, total), jnp.int32), pltpu.VMEM((total, 2 * depth), bf16)],
        cost(40 * layers * rows * depth, 6 * layers * rows * depth),
    )(phase, *blocks)


def wall_kernel(wall, phase_wall, message, from_b, mask, after, out, from_a):
    layers = wall.shape[0]
    rows = wall.shape[2]
    for y in range(0, rows, 128):
        both = message[pl.ds(2 * rows + y // 8, 16), :].astype(f32)
        from_a[:, pl.ds(y, 128)] = both[:8] + both[8:]
    odd = is_odd()
    terms = []
    for d in range(layers):
        p = phase_wall[d, :2, :]
        w = wall[d, :2, :]
        for halo, off in ((from_a, d), (from_b, layers - 1 - d)):
            if off == 0:
                w = w + mobility_step * curvature_of(p) * halo[:2] - stiffness_step * halo[2:4]
            elif off == 1:
                w = w - stiffness_step * halo[:2]
        terms.append((1.0 - p * p) * w)
    for l in range(layers):
        out[:, l, :] = mask[:, l, :] * jnp.where(odd, terms[l], terms[layers - 1 - l])


def make_walls(wall, phase_wall, message, from_b, mask, after):
    return call(
        wall_kernel,
        jax.ShapeDtypeStruct(mask.shape, f32),
        VMEM,
        [VMEM] * 5 + [ANY],
        [pltpu.VMEM(from_b.shape, f32)],
        cost(40 * mask.size, 20 * mask.size),
    )(wall, phase_wall, message, from_b, mask, after)


def final(side, message, pre, added, phase, *refs):
    if side == 0:
        out, edge, inner, halo, sems = refs
    else:
        walls = refs[1:-6]
        out, total, edge, inner, halo, sems = refs[-6:]
        if len(walls) == 4:
            total[...] = (walls[0][...] + walls[1][...]) + (walls[2][...] + walls[3][...])
        else:
            total[...] = walls[0][...]
    layers, rows, depth = pre.shape
    one, two = (0, 1) if side == 0 else (layers - 1, layers - 2)
    half = rows // 2
    copies = []

    def send(ref, layer, start, slot):
        c = pltpu.make_async_copy(
            ref.at[pl.ds(start, half)], out.at[stored(layer, layers), pl.ds(start, half)], sems.at[slot]
        )
        c.start()
        copies.append(c)

    def put_inner(y, v):
        inner[pl.ds(y, CHUNK), :] = v + added[two, pl.ds(y, CHUNK), :]
        if (y + CHUNK) % half == 0:
            send(inner, two, y + CHUNK - half, len(copies))

    def put_edge(y, v):
        edge[pl.ds(y, CHUNK), :] = v + added[one, pl.ds(y, CHUNK), :]
        if (y + CHUNK) % half == 0:
            send(edge, one, y + CHUNK - half, len(copies))

    add_halo(
        message,
        lambda y: pre[one, pl.ds(y, CHUNK), :],
        lambda y: pre[two, pl.ds(y, CHUNK), :],
        (halo, ()),
        phase,
        stored(one, layers),
        rows,
        put_edge,
        put_inner,
    )
    for c in copies:
        c.wait()


def make_final(message, pre, added, phase, side, out=None, walls=()):
    layers, rows, depth = pre.shape
    plane = pltpu.VMEM((rows, depth), f32)
    whole = jax.ShapeDtypeStruct(pre.shape, f32)
    more = [] if side == 0 else [out, *walls]
    return call(
        lambda *refs: final(side, *refs),
        whole if side == 0 else (whole, jax.ShapeDtypeStruct(walls[0].shape, f32)),
        ANY if side == 0 else (ANY, VMEM),
        [VMEM] * 4 + ([] if side == 0 else [ANY] + [VMEM] * len(walls)),
        [plane, plane, padded(rows, depth), pltpu.SemaphoreType.DMA((4,))],
        cost(30 * rows * depth, 20 * rows * depth),
        aliases={} if side == 0 else {4: 0},
    )(message, pre, added, phase, *more)


def parts_over(g, axis):
    if lax.axis_size(axis) != 4:
        return [lax.psum(g, axis)]
    return [g] + [lax.ppermute(g, axis, [(i, i ^ k) for i in range(4)]) for k in (1, 2, 3)]


def row_block(targets, owners, cells):
    n, depth = targets.shape
    digits = jnp.concatenate([owners, cells // 256, cells % 256])
    digits = jnp.pad(digits, ((0, 13), (0, depth - n))).astype(bf16)
    return jnp.concatenate([targets, digits], axis=0)


def on_device(adjoint, phase, targets, owners, target_cell, rate_index, inflow_rates, wall_mask):
    state, phase, targets = adjoint[0], phase[0], targets[0]
    owners = owners.reshape(target_cell.shape)
    layers, rows, depth = state.shape
    n = targets.shape[0]
    count = lax.axis_size("slab")
    pairs = (
        [(i, i ^ 1) for i in range(count) if i ^ 1 < count],
        [(i, i + 1) for i in range(1, count - 1, 2)] + [(i + 1, i) for i in range(1, count - 1, 2)],
    )
    doubling = count == 8

    def send(v, side):
        return lax.ppermute(v, "slab", pairs[side])

    message = make_first_message(state, targets, owners, target_cell, n + 16 if doubling else 0)
    from_a = send(message, 0)
    pre, message_b, row, mask = make_first_local(
        state, phase, inflow_rates, rate_index, wall_mask, message, count
    )
    from_b = send(message_b, 1)
    half_a, message_a, block = make_middle(from_a, pre, phase, 0, n + 16, message)
    later_a = send(message_a, 0)
    beside = lax.ppermute(block, "slab", [(i, i ^ 2) for i in range(count)]) if doubling else block
    half_b, wall_b, block = make_middle(from_b, pre, phase, 1, n + 16, block, beside, message_a)
    wall_b = send(wall_b, 1)
    if doubling:
        blocks = [block, lax.ppermute(block, "slab", [(i, i ^ 4) for i in range(count)])]
    else:
        blocks = [lax.all_gather(row_block(targets, owners, target_cell), "slab", axis=0)]
    pre, wall, phase_wall, message_b = make_second_local(half_a, half_b, phase, row, count)
    later_b = send(message_b, 1)
    walls = parts_over(make_walls(wall, phase_wall, later_a, wall_b, mask, blocks[-1]), "cond")
    added = make_injection(phase, *blocks)
    out = make_final(later_a, pre, added, phase, 0)
    out, wall_gradient = make_final(later_b, pre, added, phase, 1, out, walls)
    return out[None], wall_gradient


def solution(mesh):
    in_specs = (
        P("cond", "slab", None, None),
        P("cond", "slab", None, None),
        P("cond", "slab", None),
        P("cond", "slab", None),
        P("cond", "slab"),
        P("cond"),
        P(),
        P(None, "slab", None),
    )
    out_specs = (P("cond", "slab", None, None), P(None, "slab", None))
    return jax.shard_map(
        on_device, mesh=mesh, in_specs=in_specs, out_specs=out_specs, check_vma=False
    )
```

```python
import jax
import jax.numpy as jnp
from jax import lax
from jax.experimental import pallas as pl
from jax.experimental.pallas import tpu as pltpu
from jax.sharding import PartitionSpec as P

mobility_step = 0.02
stiffness_step = 0.01
transport_step = 0.125
wall_weight = 0.25

f32 = jnp.float32
bf16 = jnp.bfloat16
CHUNK = 64
LONG = 10**10
PAD = 8
ANY = pl.BlockSpec(memory_space=pl.ANY)
HBM = pl.BlockSpec(memory_space=pltpu.HBM)
VMEM = pl.BlockSpec(memory_space=pltpu.VMEM)
SMEM = pl.BlockSpec(memory_space=pltpu.SMEM)


def cost(flops):
    return pl.CostEstimate(flops=flops, bytes_accessed=1, transcendentals=0)


def call(kernel, outs, out_specs, in_specs, scratch, estimate, aliases=None, limit=12):
    return pl.pallas_call(
        kernel,
        out_shape=outs,
        out_specs=out_specs,
        in_specs=in_specs,
        scratch_shapes=scratch,
        input_output_aliases=aliases or {},
        cost_estimate=estimate,
        compiler_params=pltpu.CompilerParams(vmem_limit_bytes=limit * 1024 * 1024),
    )


def starts(rows):
    return range(0, rows, CHUNK)


def read(layer, y, shift=0):
    ref, lead = layer
    return ref[(*lead, pl.ds(PAD + y + shift, CHUNK), slice(None))]


def write(layer, y, v):
    ref, lead = layer
    ref[(*lead, pl.ds(PAD + y, CHUNK), slice(None))] = v


def z_sum(v):
    depth = v.shape[1]
    lane = lax.broadcasted_iota(jnp.int32, v.shape, 1)
    below = jnp.where(lane == 0, 0.0, pltpu.roll(v, 1, 1))
    above = jnp.where(lane == depth - 1, 0.0, pltpu.roll(v, depth - 1, 1))
    return below + above


def plane_part(layer, y):
    v = read(layer, y)
    return read(layer, y, 1) + read(layer, y, -1) + z_sum(v) - 6.0 * v


def clear_margins(layer):
    ref, lead = layer
    zero = jnp.zeros((PAD, ref.shape[-1]), f32)
    ref[(*lead, pl.ds(0, PAD), slice(None))] = zero
    ref[(*lead, pl.ds(ref.shape[-2] - PAD, PAD), slice(None))] = zero


def is_odd():
    return lax.rem(lax.axis_index("slab"), 2) == 1


def stored(d, layers):
    return jnp.where(is_odd(), d, layers - 1 - d)


def has_partner(count):
    position = lax.axis_index("slab")
    above = position < count - 1
    below = position > 0
    odd = is_odd()
    flags = jnp.where(odd, below, above), jnp.where(odd, above, below)
    return [jnp.where(f, 1.0, 0.0).astype(f32) for f in flags]


def copy_all(pairs, sems):
    copies = [pltpu.make_async_copy(s, d, sems.at[i]) for i, (s, d) in enumerate(pairs)]
    for c in copies:
        c.start()
    return copies


def write_message(near, far, missing, out, rows):
    clear_margins(missing)
    for y in starts(rows):
        v = read(near, y)
        rounded = v.astype(bf16)
        out[pl.ds(y, CHUNK), :] = rounded
        write(missing, y, v - rounded.astype(f32))
    for y in starts(rows):
        out[pl.ds(rows + y, CHUNK), :] = (read(far, y) + 2.0 * plane_part(missing, y)).astype(bf16)


def curvature_of(p):
    return 3.0 * p * p - 1.0


def local_step(state, first, phase, row, count, emit):
    layers = len(state)
    rows = phase.shape[1]
    depth = phase.shape[2]
    side_a, side_b = has_partner(count)
    transport = row[0:1, :]
    for d in range(layers):
        for y in starts(rows):
            lap = plane_part(state[d], y)
            if d > 0:
                lap = lap + read(state[d - 1], y)
            if d < layers - 1:
                lap = lap + read(state[d + 1], y)
            write(first[d], y, lap)
    for d in range(layers):
        at = stored(d, layers)
        for y in starts(rows):
            v = read(state[d], y)
            second = plane_part(first[d], y)
            second = second + (read(first[d - 1], y) if d > 0 else side_a * v)
            second = second + (read(first[d + 1], y) if d < layers - 1 else side_b * v)
            p = phase[at, pl.ds(y, CHUNK), :].astype(f32)
            moved = read(state[d], y, 1) - read(state[d], y, -1)
            stepped = (
                v
                + mobility_step * curvature_of(p) * read(first[d], y)
                - stiffness_step * second
                + transport * moved
            )
            emit(d, y, v, stepped)


def padded(rows, depth, layers=None):
    lead = () if layers is None else (layers,)
    return pltpu.VMEM((*lead, rows + 2 * PAD, depth), f32)


def layers_of(ref):
    return [(ref, (d,)) for d in range(ref.shape[0])]


def first_message(adjoint, targets, owners, cells, out, near, far, missing, digits, owner, cell, sems):
    layers, rows, depth = adjoint.shape
    n = targets.shape[0]
    pairs = [(adjoint.at[stored(d, layers)], ref.at[pl.ds(PAD, rows)]) for d, ref in ((0, near), (1, far))]
    pairs += [(targets, out.at[pl.ds(2 * rows, n)]), (owners, owner), (cells, cell)]
    copies = copy_all(pairs, sems)
    digits[...] = jnp.zeros(digits.shape, f32)
    for c in copies[3:]:
        c.wait()
    digits[0:1, 0:n] = owner[...].astype(f32)
    digits[1:2, 0:n] = (cell[...] >> 8).astype(f32)
    digits[2:3, 0:n] = (cell[...] & 255).astype(f32)
    out[pl.ds(2 * rows + n, 16), :] = digits[...].astype(bf16)
    for c in copies[:3]:
        c.wait()
    write_message((near, ()), (far, ()), (missing, ()), out, rows)


def make_first_message(adjoint, targets, owners, cells):
    layers, rows, depth = adjoint.shape
    extra = targets.shape[0] + 16
    row = pltpu.VMEM(owners.shape, jnp.int32)
    return call(
        first_message,
        jax.ShapeDtypeStruct((2 * rows + extra, depth), bf16),
        VMEM,
        [ANY] * 4,
        [padded(rows, depth)] * 3 + [pltpu.VMEM((16, depth), f32), row, row, pltpu.SemaphoreType.DMA((5,))],
        cost(LONG),
    )(*[pltpu.with_memory_space_constraint(v, pltpu.HBM) for v in (adjoint, targets, owners, cells)])


def transport_row(inflow, depth):
    lane = lax.broadcasted_iota(jnp.int32, (8, depth), 1)
    height = (lane.astype(f32) + 0.5) / depth
    return (transport_step * inflow) * (4.0 * height * (1.0 - height))


def first_local(
    count, adjoint, phase, rates, choice, mask, after, out, message, row, masked, state, first, missing, sems
):
    layers, rows, depth = adjoint.shape
    copies = copy_all(
        [(adjoint.at[stored(d, layers)], state.at[d, pl.ds(PAD, rows)]) for d in range(layers)], sems
    )
    row[...] = transport_row(rates[choice[0]], depth)
    masked[...] = wall_weight * mask[...].astype(f32)
    for d in range(layers):
        clear_margins((state, (d,)))
        clear_margins((first, (d,)))
    for c in copies:
        c.wait()
    own = layers_of(state)
    write_message(own[-1], own[-2], (missing, ()), message, rows)

    def emit(d, y, v, stepped):
        out[d, pl.ds(y, CHUNK), :] = stepped

    local_step(own, layers_of(first), phase, row, count, emit)


def make_first_local(adjoint, phase, rates, choice, mask, after, count):
    layers, rows, depth = adjoint.shape
    return call(
        lambda *refs: first_local(count, *refs),
        (
            jax.ShapeDtypeStruct(adjoint.shape, f32),
            jax.ShapeDtypeStruct((2 * rows, depth), bf16),
            jax.ShapeDtypeStruct((8, depth), f32),
            jax.ShapeDtypeStruct(mask.shape, f32),
        ),
        (VMEM,) * 4,
        [ANY, VMEM, SMEM, SMEM, VMEM, ANY],
        [padded(rows, depth, layers)] * 2 + [padded(rows, depth), pltpu.SemaphoreType.DMA((layers,))],
        cost(LONG),
    )(adjoint, phase, rates, choice, mask, after)


def add_halo(message, edge, inner, halo, phase, at, rows, put_edge, put_inner):
    clear_margins(halo)
    for y in starts(rows):
        near = message[pl.ds(y, CHUNK), :].astype(f32)
        write(halo, y, near)
        put_inner(y, inner(y) - stiffness_step * near)
    for y in starts(rows):
        near = read(halo, y)
        far = message[pl.ds(rows + y, CHUNK), :].astype(f32)
        curvature = curvature_of(phase[at, pl.ds(y, CHUNK), :].astype(f32))
        both = far + 2.0 * plane_part(halo, y)
        put_edge(y, edge(y) + mobility_step * curvature * near - stiffness_step * both)


def wall_rows(v, first_row):
    depth = v.shape[1]
    row = lax.broadcasted_iota(jnp.int32, (8, depth), 0) - first_row
    lane = lax.broadcasted_iota(jnp.int32, (8, depth), 1)
    pick = ((row == 0) & (lane == 0)) | ((row == 1) & (lane == depth - 1))
    pick = jnp.where(pick, 1.0, 0.0).astype(bf16)

    def part(w):
        return lax.dot_general(pick, w, (((1,), (1,)), ((), ())), preferred_element_type=f32)

    if v.dtype == bf16:
        return part(v)
    high = v.astype(bf16)
    rest = v - high.astype(f32)
    middle = rest.astype(bf16)
    low = (rest - middle.astype(f32)).astype(bf16)
    return part(high) + part(middle) + part(low)


def join_halo(side, message, pre, phase, out, halo):
    layers, rows, depth = pre.shape
    one, two = (0, 1) if side == 0 else (layers - 1, layers - 2)
    edge, inner = layers_of(out)
    clear_margins(edge)
    clear_margins(inner)
    add_halo(
        message,
        lambda y: pre[one, pl.ds(y, CHUNK), :],
        lambda y: pre[two, pl.ds(y, CHUNK), :],
        (halo, ()),
        phase,
        stored(one, layers),
        rows,
        lambda y, v: write(edge, y, v),
        lambda y, v: write(inner, y, v),
    )


def second_message(half, sent, missing, rows):
    edge, inner = layers_of(half)
    write_message(edge, inner, (missing, ()), sent, rows)
    for y in range(0, rows, 256):
        wall_part = 0.0
        for i in range(2):
            span = range(y + 128 * i, y + 128 * (i + 1), CHUNK)
            both = jnp.concatenate([read(inner, k) + 2.0 * plane_part(edge, k) for k in span])
            near = jnp.concatenate([read(edge, k) for k in span])
            wall_part = wall_part + wall_rows(near, 4 * i) + wall_rows(both, 4 * i + 2)
        high = wall_part.astype(bf16)
        low = (wall_part - high.astype(f32)).astype(bf16)
        sent[pl.ds(2 * rows + y // 16, 16), :] = jnp.concatenate([high.astype(f32), low.astype(f32)]).astype(bf16)


def middle_a(message, pre, phase, first, out, sent, block, halo, missing):
    rows, n = pre.shape[1], block.shape[0] // 2
    join_halo(0, message, pre, phase, out, halo)
    second_message(out, sent, missing, rows)
    block[pl.ds(0, n), :] = first[pl.ds(2 * rows, n), :]
    block[pl.ds(n, n), :] = message[pl.ds(2 * rows, n), :]


def make_middle_a(message, pre, phase, first):
    layers, rows, depth = pre.shape
    extra = first.shape[0] - 2 * rows
    return call(
        middle_a,
        (
            jax.ShapeDtypeStruct((2, rows + 2 * PAD, depth), f32),
            jax.ShapeDtypeStruct((2 * rows + rows // 16, depth), bf16),
            jax.ShapeDtypeStruct((2 * extra, depth), bf16),
        ),
        (VMEM,) * 3,
        [VMEM] * 4,
        [padded(rows, depth)] * 2,
        cost(LONG),
    )(message, pre, phase, first)


def middle_b(message, pre, phase, after, out, sent, halo, missing):
    join_halo(1, message, pre, phase, out, halo)
    second_message(out, sent, missing, pre.shape[1])


def make_middle_b(message, pre, phase, after):
    layers, rows, depth = pre.shape
    return call(
        middle_b,
        (
            jax.ShapeDtypeStruct((2, rows + 2 * PAD, depth), f32),
            jax.ShapeDtypeStruct((2 * rows + rows // 16, depth), bf16),
        ),
        (VMEM,) * 2,
        [VMEM, VMEM, VMEM, ANY],
        [padded(rows, depth)] * 2,
        cost(LONG),
    )(message, pre, phase, after)


def second_local(count, side_a, side_b, phase, row, own, other, out, wall, phase_wall, block, first):
    layers, rows, depth = out.shape
    n = own.shape[0]
    block[pl.ds(0, n), :] = own[...]
    block[pl.ds(n, n), :] = other[...]
    own = layers_of(side_a) + layers_of(side_b)[::-1]
    for d in range(layers):
        clear_margins((first, (d,)))
    held = []

    def emit(d, y, v, stepped):
        out[d, pl.ds(y, CHUNK), :] = stepped
        held.append(v + stepped)
        if len(held) * CHUNK == 128:
            start = y + CHUNK - 128
            wall[d, :, pl.ds(start, 128)] = wall_rows(jnp.concatenate(held), 0)
            phase_wall[d, :, pl.ds(start, 128)] = wall_rows(phase[stored(d, layers), pl.ds(start, 128), :], 0)
            held.clear()

    local_step(own, layers_of(first), phase, row, count, emit)


def make_second_local(side_a, side_b, phase, row, own, other, count):
    layers, rows, depth = phase.shape
    return call(
        lambda *refs: second_local(count, *refs),
        (
            jax.ShapeDtypeStruct((layers, rows, depth), f32),
            jax.ShapeDtypeStruct((layers, 8, rows), f32),
            jax.ShapeDtypeStruct((layers, 8, rows), f32),
            jax.ShapeDtypeStruct((2 * own.shape[0], depth), bf16),
        ),
        (VMEM,) * 4,
        [VMEM] * 6,
        [padded(rows, depth, layers)],
        cost(2 * 10**9),
    )(side_a, side_b, phase, row, own, other)


def injection(n, phase, *refs):
    sources, (out, index, rhs) = refs[:-3], refs[-3:]
    layers, rows, depth = out.shape
    position = lax.axis_index("slab").astype(f32)
    rhs[:, :depth] = jnp.ones((rhs.shape[0], depth), bf16)
    at = 0
    for source in sources:
        for first in range(0, source.shape[0], n + 16):
            rhs[pl.ds(at, n), depth:] = source[pl.ds(first, n), :]
            digits = source[pl.ds(first + n, 16), :].astype(f32)
            cell = jnp.where(digits[0:1] == position, digits[1:2] * 256.0 + digits[2:3], -1.0)
            index[0:1, pl.ds(at, n)] = cell[:, :n].astype(jnp.int32)
            at += n
    for d in range(layers):
        at = stored(d, layers)
        for y in range(0, rows, 128):
            cell = lax.broadcasted_iota(jnp.int32, (128, index.shape[1]), 0) + (at * rows + y)
            here = jnp.where(cell == index[0:1, :], 1.0, 0.0).astype(bf16)
            added = jnp.dot(here, rhs[...], preferred_element_type=f32)
            p = phase[at, pl.ds(y, 128), :].astype(f32)
            out[d, pl.ds(y, 128), :] = added[:, :depth] * p - added[:, depth:]


def make_injection(phase, n, sources):
    layers, rows, depth = phase.shape
    total = sum(r.shape[0] // (n + 16) * n for r in sources)
    return call(
        lambda *refs: injection(n, *refs),
        jax.ShapeDtypeStruct((layers, rows, depth), f32),
        VMEM,
        [VMEM] * (1 + len(sources)),
        [pltpu.VMEM((8, total), jnp.int32), pltpu.VMEM((total, 2 * depth), bf16)],
        cost(1),
    )(phase, *sources)


def unpack_walls(message, rows, out):
    for y in range(0, rows, 256):
        both = message[pl.ds(2 * rows + y // 16, 16), :].astype(f32)
        both = both[:8] + both[8:]
        for i in range(2):
            out[:4, pl.ds(y + 128 * i, 128)] = both[4 * i : 4 * i + 4]


def make_unpack(message, rows):
    return call(
        lambda message, out: unpack_walls(message, rows, out),
        jax.ShapeDtypeStruct((8, rows), f32),
        VMEM,
        [VMEM],
        [],
        cost(14 * 10**8),
    )(message)


def wall_kernel(wall, phase_wall, from_a, message_b, mask, out, from_b):
    layers = wall.shape[0]
    unpack_walls(message_b, wall.shape[2], from_b)
    odd = is_odd()
    terms = []
    for d in range(layers):
        p = phase_wall[d, :2, :]
        w = wall[d, :2, :]
        for halo, off in ((from_a, d), (from_b, layers - 1 - d)):
            if off == 0:
                w = w + mobility_step * curvature_of(p) * halo[:2] - stiffness_step * halo[2:4]
            elif off == 1:
                w = w - stiffness_step * halo[:2]
        terms.append((1.0 - p * p) * w)
    for l in range(layers):
        out[:, l, :] = mask[:, l, :] * jnp.where(odd, terms[l], terms[layers - 1 - l])


def make_walls(wall, phase_wall, from_a, message_b, mask):
    held = pltpu.VMEM(wall.shape[1:], f32)
    return call(
        wall_kernel,
        jax.ShapeDtypeStruct(mask.shape, f32),
        VMEM,
        [VMEM] * 5,
        [held],
        cost(LONG),
    )(wall, phase_wall, from_a, message_b, mask)


def final(message_a, message_b, pre, added, phase, out, token, planes, halo, sems):
    layers, rows, depth = pre.shape
    half = rows // 2
    copies = []
    token[...] = jnp.zeros(token.shape, f32)

    def put(d):
        def store(y, v):
            planes[d, pl.ds(y, CHUNK), :] = v + added[d, pl.ds(y, CHUNK), :]
            if (y + CHUNK) % half == 0:
                span = pl.ds(y + CHUNK - half, half)
                c = pltpu.make_async_copy(
                    planes.at[d, span], out.at[stored(d, layers), span], sems.at[len(copies)]
                )
                c.start()
                copies.append(c)

        return store

    def get(d):
        return lambda y: pre[d, pl.ds(y, CHUNK), :]

    for message, one, two in ((message_a, 0, 1), (message_b, layers - 1, layers - 2)):
        add_halo(message, get(one), get(two), (halo, ()), phase, stored(one, layers), rows, put(one), put(two))
    for c in copies:
        c.wait()


def make_final(message_a, message_b, pre, added, phase):
    layers, rows, depth = pre.shape
    return call(
        final,
        (jax.ShapeDtypeStruct(pre.shape, f32), jax.ShapeDtypeStruct((8, depth), f32)),
        (ANY, VMEM),
        [VMEM] * 5,
        [pltpu.VMEM(pre.shape, f32), padded(rows, depth), pltpu.SemaphoreType.DMA((2 * layers,))],
        cost(1),
    )(message_a, message_b, pre, added, phase)


def add_up(a, b, c, d, after, out):
    out[...] = (a[...] + b[...]) + (c[...] + d[...])


def make_sum(parts, after):
    return call(add_up, jax.ShapeDtypeStruct(parts[0].shape, f32), VMEM, [VMEM] * 4 + [ANY], [], cost(1))(
        *parts, after
    )


def on_device(adjoint, phase, targets, owners, target_cell, rate_index, inflow_rates, wall_mask):
    state, phase, targets = adjoint[0], phase[0], targets[0]
    owners = owners.reshape(target_cell.shape)
    count = lax.axis_size("slab")
    pairs = (
        [(i, i ^ 1) for i in range(count) if i ^ 1 < count],
        [(i, i + 1) for i in range(1, count - 1, 2)] + [(i + 1, i) for i in range(1, count - 1, 2)],
    )

    def send(v, side):
        return lax.ppermute(v, "slab", pairs[side])

    rows, n = state.shape[1], targets.shape[0]
    few = count == 8
    first = make_first_message(state, targets, owners, target_cell)
    from_a = send(first, 0)
    pre, message, row, mask = make_first_local(state, phase, inflow_rates, rate_index, wall_mask, first, count)
    from_b = send(message, 1)
    half_a, message, pair = make_middle_a(from_a, pre, phase, first)
    later_a = send(message, 0)
    beside = lax.ppermute(pair, "slab", [(i, i ^ 2) for i in range(count)]) if few else pair
    half_b, message = make_middle_b(from_b, pre, phase, message)
    later_b = send(message, 1)
    pre, wall, phase_wall, four = make_second_local(half_a, half_b, phase, row, pair, beside, count)
    if few:
        blocks = [four, lax.ppermute(four, "slab", [(i, i ^ 4) for i in range(count)])]
    else:
        blocks = [lax.all_gather(first[2 * state.shape[1] :], "slab", axis=0, tiled=True)]
    part = make_walls(wall, phase_wall, make_unpack(later_a, state.shape[1]), later_b, mask)
    conditions = lax.axis_size("cond")
    if conditions == 4:
        parts = [part] + [lax.ppermute(part, "cond", [(i, i ^ k) for i in range(4)]) for k in (1, 2, 3)]
    added = make_injection(phase, n, blocks)
    out, token = make_final(later_a, later_b, pre, added, phase)
    wall_gradient = make_sum(parts, token) if conditions == 4 else lax.psum(part, "cond")
    return out[None], wall_gradient


def solution(mesh):
    in_specs = (
        P("cond", "slab", None, None),
        P("cond", "slab", None, None),
        P("cond", "slab", None),
        P("cond", "slab", None),
        P("cond", "slab"),
        P("cond"),
        P(),
        P(None, "slab", None),
    )
    out_specs = (P("cond", "slab", None, None), P(None, "slab", None))
    return jax.shard_map(
        on_device, mesh=mesh, in_specs=in_specs, out_specs=out_specs, check_vma=False
    )
```

```python
import jax
import jax.numpy as jnp
from jax import lax
from jax.experimental import pallas as pl
from jax.experimental.pallas import tpu as pltpu
from jax.sharding import PartitionSpec as P

mobility_step = 0.02
stiffness_step = 0.01
transport_step = 0.125
wall_weight = 0.25

f32 = jnp.float32
bf16 = jnp.bfloat16
CHUNK = 64
LONG = 10**10
PAD = 8
ANY = pl.BlockSpec(memory_space=pl.ANY)
HBM = pl.BlockSpec(memory_space=pltpu.HBM)
VMEM = pl.BlockSpec(memory_space=pltpu.VMEM)
SMEM = pl.BlockSpec(memory_space=pltpu.SMEM)


def cost(flops):
    return pl.CostEstimate(flops=flops, bytes_accessed=1, transcendentals=0)


def call(kernel, outs, out_specs, in_specs, scratch, estimate, aliases=None, limit=12):
    return pl.pallas_call(
        kernel,
        out_shape=outs,
        out_specs=out_specs,
        in_specs=in_specs,
        scratch_shapes=scratch,
        input_output_aliases=aliases or {},
        cost_estimate=estimate,
        compiler_params=pltpu.CompilerParams(vmem_limit_bytes=limit * 1024 * 1024),
    )


def starts(rows):
    return range(0, rows, CHUNK)


def read(layer, y, shift=0):
    ref, lead = layer
    return ref[(*lead, pl.ds(PAD + y + shift, CHUNK), slice(None))]


def write(layer, y, v):
    ref, lead = layer
    ref[(*lead, pl.ds(PAD + y, CHUNK), slice(None))] = v


def z_sum(v):
    depth = v.shape[1]
    lane = lax.broadcasted_iota(jnp.int32, v.shape, 1)
    below = jnp.where(lane == 0, 0.0, pltpu.roll(v, 1, 1))
    above = jnp.where(lane == depth - 1, 0.0, pltpu.roll(v, depth - 1, 1))
    return below + above


def plane_part(layer, y):
    v = read(layer, y)
    return read(layer, y, 1) + read(layer, y, -1) + z_sum(v) - 6.0 * v


def clear_margins(layer):
    ref, lead = layer
    zero = jnp.zeros((PAD, ref.shape[-1]), f32)
    ref[(*lead, pl.ds(0, PAD), slice(None))] = zero
    ref[(*lead, pl.ds(ref.shape[-2] - PAD, PAD), slice(None))] = zero


def is_odd():
    return lax.rem(lax.axis_index("slab"), 2) == 1


def stored(d, layers):
    return jnp.where(is_odd(), d, layers - 1 - d)


def has_partner(count):
    position = lax.axis_index("slab")
    above = position < count - 1
    below = position > 0
    odd = is_odd()
    flags = jnp.where(odd, below, above), jnp.where(odd, above, below)
    return [jnp.where(f, 1.0, 0.0).astype(f32) for f in flags]


def copy_all(pairs, sems):
    copies = [pltpu.make_async_copy(s, d, sems.at[i]) for i, (s, d) in enumerate(pairs)]
    for c in copies:
        c.start()
    return copies


def write_message(near, far, missing, out, rows):
    clear_margins(missing)
    for y in starts(rows):
        v = read(near, y)
        rounded = v.astype(bf16)
        out[pl.ds(y, CHUNK), :] = rounded
        write(missing, y, v - rounded.astype(f32))
    for y in starts(rows):
        out[pl.ds(rows + y, CHUNK), :] = (read(far, y) + 2.0 * plane_part(missing, y)).astype(bf16)


def curvature_of(p):
    return 3.0 * p * p - 1.0


def local_step(state, first, phase, row, count, emit):
    layers = len(state)
    rows = phase.shape[1]
    depth = phase.shape[2]
    side_a, side_b = has_partner(count)
    transport = row[0:1, :]
    for d in range(layers):
        for y in starts(rows):
            lap = plane_part(state[d], y)
            if d > 0:
                lap = lap + read(state[d - 1], y)
            if d < layers - 1:
                lap = lap + read(state[d + 1], y)
            write(first[d], y, lap)
    for d in range(layers):
        at = stored(d, layers)
        for y in starts(rows):
            v = read(state[d], y)
            second = plane_part(first[d], y)
            second = second + (read(first[d - 1], y) if d > 0 else side_a * v)
            second = second + (read(first[d + 1], y) if d < layers - 1 else side_b * v)
            p = phase[at, pl.ds(y, CHUNK), :].astype(f32)
            moved = read(state[d], y, 1) - read(state[d], y, -1)
            stepped = (
                v
                + mobility_step * curvature_of(p) * read(first[d], y)
                - stiffness_step * second
                + transport * moved
            )
            emit(d, y, v, stepped)


def padded(rows, depth, layers=None):
    lead = () if layers is None else (layers,)
    return pltpu.VMEM((*lead, rows + 2 * PAD, depth), f32)


def layers_of(ref):
    return [(ref, (d,)) for d in range(ref.shape[0])]


def first_message(adjoint, targets, owners, cells, out, near, far, missing, digits, owner, cell, sems):
    layers, rows, depth = adjoint.shape
    n = targets.shape[0]
    pairs = [(adjoint.at[stored(d, layers)], ref.at[pl.ds(PAD, rows)]) for d, ref in ((0, near), (1, far))]
    pairs += [(targets, out.at[pl.ds(2 * rows, n)]), (owners, owner), (cells, cell)]
    copies = copy_all(pairs, sems)
    digits[...] = jnp.zeros(digits.shape, f32)
    for c in copies[3:]:
        c.wait()
    digits[0:1, 0:n] = owner[...].astype(f32)
    digits[1:2, 0:n] = (cell[...] >> 8).astype(f32)
    digits[2:3, 0:n] = (cell[...] & 255).astype(f32)
    out[pl.ds(2 * rows + n, 16), :] = digits[...].astype(bf16)
    for c in copies[:3]:
        c.wait()
    write_message((near, ()), (far, ()), (missing, ()), out, rows)


def make_first_message(adjoint, targets, owners, cells):
    layers, rows, depth = adjoint.shape
    extra = targets.shape[0] + 16
    row = pltpu.VMEM(owners.shape, jnp.int32)
    return call(
        first_message,
        jax.ShapeDtypeStruct((2 * rows + extra, depth), bf16),
        VMEM,
        [ANY] * 4,
        [padded(rows, depth)] * 3 + [pltpu.VMEM((16, depth), f32), row, row, pltpu.SemaphoreType.DMA((5,))],
        cost(LONG),
    )(*[pltpu.with_memory_space_constraint(v, pltpu.HBM) for v in (adjoint, targets, owners, cells)])


def transport_row(inflow, depth):
    lane = lax.broadcasted_iota(jnp.int32, (8, depth), 1)
    height = (lane.astype(f32) + 0.5) / depth
    return (transport_step * inflow) * (4.0 * height * (1.0 - height))


def first_local(
    count, adjoint, phase, rates, choice, mask, after, out, message, row, masked, near_walls, state, first, missing, sems
):
    layers, rows, depth = adjoint.shape
    copies = copy_all(
        [(adjoint.at[stored(d, layers)], state.at[d, pl.ds(PAD, rows)]) for d in range(layers)], sems
    )
    row[...] = transport_row(rates[choice[0]], depth)
    masked[...] = wall_weight * mask[...].astype(f32)
    for d in range(layers):
        clear_margins((state, (d,)))
        clear_margins((first, (d,)))
    for c in copies:
        c.wait()
    own = layers_of(state)
    write_message(own[-1], own[-2], (missing, ()), message, rows)

    def emit(d, y, v, stepped):
        out[d, pl.ds(y, CHUNK), :] = stepped

    local_step(own, layers_of(first), phase, row, count, emit)
    four = (0, 1, depth - 1, depth - 2)
    two = (0, depth - 1)
    at = stored(layers - 1, layers)
    for y in range(0, rows, 128):
        span = pl.ds(y, 128)
        high, low = split(out[layers - 1, span, :], 2)
        high2, low2 = split(out[layers - 2, span, :], 2)
        picked = pick_rows(high, four, 0, 16) + pick_rows(low, four, 4, 16) + pick_rows(phase[at, span, :], four, 12, 16)
        picked = picked + pick_rows(high2, two, 8, 16) + pick_rows(low2, two, 10, 16)
        message[pl.ds(2 * rows + y // 8, 16), :] = picked.astype(bf16)
        steps = range(y, y + 128, CHUNK)
        near = jnp.concatenate([read(own[-1], k) for k in steps])
        both = jnp.concatenate([read(own[-2], k) + 2.0 * plane_part(own[-1], k) for k in steps])
        near_walls[:, span] = pick_exact(near, four, 0) + pick_exact(both, four, 4)


def make_first_local(adjoint, phase, rates, choice, mask, after, count):
    layers, rows, depth = adjoint.shape
    return call(
        lambda *refs: first_local(count, *refs),
        (
            jax.ShapeDtypeStruct(adjoint.shape, f32),
            jax.ShapeDtypeStruct((2 * rows + rows // 8, depth), bf16),
            jax.ShapeDtypeStruct((8, depth), f32),
            jax.ShapeDtypeStruct(mask.shape, f32),
            jax.ShapeDtypeStruct((8, rows), f32),
        ),
        (VMEM,) * 5,
        [ANY, VMEM, SMEM, SMEM, VMEM, ANY],
        [padded(rows, depth, layers)] * 2 + [padded(rows, depth), pltpu.SemaphoreType.DMA((layers,))],
        cost(LONG),
    )(adjoint, phase, rates, choice, mask, after)


def add_halo(message, edge, inner, halo, phase, at, rows, put_edge, put_inner):
    clear_margins(halo)
    for y in starts(rows):
        near = message[pl.ds(y, CHUNK), :].astype(f32)
        write(halo, y, near)
        put_inner(y, inner(y) - stiffness_step * near)
    for y in starts(rows):
        near = read(halo, y)
        far = message[pl.ds(rows + y, CHUNK), :].astype(f32)
        curvature = curvature_of(phase[at, pl.ds(y, CHUNK), :].astype(f32))
        both = far + 2.0 * plane_part(halo, y)
        put_edge(y, edge(y) + mobility_step * curvature * near - stiffness_step * both)


def pick_rows(v, heights, first_row, rows=8):
    depth = v.shape[1]
    row = lax.broadcasted_iota(jnp.int32, (rows, depth), 0) - first_row
    lane = lax.broadcasted_iota(jnp.int32, (rows, depth), 1)
    pick = jnp.zeros((rows, depth), f32)
    for i, z in enumerate(heights):
        pick = pick + jnp.where((row == i) & (lane == z), 1.0, 0.0)
    return lax.dot_general(pick.astype(bf16), v, (((1,), (1,)), ((), ())), preferred_element_type=f32)


def split(v, parts):
    out = []
    for _ in range(parts):
        high = v.astype(bf16)
        out.append(high)
        v = v - high.astype(f32)
    return out


def pick_exact(v, heights, first_row):
    return sum(pick_rows(part, heights, first_row) for part in split(v, 3))


def wall_rows(v, first_row):
    heights = (0, v.shape[1] - 1)
    return pick_rows(v, heights, first_row) if v.dtype == bf16 else pick_exact(v, heights, first_row)


def join_halo(side, message, pre, phase, out, halo):
    layers, rows, depth = pre.shape
    one, two = (0, 1) if side == 0 else (layers - 1, layers - 2)
    edge, inner = layers_of(out)
    clear_margins(edge)
    clear_margins(inner)
    add_halo(
        message,
        lambda y: pre[one, pl.ds(y, CHUNK), :],
        lambda y: pre[two, pl.ds(y, CHUNK), :],
        (halo, ()),
        phase,
        stored(one, layers),
        rows,
        lambda y, v: write(edge, y, v),
        lambda y, v: write(inner, y, v),
    )


def wall_parts(half, y):
    edge, inner = layers_of(half)
    parts = 0.0
    for i in range(2):
        span = range(y + 128 * i, y + 128 * (i + 1), CHUNK)
        both = jnp.concatenate([read(inner, k) + 2.0 * plane_part(edge, k) for k in span])
        near = jnp.concatenate([read(edge, k) for k in span])
        parts = parts + wall_rows(near, 4 * i) + wall_rows(both, 4 * i + 2)
    return parts


def put_walls(half, out, start):
    rows = half.shape[1] - 2 * PAD
    for y in range(0, rows, 256):
        parts = wall_parts(half, y)
        high = parts.astype(bf16).astype(f32)
        out[pl.ds(start + y // 16, 16), :] = jnp.concatenate([high, parts - high]).astype(bf16)


def middle_a(message, pre, phase, first, out, sent, early, block, halo, missing):
    rows, n = pre.shape[1], block.shape[0] // 2
    join_halo(0, message, pre, phase, out, halo)
    write_message(*layers_of(out), (missing, ()), sent, rows)
    put_walls(out, early, 0)
    block[pl.ds(0, n), :] = first[pl.ds(2 * rows, n), :]
    block[pl.ds(n, n), :] = message[pl.ds(2 * rows, n), :]


def make_middle_a(message, pre, phase, first):
    layers, rows, depth = pre.shape
    extra = first.shape[0] - 2 * rows
    return call(
        middle_a,
        (
            jax.ShapeDtypeStruct((2, rows + 2 * PAD, depth), f32),
            jax.ShapeDtypeStruct((2 * rows, depth), bf16),
            jax.ShapeDtypeStruct((rows // 16, depth), bf16),
            jax.ShapeDtypeStruct((2 * extra, depth), bf16),
        ),
        (VMEM,) * 4,
        [VMEM] * 4,
        [padded(rows, depth)] * 2,
        cost(LONG),
    )(message, pre, phase, first)


def partner_walls(message, near_walls, rows, present):
    sent = [message[pl.ds(2 * rows + y // 8, 16), :].astype(f32) for y in range(0, rows, 128)]
    sent = jnp.concatenate(sent, axis=1)
    here = near_walls[0:4, :]
    near = sent[0:4] + sent[4:8] + mobility_step * curvature_of(sent[12:16]) * here
    near = near - stiffness_step * near_walls[4:8, :]
    far = sent[8:10] + sent[10:12]
    lane = lax.broadcasted_iota(jnp.int32, (1, rows), 1)
    out = []
    for wall in range(2):
        v = near[2 * wall : 2 * wall + 1]
        along = jnp.where(lane == 0, 0.0, pltpu.roll(v, 1, 1)) + jnp.where(lane == rows - 1, 0.0, pltpu.roll(v, rows - 1, 1))
        plane = along + near[2 * wall + 1 : 2 * wall + 2] - 6.0 * v
        both = far[wall : wall + 1] - stiffness_step * here[2 * wall : 2 * wall + 1] + 2.0 * plane
        out.append((present * v, present * both))
    return [out[0][0], out[1][0], out[0][1], out[1][1]]


def middle_b(count, message, pre, phase, near_walls, after, out, sent, walls, halo, missing):
    rows = pre.shape[1]
    join_halo(1, message, pre, phase, out, halo)
    write_message(*layers_of(out), (missing, ()), sent, rows)
    walls[...] = jnp.zeros(walls.shape, f32)
    for i, v in enumerate(partner_walls(message, near_walls, rows, has_partner(count)[1])):
        walls[i : i + 1, :] = v


def make_middle_b(message, pre, phase, near_walls, after, count):
    layers, rows, depth = pre.shape
    return call(
        lambda *refs: middle_b(count, *refs),
        (
            jax.ShapeDtypeStruct((2, rows + 2 * PAD, depth), f32),
            jax.ShapeDtypeStruct((2 * rows, depth), bf16),
            jax.ShapeDtypeStruct((8, rows), f32),
        ),
        (VMEM,) * 3,
        [VMEM] * 4 + [ANY],
        [padded(rows, depth)] * 2,
        cost(LONG),
    )(message, pre, phase, near_walls, after)


def second_local(count, side_a, side_b, phase, row, own, other, out, wall, phase_wall, block, first):
    layers, rows, depth = out.shape
    n = own.shape[0]
    block[pl.ds(0, n), :] = own[...]
    block[pl.ds(n, n), :] = other[...]
    own = layers_of(side_a) + layers_of(side_b)[::-1]
    for d in range(layers):
        clear_margins((first, (d,)))
    held = []

    def emit(d, y, v, stepped):
        out[d, pl.ds(y, CHUNK), :] = stepped
        held.append(v + stepped)
        if len(held) * CHUNK == 128:
            start = y + CHUNK - 128
            wall[d, :, pl.ds(start, 128)] = wall_rows(jnp.concatenate(held), 0)
            phase_wall[d, :, pl.ds(start, 128)] = wall_rows(phase[stored(d, layers), pl.ds(start, 128), :], 0)
            held.clear()

    local_step(own, layers_of(first), phase, row, count, emit)


def make_second_local(side_a, side_b, phase, row, own, other, count):
    layers, rows, depth = phase.shape
    return call(
        lambda *refs: second_local(count, *refs),
        (
            jax.ShapeDtypeStruct((layers, rows, depth), f32),
            jax.ShapeDtypeStruct((layers, 8, rows), f32),
            jax.ShapeDtypeStruct((layers, 8, rows), f32),
            jax.ShapeDtypeStruct((2 * own.shape[0], depth), bf16),
        ),
        (VMEM,) * 4,
        [VMEM] * 6,
        [padded(rows, depth, layers)],
        cost(13 * 10**8),
    )(side_a, side_b, phase, row, own, other)


def injection(n, phase, *refs):
    sources, (out, index, rhs) = refs[:-3], refs[-3:]
    layers, rows, depth = out.shape
    position = lax.axis_index("slab").astype(f32)
    rhs[:, :depth] = jnp.ones((rhs.shape[0], depth), bf16)
    at = 0
    for source in sources:
        for first in range(0, source.shape[0], n + 16):
            rhs[pl.ds(at, n), depth:] = source[pl.ds(first, n), :]
            digits = source[pl.ds(first + n, 16), :].astype(f32)
            cell = jnp.where(digits[0:1] == position, digits[1:2] * 256.0 + digits[2:3], -1.0)
            index[0:1, pl.ds(at, n)] = cell[:, :n].astype(jnp.int32)
            at += n
    for d in range(layers):
        at = stored(d, layers)
        for y in range(0, rows, 128):
            cell = lax.broadcasted_iota(jnp.int32, (128, index.shape[1]), 0) + (at * rows + y)
            here = jnp.where(cell == index[0:1, :], 1.0, 0.0).astype(bf16)
            added = jnp.dot(here, rhs[...], preferred_element_type=f32)
            p = phase[at, pl.ds(y, 128), :].astype(f32)
            out[d, pl.ds(y, 128), :] = added[:, :depth] * p - added[:, depth:]


def make_injection(phase, n, sources):
    layers, rows, depth = phase.shape
    total = sum(r.shape[0] // (n + 16) * n for r in sources)
    return call(
        lambda *refs: injection(n, *refs),
        jax.ShapeDtypeStruct((layers, rows, depth), f32),
        VMEM,
        [VMEM] + [VMEM] * len(sources),
        [pltpu.VMEM((8, total), jnp.int32), pltpu.VMEM((total, 2 * depth), bf16)],
        cost(6 * 10**8),
    )(phase, *sources)


def unpack_walls(message, out):
    for y in range(0, out.shape[1], 256):
        both = message[pl.ds(y // 16, 16), :].astype(f32)
        both = both[:8] + both[8:]
        for i in range(2):
            out[:4, pl.ds(y + 128 * i, 128)] = both[4 * i : 4 * i + 4]


def wall_kernel(wall, phase_wall, early_a, from_b, mask, out, from_a):
    layers = wall.shape[0]
    unpack_walls(early_a, from_a)
    odd = is_odd()
    terms = []
    for d in range(layers):
        p = phase_wall[d, :2, :]
        w = wall[d, :2, :]
        for halo, off in ((from_a, d), (from_b, layers - 1 - d)):
            if off == 0:
                w = w + mobility_step * curvature_of(p) * halo[:2] - stiffness_step * halo[2:4]
            elif off == 1:
                w = w - stiffness_step * halo[:2]
        terms.append((1.0 - p * p) * w)
    for l in range(layers):
        out[:, l, :] = mask[:, l, :] * jnp.where(odd, terms[l], terms[layers - 1 - l])


def make_walls(wall, phase_wall, early_a, from_b, mask):
    return call(
        wall_kernel,
        jax.ShapeDtypeStruct(mask.shape, f32),
        VMEM,
        [VMEM] * 5,
        [pltpu.VMEM(wall.shape[1:], f32)],
        cost(55 * 10**7),
    )(wall, phase_wall, early_a, from_b, mask)


def halo_terms(layers, message, phase, after, out, halo):
    def put(layer):
        def store(y, v):
            out[layer, pl.ds(y, CHUNK), :] = v

        return store

    def nothing(y):
        return 0.0

    add_halo(message, nothing, nothing, (halo, ()), phase, stored(0, layers), phase.shape[1], put(0), put(1))


def make_halo_terms(message, phase, after):
    layers, rows, depth = phase.shape
    return call(
        lambda *refs: halo_terms(layers, *refs),
        jax.ShapeDtypeStruct((2, rows, depth), f32),
        VMEM,
        [VMEM, VMEM, ANY],
        [padded(rows, depth)],
        cost(6 * 10**8),
    )(message, phase, after)


def final(terms_a, message_b, pre, added, phase, *refs):
    walls, (out, total, planes, halo, sems) = refs[:-5], refs[-5:]
    layers, rows, depth = pre.shape
    half = rows // 2
    copies = []
    total[...] = (walls[0][...] + walls[1][...]) + (walls[2][...] + walls[3][...]) if len(walls) == 4 else walls[0][...]

    def put(d):
        def store(y, v):
            planes[d, pl.ds(y, CHUNK), :] = v + added[d, pl.ds(y, CHUNK), :]
            if (y + CHUNK) % half == 0:
                span = pl.ds(y + CHUNK - half, half)
                c = pltpu.make_async_copy(
                    planes.at[d, span], out.at[stored(d, layers), span], sems.at[len(copies)]
                )
                c.start()
                copies.append(c)

        return store

    def get(d):
        return lambda y: pre[d, pl.ds(y, CHUNK), :]

    for d in range(2):
        for y in starts(rows):
            put(d)(y, get(d)(y) + terms_a[d, pl.ds(y, CHUNK), :])
    one, two = layers - 1, layers - 2
    add_halo(message_b, get(one), get(two), (halo, ()), phase, stored(one, layers), rows, put(one), put(two))
    for c in copies:
        c.wait()


def make_final(terms_a, message_b, pre, added, phase, walls):
    layers, rows, depth = pre.shape
    return call(
        final,
        (jax.ShapeDtypeStruct(pre.shape, f32), jax.ShapeDtypeStruct(walls[0].shape, f32)),
        (ANY, VMEM),
        [VMEM] * (5 + len(walls)),
        [pltpu.VMEM(pre.shape, f32), padded(rows, depth), pltpu.SemaphoreType.DMA((2 * layers,))],
        cost(1),
    )(terms_a, message_b, pre, added, phase, *walls)


def on_device(adjoint, phase, targets, owners, target_cell, rate_index, inflow_rates, wall_mask):
    state, phase, targets = adjoint[0], phase[0], targets[0]
    owners = owners.reshape(target_cell.shape)
    count = lax.axis_size("slab")
    pairs = (
        [(i, i ^ 1) for i in range(count) if i ^ 1 < count],
        [(i, i + 1) for i in range(1, count - 1, 2)] + [(i + 1, i) for i in range(1, count - 1, 2)],
    )

    def send(v, side):
        return lax.ppermute(v, "slab", pairs[side])

    rows, n = state.shape[1], targets.shape[0]
    few = count == 8
    first = make_first_message(state, targets, owners, target_cell)
    from_a = send(first, 0)
    pre, message, row, mask, near_walls = make_first_local(state, phase, inflow_rates, rate_index, wall_mask, first, count)
    from_b = send(message, 1)
    half_a, message, early, pair = make_middle_a(from_a, pre, phase, first)
    early = send(early, 0)
    later_a = send(message, 0)
    beside = lax.ppermute(pair, "slab", [(i, i ^ 4) for i in range(count)]) if few else pair
    half_b, message, walls_b = make_middle_b(from_b, pre, phase, near_walls, message, count)
    later_b = send(message, 1)
    pre, wall, phase_wall, four = make_second_local(half_a, half_b, phase, row, pair, beside, count)
    if few:
        blocks = [four, lax.ppermute(four, "slab", [(i, i ^ 2) for i in range(count)])]
    else:
        blocks = [lax.all_gather(first[2 * state.shape[1] :], "slab", axis=0, tiled=True)]
    part = make_walls(wall, phase_wall, early, walls_b, mask)
    if lax.axis_size("cond") == 4:
        walls = [part] + [lax.ppermute(part, "cond", [(i, i ^ k) for i in range(4)]) for k in (1, 2, 3)]
    else:
        walls = [lax.psum(part, "cond")]
    added = make_injection(phase, n, blocks)
    terms = make_halo_terms(later_a, phase, added)
    out, wall_gradient = make_final(terms, later_b, pre, added, phase, walls)
    return out[None], wall_gradient


def solution(mesh):
    in_specs = (
        P("cond", "slab", None, None),
        P("cond", "slab", None, None),
        P("cond", "slab", None),
        P("cond", "slab", None),
        P("cond", "slab"),
        P("cond"),
        P(),
        P(None, "slab", None),
    )
    out_specs = (P("cond", "slab", None, None), P(None, "slab", None))
    return jax.shard_map(
        on_device, mesh=mesh, in_specs=in_specs, out_specs=out_specs, check_vma=False
    )
```

```python
import jax
import jax.numpy as jnp
from jax import lax
from jax.experimental import pallas as pl
from jax.experimental.pallas import tpu as pltpu
from jax.sharding import PartitionSpec as P

mobility_step = 0.02
stiffness_step = 0.01
transport_step = 0.125
wall_weight = 0.25

f32 = jnp.float32
bf16 = jnp.bfloat16
CHUNK = 64
LONG = 10**10
PAD = 8
ANY = pl.BlockSpec(memory_space=pl.ANY)
HBM = pl.BlockSpec(memory_space=pltpu.HBM)
VMEM = pl.BlockSpec(memory_space=pltpu.VMEM)
SMEM = pl.BlockSpec(memory_space=pltpu.SMEM)


def cost(flops):
    return pl.CostEstimate(flops=flops, bytes_accessed=1, transcendentals=0)


def call(kernel, outs, out_specs, in_specs, scratch, estimate, aliases=None, limit=12):
    return pl.pallas_call(
        kernel,
        out_shape=outs,
        out_specs=out_specs,
        in_specs=in_specs,
        scratch_shapes=scratch,
        input_output_aliases=aliases or {},
        cost_estimate=estimate,
        compiler_params=pltpu.CompilerParams(vmem_limit_bytes=limit * 1024 * 1024),
    )


def starts(rows):
    return range(0, rows, CHUNK)


def read(layer, y, shift=0):
    ref, lead = layer
    return ref[(*lead, pl.ds(PAD + y + shift, CHUNK), slice(None))]


def write(layer, y, v):
    ref, lead = layer
    ref[(*lead, pl.ds(PAD + y, CHUNK), slice(None))] = v


def z_sum(v):
    depth = v.shape[1]
    lane = lax.broadcasted_iota(jnp.int32, v.shape, 1)
    below = jnp.where(lane == 0, 0.0, pltpu.roll(v, 1, 1))
    above = jnp.where(lane == depth - 1, 0.0, pltpu.roll(v, depth - 1, 1))
    return below + above


def plane_part(layer, y):
    v = read(layer, y)
    return read(layer, y, 1) + read(layer, y, -1) + z_sum(v) - 6.0 * v


def clear_margins(layer):
    ref, lead = layer
    zero = jnp.zeros((PAD, ref.shape[-1]), f32)
    ref[(*lead, pl.ds(0, PAD), slice(None))] = zero
    ref[(*lead, pl.ds(ref.shape[-2] - PAD, PAD), slice(None))] = zero


def is_odd():
    return lax.rem(lax.axis_index("slab"), 2) == 1


def stored(d, layers):
    return jnp.where(is_odd(), d, layers - 1 - d)


def has_partner(count):
    position = lax.axis_index("slab")
    above = position < count - 1
    below = position > 0
    odd = is_odd()
    flags = jnp.where(odd, below, above), jnp.where(odd, above, below)
    return [jnp.where(f, 1.0, 0.0).astype(f32) for f in flags]


def copy_all(pairs, sems):
    copies = [pltpu.make_async_copy(s, d, sems.at[i]) for i, (s, d) in enumerate(pairs)]
    for c in copies:
        c.start()
    return copies


def write_message(near, far, missing, out, rows):
    clear_margins(missing)
    for y in starts(rows):
        v = read(near, y)
        rounded = v.astype(bf16)
        out[pl.ds(y, CHUNK), :] = rounded
        write(missing, y, v - rounded.astype(f32))
    for y in starts(rows):
        out[pl.ds(rows + y, CHUNK), :] = (read(far, y) + 2.0 * plane_part(missing, y)).astype(bf16)


def curvature_of(p):
    return 3.0 * p * p - 1.0


def local_step(state, first, phase, row, count, emit):
    layers = len(state)
    rows = phase.shape[1]
    depth = phase.shape[2]
    side_a, side_b = has_partner(count)
    transport = row[0:1, :]
    for d in range(layers):
        for y in starts(rows):
            lap = plane_part(state[d], y)
            if d > 0:
                lap = lap + read(state[d - 1], y)
            if d < layers - 1:
                lap = lap + read(state[d + 1], y)
            write(first[d], y, lap)
    for d in range(layers):
        at = stored(d, layers)
        for y in starts(rows):
            v = read(state[d], y)
            second = plane_part(first[d], y)
            second = second + (read(first[d - 1], y) if d > 0 else side_a * v)
            second = second + (read(first[d + 1], y) if d < layers - 1 else side_b * v)
            p = phase[at, pl.ds(y, CHUNK), :].astype(f32)
            moved = read(state[d], y, 1) - read(state[d], y, -1)
            stepped = (
                v
                + mobility_step * curvature_of(p) * read(first[d], y)
                - stiffness_step * second
                + transport * moved
            )
            emit(d, y, v, stepped)


def padded(rows, depth, layers=None):
    lead = () if layers is None else (layers,)
    return pltpu.VMEM((*lead, rows + 2 * PAD, depth), f32)


def layers_of(ref):
    return [(ref, (d,)) for d in range(ref.shape[0])]


def first_message(adjoint, targets, owners, cells, out, near, far, missing, digits, owner, cell, sems):
    layers, rows, depth = adjoint.shape
    n = targets.shape[0]
    pairs = [(adjoint.at[stored(d, layers)], ref.at[pl.ds(PAD, rows)]) for d, ref in ((0, near), (1, far))]
    pairs += [(targets, out.at[pl.ds(2 * rows, n)]), (owners, owner), (cells, cell)]
    copies = copy_all(pairs, sems)
    digits[...] = jnp.zeros(digits.shape, f32)
    for c in copies[3:]:
        c.wait()
    digits[0:1, 0:n] = owner[...].astype(f32)
    digits[1:2, 0:n] = (cell[...] >> 8).astype(f32)
    digits[2:3, 0:n] = (cell[...] & 255).astype(f32)
    out[pl.ds(2 * rows + n, 16), :] = digits[...].astype(bf16)
    for c in copies[:3]:
        c.wait()
    write_message((near, ()), (far, ()), (missing, ()), out, rows)


def make_first_message(adjoint, targets, owners, cells):
    layers, rows, depth = adjoint.shape
    extra = targets.shape[0] + 16
    row = pltpu.VMEM(owners.shape, jnp.int32)
    return call(
        first_message,
        jax.ShapeDtypeStruct((2 * rows + extra, depth), bf16),
        VMEM,
        [ANY] * 4,
        [padded(rows, depth)] * 3 + [pltpu.VMEM((16, depth), f32), row, row, pltpu.SemaphoreType.DMA((5,))],
        cost(LONG),
    )(*[pltpu.with_memory_space_constraint(v, pltpu.HBM) for v in (adjoint, targets, owners, cells)])


def transport_row(inflow, depth):
    lane = lax.broadcasted_iota(jnp.int32, (8, depth), 1)
    height = (lane.astype(f32) + 0.5) / depth
    return (transport_step * inflow) * (4.0 * height * (1.0 - height))


def first_local(
    count, adjoint, phase, rates, choice, mask, after, out, message, row, masked, near_walls, state, first, missing, sems
):
    layers, rows, depth = adjoint.shape
    copies = copy_all(
        [(adjoint.at[stored(d, layers)], state.at[d, pl.ds(PAD, rows)]) for d in range(layers)], sems
    )
    row[...] = transport_row(rates[choice[0]], depth)
    masked[...] = wall_weight * mask[...].astype(f32)
    for d in range(layers):
        clear_margins((state, (d,)))
        clear_margins((first, (d,)))
    for c in copies:
        c.wait()
    own = layers_of(state)
    write_message(own[-1], own[-2], (missing, ()), message, rows)

    def emit(d, y, v, stepped):
        out[d, pl.ds(y, CHUNK), :] = stepped

    local_step(own, layers_of(first), phase, row, count, emit)
    four = (0, 1, depth - 1, depth - 2)
    two = (0, depth - 1)
    at = stored(layers - 1, layers)
    for y in range(0, rows, 128):
        span = pl.ds(y, 128)
        high, low = split(out[layers - 1, span, :], 2)
        high2, low2 = split(out[layers - 2, span, :], 2)
        picked = pick_rows(high, four, 0, 16) + pick_rows(low, four, 4, 16) + pick_rows(phase[at, span, :], four, 12, 16)
        picked = picked + pick_rows(high2, two, 8, 16) + pick_rows(low2, two, 10, 16)
        message[pl.ds(2 * rows + y // 8, 16), :] = picked.astype(bf16)
        steps = range(y, y + 128, CHUNK)
        near = jnp.concatenate([read(own[-1], k) for k in steps])
        both = jnp.concatenate([read(own[-2], k) + 2.0 * plane_part(own[-1], k) for k in steps])
        near_walls[:, span] = pick_exact(near, four, 0) + pick_exact(both, four, 4)


def make_first_local(adjoint, phase, rates, choice, mask, after, count):
    layers, rows, depth = adjoint.shape
    return call(
        lambda *refs: first_local(count, *refs),
        (
            jax.ShapeDtypeStruct(adjoint.shape, f32),
            jax.ShapeDtypeStruct((2 * rows + rows // 8, depth), bf16),
            jax.ShapeDtypeStruct((8, depth), f32),
            jax.ShapeDtypeStruct(mask.shape, f32),
            jax.ShapeDtypeStruct((8, rows), f32),
        ),
        (VMEM,) * 5,
        [ANY, VMEM, SMEM, SMEM, VMEM, ANY],
        [padded(rows, depth, layers)] * 2 + [padded(rows, depth), pltpu.SemaphoreType.DMA((layers,))],
        cost(LONG),
    )(adjoint, phase, rates, choice, mask, after)


def add_halo(message, edge, inner, halo, phase, at, rows, put_edge, put_inner):
    clear_margins(halo)
    for y in starts(rows):
        near = message[pl.ds(y, CHUNK), :].astype(f32)
        write(halo, y, near)
        put_inner(y, inner(y) - stiffness_step * near)
    for y in starts(rows):
        near = read(halo, y)
        far = message[pl.ds(rows + y, CHUNK), :].astype(f32)
        curvature = curvature_of(phase[at, pl.ds(y, CHUNK), :].astype(f32))
        both = far + 2.0 * plane_part(halo, y)
        put_edge(y, edge(y) + mobility_step * curvature * near - stiffness_step * both)


def pick_rows(v, heights, first_row, rows=8):
    depth = v.shape[1]
    row = lax.broadcasted_iota(jnp.int32, (rows, depth), 0) - first_row
    lane = lax.broadcasted_iota(jnp.int32, (rows, depth), 1)
    pick = jnp.zeros((rows, depth), f32)
    for i, z in enumerate(heights):
        pick = pick + jnp.where((row == i) & (lane == z), 1.0, 0.0)
    return lax.dot_general(pick.astype(bf16), v, (((1,), (1,)), ((), ())), preferred_element_type=f32)


def split(v, parts):
    out = []
    for _ in range(parts):
        high = v.astype(bf16)
        out.append(high)
        v = v - high.astype(f32)
    return out


def pick_exact(v, heights, first_row):
    return sum(pick_rows(part, heights, first_row) for part in split(v, 3))


def wall_rows(v, first_row):
    heights = (0, v.shape[1] - 1)
    return pick_rows(v, heights, first_row) if v.dtype == bf16 else pick_exact(v, heights, first_row)


def join_halo(side, message, pre, phase, out, halo):
    layers, rows, depth = pre.shape
    one, two = (0, 1) if side == 0 else (layers - 1, layers - 2)
    edge, inner = layers_of(out)
    clear_margins(edge)
    clear_margins(inner)
    add_halo(
        message,
        lambda y: pre[one, pl.ds(y, CHUNK), :],
        lambda y: pre[two, pl.ds(y, CHUNK), :],
        (halo, ()),
        phase,
        stored(one, layers),
        rows,
        lambda y, v: write(edge, y, v),
        lambda y, v: write(inner, y, v),
    )


def wall_parts(half, y):
    edge, inner = layers_of(half)
    parts = 0.0
    for i in range(2):
        span = range(y + 128 * i, y + 128 * (i + 1), CHUNK)
        both = jnp.concatenate([read(inner, k) + 2.0 * plane_part(edge, k) for k in span])
        near = jnp.concatenate([read(edge, k) for k in span])
        parts = parts + wall_rows(near, 4 * i) + wall_rows(both, 4 * i + 2)
    return parts


def put_walls(half, out, start):
    rows = half.shape[1] - 2 * PAD
    for y in range(0, rows, 256):
        parts = wall_parts(half, y)
        high = parts.astype(bf16).astype(f32)
        out[pl.ds(start + y // 16, 16), :] = jnp.concatenate([high, parts - high]).astype(bf16)


def middle_a(message, pre, phase, first, out, sent, early, block, halo, missing):
    rows, n = pre.shape[1], block.shape[0] // 2
    join_halo(0, message, pre, phase, out, halo)
    write_message(*layers_of(out), (missing, ()), sent, rows)
    put_walls(out, early, 0)
    block[pl.ds(0, n), :] = first[pl.ds(2 * rows, n), :]
    block[pl.ds(n, n), :] = message[pl.ds(2 * rows, n), :]


def make_middle_a(message, pre, phase, first):
    layers, rows, depth = pre.shape
    extra = first.shape[0] - 2 * rows
    return call(
        middle_a,
        (
            jax.ShapeDtypeStruct((2, rows + 2 * PAD, depth), f32),
            jax.ShapeDtypeStruct((2 * rows, depth), bf16),
            jax.ShapeDtypeStruct((rows // 16, depth), bf16),
            jax.ShapeDtypeStruct((2 * extra, depth), bf16),
        ),
        (VMEM,) * 4,
        [VMEM] * 4,
        [padded(rows, depth)] * 2,
        cost(LONG),
    )(message, pre, phase, first)


def partner_walls(message, near_walls, rows, present):
    sent = [message[pl.ds(2 * rows + y // 8, 16), :].astype(f32) for y in range(0, rows, 128)]
    sent = jnp.concatenate(sent, axis=1)
    here = near_walls[0:4, :]
    near = sent[0:4] + sent[4:8] + mobility_step * curvature_of(sent[12:16]) * here
    near = near - stiffness_step * near_walls[4:8, :]
    far = sent[8:10] + sent[10:12]
    lane = lax.broadcasted_iota(jnp.int32, (1, rows), 1)
    out = []
    for wall in range(2):
        v = near[2 * wall : 2 * wall + 1]
        along = jnp.where(lane == 0, 0.0, pltpu.roll(v, 1, 1)) + jnp.where(lane == rows - 1, 0.0, pltpu.roll(v, rows - 1, 1))
        plane = along + near[2 * wall + 1 : 2 * wall + 2] - 6.0 * v
        both = far[wall : wall + 1] - stiffness_step * here[2 * wall : 2 * wall + 1] + 2.0 * plane
        out.append((present * v, present * both))
    return [out[0][0], out[1][0], out[0][1], out[1][1]]


def middle_b(count, message, pre, phase, near_walls, after, out, sent, walls, halo, missing):
    rows = pre.shape[1]
    join_halo(1, message, pre, phase, out, halo)
    write_message(*layers_of(out), (missing, ()), sent, rows)
    walls[...] = jnp.zeros(walls.shape, f32)
    for i, v in enumerate(partner_walls(message, near_walls, rows, has_partner(count)[1])):
        walls[i : i + 1, :] = v


def make_middle_b(message, pre, phase, near_walls, after, count):
    layers, rows, depth = pre.shape
    return call(
        lambda *refs: middle_b(count, *refs),
        (
            jax.ShapeDtypeStruct((2, rows + 2 * PAD, depth), f32),
            jax.ShapeDtypeStruct((2 * rows, depth), bf16),
            jax.ShapeDtypeStruct((8, rows), f32),
        ),
        (VMEM,) * 3,
        [VMEM] * 4 + [ANY],
        [padded(rows, depth)] * 2,
        cost(6 * 10**8),
    )(message, pre, phase, near_walls, after)


def join(one, two, out):
    n = one.shape[0]
    out[pl.ds(0, n), :] = one[...]
    out[pl.ds(n, n), :] = two[...]


def make_join(one, two):
    return call(
        join,
        jax.ShapeDtypeStruct((2 * one.shape[0], one.shape[1]), bf16),
        VMEM,
        [VMEM, VMEM],
        [],
        cost(15 * 10**8),
    )(one, two)


def second_local(count, side_a, side_b, phase, row, own, other, out, wall, phase_wall, block, first):
    layers, rows, depth = out.shape
    n = own.shape[0]
    block[pl.ds(0, n), :] = own[...]
    block[pl.ds(n, n), :] = other[...]
    own = layers_of(side_a) + layers_of(side_b)[::-1]
    for d in range(layers):
        clear_margins((first, (d,)))
    held = []

    def emit(d, y, v, stepped):
        out[d, pl.ds(y, CHUNK), :] = stepped
        held.append(v + stepped)
        if len(held) * CHUNK == 128:
            start = y + CHUNK - 128
            wall[d, :, pl.ds(start, 128)] = wall_rows(jnp.concatenate(held), 0)
            phase_wall[d, :, pl.ds(start, 128)] = wall_rows(phase[stored(d, layers), pl.ds(start, 128), :], 0)
            held.clear()

    local_step(own, layers_of(first), phase, row, count, emit)


def make_second_local(side_a, side_b, phase, row, own, other, count):
    layers, rows, depth = phase.shape
    return call(
        lambda *refs: second_local(count, *refs),
        (
            jax.ShapeDtypeStruct((layers, rows, depth), f32),
            jax.ShapeDtypeStruct((layers, 8, rows), f32),
            jax.ShapeDtypeStruct((layers, 8, rows), f32),
            jax.ShapeDtypeStruct((2 * own.shape[0], depth), bf16),
        ),
        (VMEM,) * 4,
        [VMEM] * 6,
        [padded(rows, depth, layers)],
        cost(13 * 10**8),
    )(side_a, side_b, phase, row, own, other)


def injection(n, phase, pre, *refs):
    sources, (out, index, rhs) = refs[:-3], refs[-3:]
    layers, rows, depth = out.shape
    position = lax.axis_index("slab").astype(f32)
    rhs[:, :depth] = jnp.ones((rhs.shape[0], depth), bf16)
    at = 0
    for source in sources:
        for first in range(0, source.shape[0], n + 16):
            rhs[pl.ds(at, n), depth:] = source[pl.ds(first, n), :]
            digits = source[pl.ds(first + n, 16), :].astype(f32)
            cell = jnp.where(digits[0:1] == position, digits[1:2] * 256.0 + digits[2:3], -1.0)
            index[0:1, pl.ds(at, n)] = cell[:, :n].astype(jnp.int32)
            at += n
    for d in range(layers):
        at = stored(d, layers)
        for y in range(0, rows, 128):
            cell = lax.broadcasted_iota(jnp.int32, (128, index.shape[1]), 0) + (at * rows + y)
            here = jnp.where(cell == index[0:1, :], 1.0, 0.0).astype(bf16)
            added = jnp.dot(here, rhs[...], preferred_element_type=f32)
            p = phase[at, pl.ds(y, 128), :].astype(f32)
            out[d, pl.ds(y, 128), :] = pre[d, pl.ds(y, 128), :] + (added[:, :depth] * p - added[:, depth:])


def make_injection(phase, n, pre, sources):
    layers, rows, depth = phase.shape
    total = sum(r.shape[0] // (n + 16) * n for r in sources)
    return call(
        lambda *refs: injection(n, *refs),
        jax.ShapeDtypeStruct((layers, rows, depth), f32),
        VMEM,
        [VMEM, VMEM] + [VMEM] * len(sources),
        [pltpu.VMEM((8, total), jnp.int32), pltpu.VMEM((total, 2 * depth), bf16)],
        cost(1),
    )(phase, pre, *sources)


def unpack_walls(message, out):
    for y in range(0, out.shape[1], 256):
        both = message[pl.ds(y // 16, 16), :].astype(f32)
        both = both[:8] + both[8:]
        for i in range(2):
            out[:4, pl.ds(y + 128 * i, 128)] = both[4 * i : 4 * i + 4]


def wall_kernel(wall, phase_wall, early_a, from_b, mask, out, from_a):
    layers = wall.shape[0]
    unpack_walls(early_a, from_a)
    odd = is_odd()
    terms = []
    for d in range(layers):
        p = phase_wall[d, :2, :]
        w = wall[d, :2, :]
        for halo, off in ((from_a, d), (from_b, layers - 1 - d)):
            if off == 0:
                w = w + mobility_step * curvature_of(p) * halo[:2] - stiffness_step * halo[2:4]
            elif off == 1:
                w = w - stiffness_step * halo[:2]
        terms.append((1.0 - p * p) * w)
    for l in range(layers):
        out[:, l, :] = mask[:, l, :] * jnp.where(odd, terms[l], terms[layers - 1 - l])


def make_walls(wall, phase_wall, early_a, from_b, mask):
    return call(
        wall_kernel,
        jax.ShapeDtypeStruct(mask.shape, f32),
        VMEM,
        [VMEM] * 5,
        [pltpu.VMEM(wall.shape[1:], f32)],
        cost(3 * 10**8),
    )(wall, phase_wall, early_a, from_b, mask)


def layers_at_a(message, phase, state, out, halo):
    layers = state.shape[0]

    def put(d):
        def store(y, v):
            out[d, pl.ds(y, CHUNK), :] = v

        return store

    def get(d):
        return lambda y: state[d, pl.ds(y, CHUNK), :]

    add_halo(message, get(0), get(1), (halo, ()), phase, stored(0, layers), phase.shape[1], put(0), put(1))


def make_layers_at_a(message, phase, state):
    layers, rows, depth = phase.shape
    return call(
        layers_at_a,
        jax.ShapeDtypeStruct((2, rows, depth), f32),
        VMEM,
        [VMEM] * 3,
        [padded(rows, depth)],
        cost(15 * 10**8),
    )(message, phase, state)


def final(at_a, message_b, state, phase, *refs):
    walls, (out, total, planes, summed, halo, sems) = refs[:-6], refs[-6:]
    layers, rows, depth = state.shape
    half = rows // 2
    copies = []

    def send(source, target):
        c = pltpu.make_async_copy(source, target, sems.at[len(copies)])
        c.start()
        copies.append(c)

    for d in range(2):
        send(at_a.at[d], out.at[stored(d, layers)])
    if len(walls) == 4:
        summed[...] = (walls[0][...] + walls[3][...]) + (walls[1][...] + walls[2][...])
    else:
        summed[...] = walls[0][...]
    send(summed, total)

    def put(i):
        def store(y, v):
            planes[i, pl.ds(y, CHUNK), :] = v
            if (y + CHUNK) % half == 0:
                span = pl.ds(y + CHUNK - half, half)
                send(planes.at[i, span], out.at[stored(layers - 1 - i, layers), span])

        return store

    def get(d):
        return lambda y: state[d, pl.ds(y, CHUNK), :]

    one, two = layers - 1, layers - 2
    add_halo(message_b, get(one), get(two), (halo, ()), phase, stored(one, layers), rows, put(0), put(1))
    for c in copies:
        c.wait()


def make_final(at_a, message_b, state, phase, walls):
    layers, rows, depth = state.shape
    return call(
        final,
        (jax.ShapeDtypeStruct(state.shape, f32), jax.ShapeDtypeStruct(walls[0].shape, f32)),
        (ANY, ANY),
        [VMEM] * (4 + len(walls)),
        [
            pltpu.VMEM((2, rows, depth), f32),
            pltpu.VMEM(walls[0].shape, f32),
            padded(rows, depth),
            pltpu.SemaphoreType.DMA((7,)),
        ],
        cost(1),
    )(at_a, message_b, state, phase, *walls)


def on_device(adjoint, phase, targets, owners, target_cell, rate_index, inflow_rates, wall_mask):
    state, phase, targets = adjoint[0], phase[0], targets[0]
    owners = owners.reshape(target_cell.shape)
    count = lax.axis_size("slab")
    pairs = (
        [(i, i ^ 1) for i in range(count) if i ^ 1 < count],
        [(i, i + 1) for i in range(1, count - 1, 2)] + [(i + 1, i) for i in range(1, count - 1, 2)],
    )

    def send(v, side):
        return lax.ppermute(v, "slab", pairs[side])

    rows, n = state.shape[1], targets.shape[0]
    few = count == 8
    first = make_first_message(state, targets, owners, target_cell)
    from_a = send(first, 0)
    pre, message, row, mask, near_walls = make_first_local(state, phase, inflow_rates, rate_index, wall_mask, first, count)
    from_b = send(message, 1)
    half_a, message, early, pair = make_middle_a(from_a, pre, phase, first)
    early = send(early, 0)
    later_a = send(message, 0)
    four = far = pair
    if few:
        four = make_join(pair, lax.ppermute(pair, "slab", [(i, i ^ 4) for i in range(count)]))
        far = lax.ppermute(four, "slab", [(i, i ^ 2) for i in range(count)])
    half_b, message, walls_b = make_middle_b(from_b, pre, phase, near_walls, four, count)
    later_b = send(message, 1)
    pre, wall, phase_wall, block = make_second_local(half_a, half_b, phase, row, four, far, count)
    if not few:
        block = lax.all_gather(first[2 * state.shape[1] :], "slab", axis=0, tiled=True)
    part = make_walls(wall, phase_wall, early, walls_b, mask)
    if lax.axis_size("cond") == 4:
        walls = [part] + [lax.ppermute(part, "cond", [(i, i ^ k) for i in range(4)]) for k in (3, 2, 1)]
    else:
        walls = [lax.psum(part, "cond")]
    state = make_injection(phase, n, pre, [block])
    at_a = make_layers_at_a(later_a, phase, state)
    out, wall_gradient = make_final(at_a, later_b, state, phase, walls)
    return out[None], wall_gradient


def solution(mesh):
    in_specs = (
        P("cond", "slab", None, None),
        P("cond", "slab", None, None),
        P("cond", "slab", None),
        P("cond", "slab", None),
        P("cond", "slab"),
        P("cond"),
        P(),
        P(None, "slab", None),
    )
    out_specs = (P("cond", "slab", None, None), P(None, "slab", None))
    return jax.shard_map(
        on_device, mesh=mesh, in_specs=in_specs, out_specs=out_specs, check_vma=False
    )
```

```python
import jax
import jax.numpy as jnp
from jax import lax
from jax.experimental import pallas as pl
from jax.experimental.pallas import tpu as pltpu
from jax.sharding import PartitionSpec as P

mobility_step = 0.02
stiffness_step = 0.01
transport_step = 0.125
wall_weight = 0.25

f32 = jnp.float32
bf16 = jnp.bfloat16
CHUNK = 64
LONG = 10**10
PAD = 8
ANY = pl.BlockSpec(memory_space=pl.ANY)
HBM = pl.BlockSpec(memory_space=pltpu.HBM)
VMEM = pl.BlockSpec(memory_space=pltpu.VMEM)
SMEM = pl.BlockSpec(memory_space=pltpu.SMEM)


def cost(flops):
    return pl.CostEstimate(flops=flops, bytes_accessed=1, transcendentals=0)


def call(kernel, outs, out_specs, in_specs, scratch, estimate, aliases=None, limit=12):
    return pl.pallas_call(
        kernel,
        out_shape=outs,
        out_specs=out_specs,
        in_specs=in_specs,
        scratch_shapes=scratch,
        input_output_aliases=aliases or {},
        cost_estimate=estimate,
        compiler_params=pltpu.CompilerParams(vmem_limit_bytes=limit * 1024 * 1024),
    )


def starts(rows):
    return range(0, rows, CHUNK)


def read(layer, y, shift=0):
    ref, lead = layer
    return ref[(*lead, pl.ds(PAD + y + shift, CHUNK), slice(None))]


def write(layer, y, v):
    ref, lead = layer
    ref[(*lead, pl.ds(PAD + y, CHUNK), slice(None))] = v


def z_sum(v):
    depth = v.shape[1]
    lane = lax.broadcasted_iota(jnp.int32, v.shape, 1)
    below = jnp.where(lane == 0, 0.0, pltpu.roll(v, 1, 1))
    above = jnp.where(lane == depth - 1, 0.0, pltpu.roll(v, depth - 1, 1))
    return below + above


def plane_part(layer, y):
    v = read(layer, y)
    return read(layer, y, 1) + read(layer, y, -1) + z_sum(v) - 6.0 * v


def clear_margins(layer):
    ref, lead = layer
    zero = jnp.zeros((PAD, ref.shape[-1]), f32)
    ref[(*lead, pl.ds(0, PAD), slice(None))] = zero
    ref[(*lead, pl.ds(ref.shape[-2] - PAD, PAD), slice(None))] = zero


def is_odd():
    return lax.rem(lax.axis_index("slab"), 2) == 1


def stored(d, layers):
    return jnp.where(is_odd(), d, layers - 1 - d)


def has_partner(count):
    position = lax.axis_index("slab")
    above = position < count - 1
    below = position > 0
    odd = is_odd()
    flags = jnp.where(odd, below, above), jnp.where(odd, above, below)
    return [jnp.where(f, 1.0, 0.0).astype(f32) for f in flags]


def copy_all(pairs, sems):
    copies = [pltpu.make_async_copy(s, d, sems.at[i]) for i, (s, d) in enumerate(pairs)]
    for c in copies:
        c.start()
    return copies


def write_message(near, far, missing, out, rows):
    clear_margins(missing)
    for y in starts(rows):
        v = read(near, y)
        rounded = v.astype(bf16)
        out[pl.ds(y, CHUNK), :] = rounded
        write(missing, y, v - rounded.astype(f32))
    for y in starts(rows):
        out[pl.ds(rows + y, CHUNK), :] = (read(far, y) + 2.0 * plane_part(missing, y)).astype(bf16)


def curvature_of(p):
    return 3.0 * p * p - 1.0


def local_step(state, first, phase, row, count, emit):
    layers = len(state)
    rows = phase.shape[1]
    depth = phase.shape[2]
    side_a, side_b = has_partner(count)
    transport = row[0:1, :]
    for d in range(layers):
        for y in starts(rows):
            lap = plane_part(state[d], y)
            if d > 0:
                lap = lap + read(state[d - 1], y)
            if d < layers - 1:
                lap = lap + read(state[d + 1], y)
            write(first[d], y, lap)
    for d in range(layers):
        at = stored(d, layers)
        for y in starts(rows):
            v = read(state[d], y)
            second = plane_part(first[d], y)
            second = second + (read(first[d - 1], y) if d > 0 else side_a * v)
            second = second + (read(first[d + 1], y) if d < layers - 1 else side_b * v)
            p = phase[at, pl.ds(y, CHUNK), :].astype(f32)
            moved = read(state[d], y, 1) - read(state[d], y, -1)
            stepped = (
                v
                + mobility_step * curvature_of(p) * read(first[d], y)
                - stiffness_step * second
                + transport * moved
            )
            emit(d, y, v, stepped)


def padded(rows, depth, layers=None):
    lead = () if layers is None else (layers,)
    return pltpu.VMEM((*lead, rows + 2 * PAD, depth), f32)


def layers_of(ref):
    return [(ref, (d,)) for d in range(ref.shape[0])]


def first_message(adjoint, targets, owners, cells, rates, out, held, near, far, missing, digits, owner, cell, sems):
    layers, rows, depth = adjoint.shape
    n = targets.shape[0]
    pairs = [(adjoint.at[stored(d, layers)], ref.at[pl.ds(PAD, rows)]) for d, ref in ((0, near), (1, far))]
    pairs += [(targets, out.at[pl.ds(2 * rows, n)]), (owners, owner), (cells, cell), (rates, held)]
    copies = copy_all(pairs, sems)
    digits[...] = jnp.zeros(digits.shape, f32)
    for c in copies[3:]:
        c.wait()
    digits[0:1, 0:n] = owner[...].astype(f32)
    digits[1:2, 0:n] = (cell[...] >> 8).astype(f32)
    digits[2:3, 0:n] = (cell[...] & 255).astype(f32)
    out[pl.ds(2 * rows + n, 16), :] = digits[...].astype(bf16)
    for c in copies[:3]:
        c.wait()
    write_message((near, ()), (far, ()), (missing, ()), out, rows)


def make_first_message(adjoint, targets, owners, cells, rates):
    layers, rows, depth = adjoint.shape
    extra = targets.shape[0] + 16
    row = pltpu.VMEM(owners.shape, jnp.int32)
    return call(
        first_message,
        (jax.ShapeDtypeStruct((2 * rows + extra, depth), bf16), jax.ShapeDtypeStruct(rates.shape, f32)),
        (VMEM, VMEM),
        [ANY] * 5,
        [padded(rows, depth)] * 3 + [pltpu.VMEM((16, depth), f32), row, row, pltpu.SemaphoreType.DMA((6,))],
        cost(LONG),
    )(*[pltpu.with_memory_space_constraint(v, pltpu.HBM) for v in (adjoint, targets, owners, cells, rates)])


def transport_row(inflow, depth):
    lane = lax.broadcasted_iota(jnp.int32, (8, depth), 1)
    height = (lane.astype(f32) + 0.5) / depth
    return (transport_step * inflow) * (4.0 * height * (1.0 - height))


def first_local(
    count, adjoint, phase, rates, choice, mask, after, out, message, row, masked, near_walls, state, first, missing, sems
):
    layers, rows, depth = adjoint.shape
    copies = copy_all(
        [(adjoint.at[stored(d, layers)], state.at[d, pl.ds(PAD, rows)]) for d in range(layers)], sems
    )
    row[...] = transport_row(rates[0, choice[0]], depth)
    masked[...] = wall_weight * mask[...].astype(f32)
    for d in range(layers):
        clear_margins((state, (d,)))
        clear_margins((first, (d,)))
    for c in copies:
        c.wait()
    own = layers_of(state)
    write_message(own[-1], own[-2], (missing, ()), message, rows)

    def emit(d, y, v, stepped):
        out[d, pl.ds(y, CHUNK), :] = stepped

    local_step(own, layers_of(first), phase, row, count, emit)
    four = (0, 1, depth - 1, depth - 2)
    two = (0, depth - 1)
    at = stored(layers - 1, layers)
    for y in range(0, rows, 128):
        span = pl.ds(y, 128)
        high, low = split(out[layers - 1, span, :], 2)
        high2, low2 = split(out[layers - 2, span, :], 2)
        picked = pick_rows(high, four, 0, 16) + pick_rows(low, four, 4, 16) + pick_rows(phase[at, span, :], four, 12, 16)
        picked = picked + pick_rows(high2, two, 8, 16) + pick_rows(low2, two, 10, 16)
        message[pl.ds(2 * rows + y // 8, 16), :] = picked.astype(bf16)
        steps = range(y, y + 128, CHUNK)
        near = jnp.concatenate([read(own[-1], k) for k in steps])
        both = jnp.concatenate([read(own[-2], k) + 2.0 * plane_part(own[-1], k) for k in steps])
        near_walls[:, span] = pick_exact(near, four, 0) + pick_exact(both, four, 4)


def make_first_local(adjoint, phase, rates, choice, mask, after, count):
    layers, rows, depth = adjoint.shape
    return call(
        lambda *refs: first_local(count, *refs),
        (
            jax.ShapeDtypeStruct(adjoint.shape, f32),
            jax.ShapeDtypeStruct((2 * rows + rows // 8, depth), bf16),
            jax.ShapeDtypeStruct((8, depth), f32),
            jax.ShapeDtypeStruct(mask.shape, f32),
            jax.ShapeDtypeStruct((8, rows), f32),
        ),
        (VMEM,) * 5,
        [ANY, VMEM, SMEM, SMEM, VMEM, ANY],
        [padded(rows, depth, layers)] * 2 + [padded(rows, depth), pltpu.SemaphoreType.DMA((layers,))],
        cost(LONG),
    )(adjoint, phase, rates, choice, mask, after)


def add_halo(message, edge, inner, halo, phase, at, rows, put_edge, put_inner):
    clear_margins(halo)
    for y in starts(rows):
        near = message[pl.ds(y, CHUNK), :].astype(f32)
        write(halo, y, near)
        put_inner(y, inner(y) - stiffness_step * near)
    for y in starts(rows):
        near = read(halo, y)
        far = message[pl.ds(rows + y, CHUNK), :].astype(f32)
        curvature = curvature_of(phase[at, pl.ds(y, CHUNK), :].astype(f32))
        both = far + 2.0 * plane_part(halo, y)
        put_edge(y, edge(y) + mobility_step * curvature * near - stiffness_step * both)


def pick_rows(v, heights, first_row, rows=8):
    depth = v.shape[1]
    row = lax.broadcasted_iota(jnp.int32, (rows, depth), 0) - first_row
    lane = lax.broadcasted_iota(jnp.int32, (rows, depth), 1)
    pick = jnp.zeros((rows, depth), f32)
    for i, z in enumerate(heights):
        pick = pick + jnp.where((row == i) & (lane == z), 1.0, 0.0)
    return lax.dot_general(pick.astype(bf16), v, (((1,), (1,)), ((), ())), preferred_element_type=f32)


def split(v, parts):
    out = []
    for _ in range(parts):
        high = v.astype(bf16)
        out.append(high)
        v = v - high.astype(f32)
    return out


def pick_exact(v, heights, first_row):
    return sum(pick_rows(part, heights, first_row) for part in split(v, 3))


def wall_rows(v, first_row):
    heights = (0, v.shape[1] - 1)
    return pick_rows(v, heights, first_row) if v.dtype == bf16 else pick_exact(v, heights, first_row)


def join_halo(side, message, pre, phase, out, halo):
    layers, rows, depth = pre.shape
    one, two = (0, 1) if side == 0 else (layers - 1, layers - 2)
    edge, inner = layers_of(out)
    clear_margins(edge)
    clear_margins(inner)
    add_halo(
        message,
        lambda y: pre[one, pl.ds(y, CHUNK), :],
        lambda y: pre[two, pl.ds(y, CHUNK), :],
        (halo, ()),
        phase,
        stored(one, layers),
        rows,
        lambda y, v: write(edge, y, v),
        lambda y, v: write(inner, y, v),
    )


def wall_parts(half, y):
    edge, inner = layers_of(half)
    parts = 0.0
    for i in range(2):
        span = range(y + 128 * i, y + 128 * (i + 1), CHUNK)
        both = jnp.concatenate([read(inner, k) + 2.0 * plane_part(edge, k) for k in span])
        near = jnp.concatenate([read(edge, k) for k in span])
        parts = parts + wall_rows(near, 4 * i) + wall_rows(both, 4 * i + 2)
    return parts


def put_walls(half, out, start):
    rows = half.shape[1] - 2 * PAD
    for y in range(0, rows, 256):
        parts = wall_parts(half, y)
        high = parts.astype(bf16).astype(f32)
        out[pl.ds(start + y // 16, 16), :] = jnp.concatenate([high, parts - high]).astype(bf16)


def middle_a(message, pre, phase, first, out, sent, early, block, halo, missing):
    rows, n = pre.shape[1], block.shape[0] // 2
    join_halo(0, message, pre, phase, out, halo)
    write_message(*layers_of(out), (missing, ()), sent, rows)
    put_walls(out, early, 0)
    block[pl.ds(0, n), :] = first[pl.ds(2 * rows, n), :]
    block[pl.ds(n, n), :] = message[pl.ds(2 * rows, n), :]


def make_middle_a(message, pre, phase, first):
    layers, rows, depth = pre.shape
    extra = first.shape[0] - 2 * rows
    return call(
        middle_a,
        (
            jax.ShapeDtypeStruct((2, rows + 2 * PAD, depth), f32),
            jax.ShapeDtypeStruct((2 * rows, depth), bf16),
            jax.ShapeDtypeStruct((rows // 16, depth), bf16),
            jax.ShapeDtypeStruct((2 * extra, depth), bf16),
        ),
        (VMEM,) * 4,
        [VMEM] * 4,
        [padded(rows, depth)] * 2,
        cost(LONG),
    )(message, pre, phase, first)


def partner_walls(message, near_walls, rows, present):
    sent = [message[pl.ds(2 * rows + y // 8, 16), :].astype(f32) for y in range(0, rows, 128)]
    sent = jnp.concatenate(sent, axis=1)
    here = near_walls[0:4, :]
    near = sent[0:4] + sent[4:8] + mobility_step * curvature_of(sent[12:16]) * here
    near = near - stiffness_step * near_walls[4:8, :]
    far = sent[8:10] + sent[10:12]
    lane = lax.broadcasted_iota(jnp.int32, (1, rows), 1)
    out = []
    for wall in range(2):
        v = near[2 * wall : 2 * wall + 1]
        along = jnp.where(lane == 0, 0.0, pltpu.roll(v, 1, 1)) + jnp.where(lane == rows - 1, 0.0, pltpu.roll(v, rows - 1, 1))
        plane = along + near[2 * wall + 1 : 2 * wall + 2] - 6.0 * v
        both = far[wall : wall + 1] - stiffness_step * here[2 * wall : 2 * wall + 1] + 2.0 * plane
        out.append((present * v, present * both))
    return [out[0][0], out[1][0], out[0][1], out[1][1]]


def middle_b(count, message, pre, phase, near_walls, after, out, sent, walls, halo, missing):
    rows = pre.shape[1]
    join_halo(1, message, pre, phase, out, halo)
    write_message(*layers_of(out), (missing, ()), sent, rows)
    walls[...] = jnp.zeros(walls.shape, f32)
    for i, v in enumerate(partner_walls(message, near_walls, rows, has_partner(count)[1])):
        walls[i : i + 1, :] = v


def make_middle_b(message, pre, phase, near_walls, after, count):
    layers, rows, depth = pre.shape
    return call(
        lambda *refs: middle_b(count, *refs),
        (
            jax.ShapeDtypeStruct((2, rows + 2 * PAD, depth), f32),
            jax.ShapeDtypeStruct((2 * rows, depth), bf16),
            jax.ShapeDtypeStruct((8, rows), f32),
        ),
        (VMEM,) * 3,
        [VMEM] * 4 + [ANY],
        [padded(rows, depth)] * 2,
        cost(6 * 10**8),
    )(message, pre, phase, near_walls, after)


def join(one, two, out):
    n = one.shape[0]
    out[pl.ds(0, n), :] = one[...]
    out[pl.ds(n, n), :] = two[...]


def make_join(one, two):
    return call(
        join,
        jax.ShapeDtypeStruct((2 * one.shape[0], one.shape[1]), bf16),
        VMEM,
        [VMEM, VMEM],
        [],
        cost(15 * 10**8),
    )(one, two)


def second_local(count, side_a, side_b, phase, row, own, other, out, wall, phase_wall, block, first):
    layers, rows, depth = out.shape
    n = own.shape[0]
    block[pl.ds(0, n), :] = own[...]
    block[pl.ds(n, n), :] = other[...]
    own = layers_of(side_a) + layers_of(side_b)[::-1]
    for d in range(layers):
        clear_margins((first, (d,)))
    held = []

    def emit(d, y, v, stepped):
        out[d, pl.ds(y, CHUNK), :] = stepped
        held.append(v + stepped)
        if len(held) * CHUNK == 128:
            start = y + CHUNK - 128
            wall[d, :, pl.ds(start, 128)] = wall_rows(jnp.concatenate(held), 0)
            phase_wall[d, :, pl.ds(start, 128)] = wall_rows(phase[stored(d, layers), pl.ds(start, 128), :], 0)
            held.clear()

    local_step(own, layers_of(first), phase, row, count, emit)


def make_second_local(side_a, side_b, phase, row, own, other, count):
    layers, rows, depth = phase.shape
    return call(
        lambda *refs: second_local(count, *refs),
        (
            jax.ShapeDtypeStruct((layers, rows, depth), f32),
            jax.ShapeDtypeStruct((layers, 8, rows), f32),
            jax.ShapeDtypeStruct((layers, 8, rows), f32),
            jax.ShapeDtypeStruct((2 * own.shape[0], depth), bf16),
        ),
        (VMEM,) * 4,
        [VMEM] * 6,
        [padded(rows, depth, layers)],
        cost(13 * 10**8),
    )(side_a, side_b, phase, row, own, other)


def injection(n, phase, pre, *refs):
    sources, (out, index, rhs) = refs[:-3], refs[-3:]
    layers, rows, depth = out.shape
    position = lax.axis_index("slab").astype(f32)
    rhs[:, :depth] = jnp.ones((rhs.shape[0], depth), bf16)
    at = 0
    for source in sources:
        for first in range(0, source.shape[0], n + 16):
            rhs[pl.ds(at, n), depth:] = source[pl.ds(first, n), :]
            digits = source[pl.ds(first + n, 16), :].astype(f32)
            cell = jnp.where(digits[0:1] == position, digits[1:2] * 256.0 + digits[2:3], -1.0)
            index[0:1, pl.ds(at, n)] = cell[:, :n].astype(jnp.int32)
            at += n
    for d in range(layers):
        at = stored(d, layers)
        for y in range(0, rows, 128):
            cell = lax.broadcasted_iota(jnp.int32, (128, index.shape[1]), 0) + (at * rows + y)
            here = jnp.where(cell == index[0:1, :], 1.0, 0.0).astype(bf16)
            added = jnp.dot(here, rhs[...], preferred_element_type=f32)
            p = phase[at, pl.ds(y, 128), :].astype(f32)
            out[d, pl.ds(y, 128), :] = pre[d, pl.ds(y, 128), :] + (added[:, :depth] * p - added[:, depth:])


def make_injection(phase, n, pre, sources):
    layers, rows, depth = phase.shape
    total = sum(r.shape[0] // (n + 16) * n for r in sources)
    return call(
        lambda *refs: injection(n, *refs),
        jax.ShapeDtypeStruct((layers, rows, depth), f32),
        VMEM,
        [VMEM, VMEM] + [VMEM] * len(sources),
        [pltpu.VMEM((8, total), jnp.int32), pltpu.VMEM((total, 2 * depth), bf16)],
        cost(1),
    )(phase, pre, *sources)


def unpack_walls(message, out):
    for y in range(0, out.shape[1], 256):
        both = message[pl.ds(y // 16, 16), :].astype(f32)
        both = both[:8] + both[8:]
        for i in range(2):
            out[:4, pl.ds(y + 128 * i, 128)] = both[4 * i : 4 * i + 4]


def wall_kernel(wall, phase_wall, early_a, from_b, mask, out, from_a):
    layers = wall.shape[0]
    unpack_walls(early_a, from_a)
    odd = is_odd()
    terms = []
    for d in range(layers):
        p = phase_wall[d, :2, :]
        w = wall[d, :2, :]
        for halo, off in ((from_a, d), (from_b, layers - 1 - d)):
            if off == 0:
                w = w + mobility_step * curvature_of(p) * halo[:2] - stiffness_step * halo[2:4]
            elif off == 1:
                w = w - stiffness_step * halo[:2]
        terms.append((1.0 - p * p) * w)
    for l in range(layers):
        out[:, l, :] = mask[:, l, :] * jnp.where(odd, terms[l], terms[layers - 1 - l])


def make_walls(wall, phase_wall, early_a, from_b, mask):
    return call(
        wall_kernel,
        jax.ShapeDtypeStruct(mask.shape, f32),
        VMEM,
        [VMEM] * 5,
        [pltpu.VMEM(wall.shape[1:], f32)],
        cost(3 * 10**8),
    )(wall, phase_wall, early_a, from_b, mask)


def layers_at_a(message, phase, state, out, halo):
    layers = state.shape[0]

    def put(d):
        def store(y, v):
            out[d, pl.ds(y, CHUNK), :] = v

        return store

    def get(d):
        return lambda y: state[d, pl.ds(y, CHUNK), :]

    add_halo(message, get(0), get(1), (halo, ()), phase, stored(0, layers), phase.shape[1], put(0), put(1))


def make_layers_at_a(message, phase, state):
    layers, rows, depth = phase.shape
    return call(
        layers_at_a,
        jax.ShapeDtypeStruct((2, rows, depth), f32),
        VMEM,
        [VMEM] * 3,
        [padded(rows, depth)],
        cost(15 * 10**8),
    )(message, phase, state)


def final(at_a, message_b, state, phase, *refs):
    walls, (out, total, planes, summed, halo, sems) = refs[:-6], refs[-6:]
    layers, rows, depth = state.shape
    half = rows // 2
    copies = []

    def send(source, target):
        c = pltpu.make_async_copy(source, target, sems.at[len(copies)])
        c.start()
        copies.append(c)

    for d in range(2):
        send(at_a.at[d], out.at[stored(d, layers)])
    if len(walls) == 4:
        summed[...] = (walls[0][...] + walls[3][...]) + (walls[1][...] + walls[2][...])
    else:
        summed[...] = walls[0][...]
    send(summed, total)

    def put(i):
        def store(y, v):
            planes[i, pl.ds(y, CHUNK), :] = v
            if (y + CHUNK) % half == 0:
                span = pl.ds(y + CHUNK - half, half)
                send(planes.at[i, span], out.at[stored(layers - 1 - i, layers), span])

        return store

    def get(d):
        return lambda y: state[d, pl.ds(y, CHUNK), :]

    one, two = layers - 1, layers - 2
    add_halo(message_b, get(one), get(two), (halo, ()), phase, stored(one, layers), rows, put(0), put(1))
    for c in copies:
        c.wait()


def make_final(at_a, message_b, state, phase, walls):
    layers, rows, depth = state.shape
    return call(
        final,
        (jax.ShapeDtypeStruct(state.shape, f32), jax.ShapeDtypeStruct(walls[0].shape, f32)),
        (ANY, ANY),
        [VMEM] * (4 + len(walls)),
        [
            pltpu.VMEM((2, rows, depth), f32),
            pltpu.VMEM(walls[0].shape, f32),
            padded(rows, depth),
            pltpu.SemaphoreType.DMA((7,)),
        ],
        cost(1),
    )(at_a, message_b, state, phase, *walls)


def on_device(adjoint, phase, targets, owners, target_cell, rate_index, inflow_rates, wall_mask):
    state, phase, targets = adjoint[0], phase[0], targets[0]
    owners = owners.reshape(target_cell.shape)
    count = lax.axis_size("slab")
    pairs = (
        [(i, i ^ 1) for i in range(count) if i ^ 1 < count],
        [(i, i + 1) for i in range(1, count - 1, 2)] + [(i + 1, i) for i in range(1, count - 1, 2)],
    )

    def send(v, side):
        return lax.ppermute(v, "slab", pairs[side])

    rows, n = state.shape[1], targets.shape[0]
    few = count == 8
    first, rates = make_first_message(state, targets, owners, target_cell, inflow_rates[None])
    from_a = send(first, 0)
    pre, message, row, mask, near_walls = make_first_local(state, phase, rates, rate_index, wall_mask, first, count)
    from_b = send(message, 1)
    half_a, message, early, pair = make_middle_a(from_a, pre, phase, first)
    early = send(early, 0)
    later_a = send(message, 0)
    four = far = pair
    if few:
        four = make_join(pair, lax.ppermute(pair, "slab", [(i, i ^ 2) for i in range(count)]))
        far = lax.ppermute(four, "slab", [(i, i ^ 4) for i in range(count)])
    half_b, message, walls_b = make_middle_b(from_b, pre, phase, near_walls, four, count)
    later_b = send(message, 1)
    pre, wall, phase_wall, block = make_second_local(half_a, half_b, phase, row, four, far, count)
    if not few:
        block = lax.all_gather(first[2 * state.shape[1] :], "slab", axis=0, tiled=True)
    part = make_walls(wall, phase_wall, early, walls_b, mask)
    if lax.axis_size("cond") == 4:
        walls = [part] + [lax.ppermute(part, "cond", [(i, i ^ k) for i in range(4)]) for k in (3, 2, 1)]
    else:
        walls = [lax.psum(part, "cond")]
    state = make_injection(phase, n, pre, [block])
    at_a = make_layers_at_a(later_a, phase, state)
    out, wall_gradient = make_final(at_a, later_b, state, phase, walls)
    return out[None], wall_gradient


def solution(mesh):
    in_specs = (
        P("cond", "slab", None, None),
        P("cond", "slab", None, None),
        P("cond", "slab", None),
        P("cond", "slab", None),
        P("cond", "slab"),
        P("cond"),
        P(),
        P(None, "slab", None),
    )
    out_specs = (P("cond", "slab", None, None), P(None, "slab", None))
    return jax.shard_map(
        on_device, mesh=mesh, in_specs=in_specs, out_specs=out_specs, check_vma=False
    )
```

```python
import jax
import jax.numpy as jnp
from jax import lax
from jax.experimental import pallas as pl
from jax.experimental.pallas import tpu as pltpu
from jax.sharding import PartitionSpec as P

mobility_step = 0.02
stiffness_step = 0.01
transport_step = 0.125
wall_weight = 0.25

f32 = jnp.float32
bf16 = jnp.bfloat16
CHUNK = 64
LONG = 10**10
PAD = 8
ANY = pl.BlockSpec(memory_space=pl.ANY)
HBM = pl.BlockSpec(memory_space=pltpu.HBM)
VMEM = pl.BlockSpec(memory_space=pltpu.VMEM)
SMEM = pl.BlockSpec(memory_space=pltpu.SMEM)


def cost(flops):
    return pl.CostEstimate(flops=flops, bytes_accessed=1, transcendentals=0)


def call(kernel, outs, out_specs, in_specs, scratch, estimate, aliases=None, limit=12):
    return pl.pallas_call(
        kernel,
        out_shape=outs,
        out_specs=out_specs,
        in_specs=in_specs,
        scratch_shapes=scratch,
        input_output_aliases=aliases or {},
        cost_estimate=estimate,
        compiler_params=pltpu.CompilerParams(vmem_limit_bytes=limit * 1024 * 1024),
    )


def starts(rows):
    return range(0, rows, CHUNK)


def read(layer, y, shift=0):
    ref, lead = layer
    return ref[(*lead, pl.ds(PAD + y + shift, CHUNK), slice(None))]


def write(layer, y, v):
    ref, lead = layer
    ref[(*lead, pl.ds(PAD + y, CHUNK), slice(None))] = v


def z_sum(v):
    depth = v.shape[1]
    lane = lax.broadcasted_iota(jnp.int32, v.shape, 1)
    below = jnp.where(lane == 0, 0.0, pltpu.roll(v, 1, 1))
    above = jnp.where(lane == depth - 1, 0.0, pltpu.roll(v, depth - 1, 1))
    return below + above


def plane_part(layer, y):
    v = read(layer, y)
    return read(layer, y, 1) + read(layer, y, -1) + z_sum(v) - 6.0 * v


def clear_margins(layer):
    ref, lead = layer
    zero = jnp.zeros((PAD, ref.shape[-1]), f32)
    ref[(*lead, pl.ds(0, PAD), slice(None))] = zero
    ref[(*lead, pl.ds(ref.shape[-2] - PAD, PAD), slice(None))] = zero


def is_odd():
    return lax.rem(lax.axis_index("slab"), 2) == 1


def stored(d, layers):
    return jnp.where(is_odd(), d, layers - 1 - d)


def has_partner(count):
    position = lax.axis_index("slab")
    above = position < count - 1
    below = position > 0
    odd = is_odd()
    flags = jnp.where(odd, below, above), jnp.where(odd, above, below)
    return [jnp.where(f, 1.0, 0.0).astype(f32) for f in flags]


def copy_all(pairs, sems):
    copies = [pltpu.make_async_copy(s, d, sems.at[i]) for i, (s, d) in enumerate(pairs)]
    for c in copies:
        c.start()
    return copies


def write_message(near, far, missing, out, rows):
    clear_margins(missing)
    for y in starts(rows):
        v = read(near, y)
        rounded = v.astype(bf16)
        out[pl.ds(y, CHUNK), :] = rounded
        write(missing, y, v - rounded.astype(f32))
    for y in starts(rows):
        out[pl.ds(rows + y, CHUNK), :] = (read(far, y) + 2.0 * plane_part(missing, y)).astype(bf16)


def curvature_of(p):
    return 3.0 * p * p - 1.0


def local_step(state, first, phase, row, count, emit):
    layers = len(state)
    rows = phase.shape[1]
    depth = phase.shape[2]
    side_a, side_b = has_partner(count)
    transport = row[0:1, :]
    for d in range(layers):
        for y in starts(rows):
            lap = plane_part(state[d], y)
            if d > 0:
                lap = lap + read(state[d - 1], y)
            if d < layers - 1:
                lap = lap + read(state[d + 1], y)
            write(first[d], y, lap)
    for d in range(layers):
        at = stored(d, layers)
        for y in starts(rows):
            v = read(state[d], y)
            second = plane_part(first[d], y)
            second = second + (read(first[d - 1], y) if d > 0 else side_a * v)
            second = second + (read(first[d + 1], y) if d < layers - 1 else side_b * v)
            p = phase[at, pl.ds(y, CHUNK), :].astype(f32)
            moved = read(state[d], y, 1) - read(state[d], y, -1)
            stepped = (
                v
                + mobility_step * curvature_of(p) * read(first[d], y)
                - stiffness_step * second
                + transport * moved
            )
            emit(d, y, v, stepped)


def padded(rows, depth, layers=None):
    lead = () if layers is None else (layers,)
    return pltpu.VMEM((*lead, rows + 2 * PAD, depth), f32)


def layers_of(ref):
    return [(ref, (d,)) for d in range(ref.shape[0])]


def first_message(adjoint, targets, owners, cells, rates, out, held, near, far, missing, digits, owner, cell, sems):
    layers, rows, depth = adjoint.shape
    n = targets.shape[0]
    pairs = [(adjoint.at[stored(d, layers)], ref.at[pl.ds(PAD, rows)]) for d, ref in ((0, near), (1, far))]
    pairs += [(targets, out.at[pl.ds(2 * rows, n)]), (owners, owner), (cells, cell), (rates, held)]
    copies = copy_all(pairs, sems)
    digits[...] = jnp.zeros(digits.shape, f32)
    for c in copies[3:]:
        c.wait()
    digits[0:1, 0:n] = owner[...].astype(f32)
    digits[1:2, 0:n] = (cell[...] >> 8).astype(f32)
    digits[2:3, 0:n] = (cell[...] & 255).astype(f32)
    out[pl.ds(2 * rows + n, 16), :] = digits[...].astype(bf16)
    for c in copies[:3]:
        c.wait()
    write_message((near, ()), (far, ()), (missing, ()), out, rows)


def make_first_message(adjoint, targets, owners, cells, rates):
    layers, rows, depth = adjoint.shape
    extra = targets.shape[0] + 16
    row = pltpu.VMEM(owners.shape, jnp.int32)
    return call(
        first_message,
        (jax.ShapeDtypeStruct((2 * rows + extra, depth), bf16), jax.ShapeDtypeStruct(rates.shape, f32)),
        (VMEM, VMEM),
        [ANY] * 5,
        [padded(rows, depth)] * 3 + [pltpu.VMEM((16, depth), f32), row, row, pltpu.SemaphoreType.DMA((6,))],
        cost(LONG),
    )(*[pltpu.with_memory_space_constraint(v, pltpu.HBM) for v in (adjoint, targets, owners, cells, rates)])


def transport_row(inflow, depth):
    lane = lax.broadcasted_iota(jnp.int32, (8, depth), 1)
    height = (lane.astype(f32) + 0.5) / depth
    return (transport_step * inflow) * (4.0 * height * (1.0 - height))


def first_local(
    count, adjoint, phase, rates, choice, mask, after, out, message, row, masked, near_walls, state, first, missing, sems
):
    layers, rows, depth = adjoint.shape
    copies = copy_all(
        [(adjoint.at[stored(d, layers)], state.at[d, pl.ds(PAD, rows)]) for d in range(layers)], sems
    )
    row[...] = transport_row(rates[0, choice[0]], depth)
    masked[...] = wall_weight * mask[...].astype(f32)
    for d in range(layers):
        clear_margins((state, (d,)))
        clear_margins((first, (d,)))
    for c in copies:
        c.wait()
    own = layers_of(state)
    write_message(own[-1], own[-2], (missing, ()), message, rows)

    def emit(d, y, v, stepped):
        out[d, pl.ds(y, CHUNK), :] = stepped

    local_step(own, layers_of(first), phase, row, count, emit)
    four = (0, 1, depth - 1, depth - 2)
    two = (0, depth - 1)
    at = stored(layers - 1, layers)
    for y in range(0, rows, 128):
        span = pl.ds(y, 128)
        high, low = split(out[layers - 1, span, :], 2)
        high2, low2 = split(out[layers - 2, span, :], 2)
        picked = pick_rows(high, four, 0, 16) + pick_rows(low, four, 4, 16) + pick_rows(phase[at, span, :], four, 12, 16)
        picked = picked + pick_rows(high2, two, 8, 16) + pick_rows(low2, two, 10, 16)
        message[pl.ds(2 * rows + y // 8, 16), :] = picked.astype(bf16)
        steps = range(y, y + 128, CHUNK)
        near = jnp.concatenate([read(own[-1], k) for k in steps])
        both = jnp.concatenate([read(own[-2], k) + 2.0 * plane_part(own[-1], k) for k in steps])
        near_walls[:, span] = pick_exact(near, four, 0) + pick_exact(both, four, 4)


def make_first_local(adjoint, phase, rates, choice, mask, after, count):
    layers, rows, depth = adjoint.shape
    return call(
        lambda *refs: first_local(count, *refs),
        (
            jax.ShapeDtypeStruct(adjoint.shape, f32),
            jax.ShapeDtypeStruct((2 * rows + rows // 8, depth), bf16),
            jax.ShapeDtypeStruct((8, depth), f32),
            jax.ShapeDtypeStruct(mask.shape, f32),
            jax.ShapeDtypeStruct((8, rows), f32),
        ),
        (VMEM,) * 5,
        [ANY, VMEM, SMEM, SMEM, VMEM, ANY],
        [padded(rows, depth, layers)] * 2 + [padded(rows, depth), pltpu.SemaphoreType.DMA((layers,))],
        cost(LONG),
    )(adjoint, phase, rates, choice, mask, after)


def add_halo(message, edge, inner, halo, phase, at, rows, put_edge, put_inner):
    clear_margins(halo)
    for y in starts(rows):
        near = message[pl.ds(y, CHUNK), :].astype(f32)
        write(halo, y, near)
        put_inner(y, inner(y) - stiffness_step * near)
    for y in starts(rows):
        near = read(halo, y)
        far = message[pl.ds(rows + y, CHUNK), :].astype(f32)
        curvature = curvature_of(phase[at, pl.ds(y, CHUNK), :].astype(f32))
        both = far + 2.0 * plane_part(halo, y)
        put_edge(y, edge(y) + mobility_step * curvature * near - stiffness_step * both)


def pick_rows(v, heights, first_row, rows=8):
    depth = v.shape[1]
    row = lax.broadcasted_iota(jnp.int32, (rows, depth), 0) - first_row
    lane = lax.broadcasted_iota(jnp.int32, (rows, depth), 1)
    pick = jnp.zeros((rows, depth), f32)
    for i, z in enumerate(heights):
        pick = pick + jnp.where((row == i) & (lane == z), 1.0, 0.0)
    return lax.dot_general(pick.astype(bf16), v, (((1,), (1,)), ((), ())), preferred_element_type=f32)


def split(v, parts):
    out = []
    for _ in range(parts):
        high = v.astype(bf16)
        out.append(high)
        v = v - high.astype(f32)
    return out


def pick_exact(v, heights, first_row):
    return sum(pick_rows(part, heights, first_row) for part in split(v, 3))


def wall_rows(v, first_row):
    heights = (0, v.shape[1] - 1)
    return pick_rows(v, heights, first_row) if v.dtype == bf16 else pick_exact(v, heights, first_row)


def join_halo(side, message, pre, phase, out, halo):
    layers, rows, depth = pre.shape
    one, two = (0, 1) if side == 0 else (layers - 1, layers - 2)
    edge, inner = layers_of(out)
    clear_margins(edge)
    clear_margins(inner)
    add_halo(
        message,
        lambda y: pre[one, pl.ds(y, CHUNK), :],
        lambda y: pre[two, pl.ds(y, CHUNK), :],
        (halo, ()),
        phase,
        stored(one, layers),
        rows,
        lambda y, v: write(edge, y, v),
        lambda y, v: write(inner, y, v),
    )


def wall_parts(half, y):
    edge, inner = layers_of(half)
    parts = 0.0
    for i in range(2):
        span = range(y + 128 * i, y + 128 * (i + 1), CHUNK)
        both = jnp.concatenate([read(inner, k) + 2.0 * plane_part(edge, k) for k in span])
        near = jnp.concatenate([read(edge, k) for k in span])
        parts = parts + wall_rows(near, 4 * i) + wall_rows(both, 4 * i + 2)
    return parts


def put_walls(half, out, start):
    rows = half.shape[1] - 2 * PAD
    for y in range(0, rows, 256):
        parts = wall_parts(half, y)
        high = parts.astype(bf16).astype(f32)
        out[pl.ds(start + y // 16, 16), :] = jnp.concatenate([high, parts - high]).astype(bf16)


def middle_a(message, pre, phase, first, out, sent, early, block, halo, missing):
    rows, n = pre.shape[1], block.shape[0] // 2
    join_halo(0, message, pre, phase, out, halo)
    write_message(*layers_of(out), (missing, ()), sent, rows)
    put_walls(out, early, 0)
    block[pl.ds(0, n), :] = first[pl.ds(2 * rows, n), :]
    block[pl.ds(n, n), :] = message[pl.ds(2 * rows, n), :]


def make_middle_a(message, pre, phase, first):
    layers, rows, depth = pre.shape
    extra = first.shape[0] - 2 * rows
    return call(
        middle_a,
        (
            jax.ShapeDtypeStruct((2, rows + 2 * PAD, depth), f32),
            jax.ShapeDtypeStruct((2 * rows, depth), bf16),
            jax.ShapeDtypeStruct((rows // 16, depth), bf16),
            jax.ShapeDtypeStruct((2 * extra, depth), bf16),
        ),
        (VMEM,) * 4,
        [VMEM] * 4,
        [padded(rows, depth)] * 2,
        cost(LONG),
    )(message, pre, phase, first)


def partner_walls(message, near_walls, rows, present):
    sent = [message[pl.ds(2 * rows + y // 8, 16), :].astype(f32) for y in range(0, rows, 128)]
    sent = jnp.concatenate(sent, axis=1)
    here = near_walls[0:4, :]
    near = sent[0:4] + sent[4:8] + mobility_step * curvature_of(sent[12:16]) * here
    near = near - stiffness_step * near_walls[4:8, :]
    far = sent[8:10] + sent[10:12]
    lane = lax.broadcasted_iota(jnp.int32, (1, rows), 1)
    out = []
    for wall in range(2):
        v = near[2 * wall : 2 * wall + 1]
        along = jnp.where(lane == 0, 0.0, pltpu.roll(v, 1, 1)) + jnp.where(lane == rows - 1, 0.0, pltpu.roll(v, rows - 1, 1))
        plane = along + near[2 * wall + 1 : 2 * wall + 2] - 6.0 * v
        both = far[wall : wall + 1] - stiffness_step * here[2 * wall : 2 * wall + 1] + 2.0 * plane
        out.append((present * v, present * both))
    return [out[0][0], out[1][0], out[0][1], out[1][1]]


def middle_b(count, message, pre, phase, near_walls, after, out, sent, walls, halo, missing):
    rows = pre.shape[1]
    join_halo(1, message, pre, phase, out, halo)
    write_message(*layers_of(out), (missing, ()), sent, rows)
    walls[...] = jnp.zeros(walls.shape, f32)
    for i, v in enumerate(partner_walls(message, near_walls, rows, has_partner(count)[1])):
        walls[i : i + 1, :] = v


def make_middle_b(message, pre, phase, near_walls, after, count):
    layers, rows, depth = pre.shape
    return call(
        lambda *refs: middle_b(count, *refs),
        (
            jax.ShapeDtypeStruct((2, rows + 2 * PAD, depth), f32),
            jax.ShapeDtypeStruct((2 * rows, depth), bf16),
            jax.ShapeDtypeStruct((8, rows), f32),
        ),
        (VMEM,) * 3,
        [VMEM] * 4 + [ANY],
        [padded(rows, depth)] * 2,
        cost(6 * 10**8),
    )(message, pre, phase, near_walls, after)


def join(one, two, after, out):
    n = one.shape[0]
    out[pl.ds(0, n), :] = one[...]
    out[pl.ds(n, n), :] = two[...]


def make_join(one, two, after, flops):
    return call(
        join,
        jax.ShapeDtypeStruct((2 * one.shape[0], one.shape[1]), bf16),
        VMEM,
        [VMEM, VMEM, ANY],
        [],
        cost(flops),
    )(one, two, after)


def second_local(count, side_a, side_b, phase, row, out, wall, phase_wall, first):
    layers, rows, depth = out.shape
    own = layers_of(side_a) + layers_of(side_b)[::-1]
    for d in range(layers):
        clear_margins((first, (d,)))
    held = []

    def emit(d, y, v, stepped):
        out[d, pl.ds(y, CHUNK), :] = stepped
        held.append(v + stepped)
        if len(held) * CHUNK == 128:
            start = y + CHUNK - 128
            wall[d, :, pl.ds(start, 128)] = wall_rows(jnp.concatenate(held), 0)
            phase_wall[d, :, pl.ds(start, 128)] = wall_rows(phase[stored(d, layers), pl.ds(start, 128), :], 0)
            held.clear()

    local_step(own, layers_of(first), phase, row, count, emit)


def make_second_local(side_a, side_b, phase, row, count):
    layers, rows, depth = phase.shape
    return call(
        lambda *refs: second_local(count, *refs),
        (
            jax.ShapeDtypeStruct((layers, rows, depth), f32),
            jax.ShapeDtypeStruct((layers, 8, rows), f32),
            jax.ShapeDtypeStruct((layers, 8, rows), f32),
        ),
        (VMEM,) * 3,
        [VMEM] * 4,
        [padded(rows, depth, layers)],
        cost(13 * 10**8),
    )(side_a, side_b, phase, row)


def injection(n, phase, pre, *refs):
    sources, (out, index, rhs) = refs[:-3], refs[-3:]
    layers, rows, depth = out.shape
    position = lax.axis_index("slab").astype(f32)
    rhs[:, :depth] = jnp.ones((rhs.shape[0], depth), bf16)
    at = 0
    for source in sources:
        for first in range(0, source.shape[0], n + 16):
            rhs[pl.ds(at, n), depth:] = source[pl.ds(first, n), :]
            digits = source[pl.ds(first + n, 16), :].astype(f32)
            cell = jnp.where(digits[0:1] == position, digits[1:2] * 256.0 + digits[2:3], -1.0)
            index[0:1, pl.ds(at, n)] = cell[:, :n].astype(jnp.int32)
            at += n
    for d in range(layers):
        at = stored(d, layers)
        for y in range(0, rows, 128):
            cell = lax.broadcasted_iota(jnp.int32, (128, index.shape[1]), 0) + (at * rows + y)
            here = jnp.where(cell == index[0:1, :], 1.0, 0.0).astype(bf16)
            added = jnp.dot(here, rhs[...], preferred_element_type=f32)
            p = phase[at, pl.ds(y, 128), :].astype(f32)
            out[d, pl.ds(y, 128), :] = pre[d, pl.ds(y, 128), :] + (added[:, :depth] * p - added[:, depth:])


def make_injection(phase, n, pre, sources):
    layers, rows, depth = phase.shape
    total = sum(r.shape[0] // (n + 16) * n for r in sources)
    return call(
        lambda *refs: injection(n, *refs),
        jax.ShapeDtypeStruct((layers, rows, depth), f32),
        VMEM,
        [VMEM, VMEM] + [VMEM] * len(sources),
        [pltpu.VMEM((8, total), jnp.int32), pltpu.VMEM((total, 2 * depth), bf16)],
        cost(1),
    )(phase, pre, *sources)


def unpack_walls(message, out):
    for y in range(0, out.shape[1], 256):
        both = message[pl.ds(y // 16, 16), :].astype(f32)
        both = both[:8] + both[8:]
        for i in range(2):
            out[:4, pl.ds(y + 128 * i, 128)] = both[4 * i : 4 * i + 4]


def wall_kernel(wall, phase_wall, early_a, from_b, mask, after, out, from_a):
    layers = wall.shape[0]
    unpack_walls(early_a, from_a)
    odd = is_odd()
    terms = []
    for d in range(layers):
        p = phase_wall[d, :2, :]
        w = wall[d, :2, :]
        for halo, off in ((from_a, d), (from_b, layers - 1 - d)):
            if off == 0:
                w = w + mobility_step * curvature_of(p) * halo[:2] - stiffness_step * halo[2:4]
            elif off == 1:
                w = w - stiffness_step * halo[:2]
        terms.append((1.0 - p * p) * w)
    for l in range(layers):
        out[:, l, :] = mask[:, l, :] * jnp.where(odd, terms[l], terms[layers - 1 - l])


def make_walls(wall, phase_wall, early_a, from_b, mask, after):
    return call(
        wall_kernel,
        jax.ShapeDtypeStruct(mask.shape, f32),
        VMEM,
        [VMEM] * 5 + [ANY],
        [pltpu.VMEM(wall.shape[1:], f32)],
        cost(3 * 10**8),
    )(wall, phase_wall, early_a, from_b, mask, after)


def layers_at_a(message, phase, state, out, halo):
    layers = state.shape[0]

    def put(d):
        def store(y, v):
            out[d, pl.ds(y, CHUNK), :] = v

        return store

    def get(d):
        return lambda y: state[d, pl.ds(y, CHUNK), :]

    add_halo(message, get(0), get(1), (halo, ()), phase, stored(0, layers), phase.shape[1], put(0), put(1))


def make_layers_at_a(message, phase, state):
    layers, rows, depth = phase.shape
    return call(
        layers_at_a,
        jax.ShapeDtypeStruct((2, rows, depth), f32),
        VMEM,
        [VMEM] * 3,
        [padded(rows, depth)],
        cost(15 * 10**8),
    )(message, phase, state)


def final(at_a, message_b, state, phase, *refs):
    walls, (out, total, planes, summed, halo, sems) = refs[:-6], refs[-6:]
    layers, rows, depth = state.shape
    half = rows // 2
    copies = []

    def send(source, target):
        c = pltpu.make_async_copy(source, target, sems.at[len(copies)])
        c.start()
        copies.append(c)

    for d in range(2):
        send(at_a.at[d], out.at[stored(d, layers)])
    if len(walls) == 4:
        summed[...] = (walls[0][...] + walls[3][...]) + (walls[1][...] + walls[2][...])
    else:
        summed[...] = walls[0][...]
    send(summed, total)

    def put(i):
        def store(y, v):
            planes[i, pl.ds(y, CHUNK), :] = v
            if (y + CHUNK) % half == 0:
                span = pl.ds(y + CHUNK - half, half)
                send(planes.at[i, span], out.at[stored(layers - 1 - i, layers), span])

        return store

    def get(d):
        return lambda y: state[d, pl.ds(y, CHUNK), :]

    one, two = layers - 1, layers - 2
    add_halo(message_b, get(one), get(two), (halo, ()), phase, stored(one, layers), rows, put(0), put(1))
    for c in copies:
        c.wait()


def make_final(at_a, message_b, state, phase, walls):
    layers, rows, depth = state.shape
    return call(
        final,
        (jax.ShapeDtypeStruct(state.shape, f32), jax.ShapeDtypeStruct(walls[0].shape, f32)),
        (ANY, ANY),
        [VMEM] * (4 + len(walls)),
        [
            pltpu.VMEM((2, rows, depth), f32),
            pltpu.VMEM(walls[0].shape, f32),
            padded(rows, depth),
            pltpu.SemaphoreType.DMA((7,)),
        ],
        cost(1),
    )(at_a, message_b, state, phase, *walls)


def on_device(adjoint, phase, targets, owners, target_cell, rate_index, inflow_rates, wall_mask):
    state, phase, targets = adjoint[0], phase[0], targets[0]
    owners = owners.reshape(target_cell.shape)
    count = lax.axis_size("slab")
    pairs = (
        [(i, i ^ 1) for i in range(count) if i ^ 1 < count],
        [(i, i + 1) for i in range(1, count - 1, 2)] + [(i + 1, i) for i in range(1, count - 1, 2)],
    )

    def send(v, side):
        return lax.ppermute(v, "slab", pairs[side])

    rows, n = state.shape[1], targets.shape[0]
    few = count == 8
    first, rates = make_first_message(state, targets, owners, target_cell, inflow_rates[None])
    from_a = send(first, 0)
    pre, message, row, mask, near_walls = make_first_local(state, phase, rates, rate_index, wall_mask, first, count)
    from_b = send(message, 1)
    half_a, message, early, pair = make_middle_a(from_a, pre, phase, first)
    early = send(early, 0)
    later_a = send(message, 0)
    four = far = pair
    if few:
        four = make_join(pair, lax.ppermute(pair, "slab", [(i, i ^ 4) for i in range(count)]), pair, 15 * 10**8)
        far = lax.ppermute(four, "slab", [(i, i ^ 2) for i in range(count)])
    half_b, message, walls_b = make_middle_b(from_b, pre, phase, near_walls, four, count)
    later_b = send(message, 1)
    pre, wall, phase_wall = make_second_local(half_a, half_b, phase, row, count)
    block = make_join(four, far, wall, 1)
    if not few:
        block = lax.all_gather(first[2 * state.shape[1] :], "slab", axis=0, tiled=True)
    part = make_walls(wall, phase_wall, early, walls_b, mask, block)
    if lax.axis_size("cond") == 4:
        walls = [part] + [lax.ppermute(part, "cond", [(i, i ^ k) for i in range(4)]) for k in (3, 2, 1)]
    else:
        walls = [lax.psum(part, "cond")]
    state = make_injection(phase, n, pre, [block])
    at_a = make_layers_at_a(later_a, phase, state)
    out, wall_gradient = make_final(at_a, later_b, state, phase, walls)
    return out[None], wall_gradient


def solution(mesh):
    in_specs = (
        P("cond", "slab", None, None),
        P("cond", "slab", None, None),
        P("cond", "slab", None),
        P("cond", "slab", None),
        P("cond", "slab"),
        P("cond"),
        P(),
        P(None, "slab", None),
    )
    out_specs = (P("cond", "slab", None, None), P(None, "slab", None))
    return jax.shard_map(
        on_device, mesh=mesh, in_specs=in_specs, out_specs=out_specs, check_vma=False
    )
```

```python
import jax
import jax.numpy as jnp
from jax import lax
from jax.experimental import pallas as pl
from jax.experimental.pallas import tpu as pltpu
from jax.sharding import PartitionSpec as P

mobility_step = 0.02
stiffness_step = 0.01
transport_step = 0.125
wall_weight = 0.25

f32 = jnp.float32
bf16 = jnp.bfloat16
CHUNK = 64
LONG = 10**10
PAD = 8
ANY = pl.BlockSpec(memory_space=pl.ANY)
HBM = pl.BlockSpec(memory_space=pltpu.HBM)
VMEM = pl.BlockSpec(memory_space=pltpu.VMEM)
SMEM = pl.BlockSpec(memory_space=pltpu.SMEM)


def cost(flops):
    return pl.CostEstimate(flops=flops, bytes_accessed=1, transcendentals=0)


def call(kernel, outs, out_specs, in_specs, scratch, estimate, aliases=None, limit=12):
    return pl.pallas_call(
        kernel,
        out_shape=outs,
        out_specs=out_specs,
        in_specs=in_specs,
        scratch_shapes=scratch,
        input_output_aliases=aliases or {},
        cost_estimate=estimate,
        compiler_params=pltpu.CompilerParams(vmem_limit_bytes=limit * 1024 * 1024),
    )


def starts(rows):
    return range(0, rows, CHUNK)


def read(layer, y, shift=0):
    ref, lead = layer
    return ref[(*lead, pl.ds(PAD + y + shift, CHUNK), slice(None))]


def write(layer, y, v):
    ref, lead = layer
    ref[(*lead, pl.ds(PAD + y, CHUNK), slice(None))] = v


def z_sum(v):
    depth = v.shape[1]
    lane = lax.broadcasted_iota(jnp.int32, v.shape, 1)
    below = jnp.where(lane == 0, 0.0, pltpu.roll(v, 1, 1))
    above = jnp.where(lane == depth - 1, 0.0, pltpu.roll(v, depth - 1, 1))
    return below + above


def plane_part(layer, y):
    v = read(layer, y)
    return read(layer, y, 1) + read(layer, y, -1) + z_sum(v) - 6.0 * v


def clear_margins(layer):
    ref, lead = layer
    zero = jnp.zeros((PAD, ref.shape[-1]), f32)
    ref[(*lead, pl.ds(0, PAD), slice(None))] = zero
    ref[(*lead, pl.ds(ref.shape[-2] - PAD, PAD), slice(None))] = zero


def is_odd():
    return lax.rem(lax.axis_index("slab"), 2) == 1


def stored(d, layers):
    return jnp.where(is_odd(), d, layers - 1 - d)


def has_partner(count):
    position = lax.axis_index("slab")
    above = position < count - 1
    below = position > 0
    odd = is_odd()
    flags = jnp.where(odd, below, above), jnp.where(odd, above, below)
    return [jnp.where(f, 1.0, 0.0).astype(f32) for f in flags]


def copy_all(pairs, sems):
    copies = [pltpu.make_async_copy(s, d, sems.at[i]) for i, (s, d) in enumerate(pairs)]
    for c in copies:
        c.start()
    return copies


def write_message(near, far, missing, out, rows):
    clear_margins(missing)
    for y in starts(rows):
        v = read(near, y)
        rounded = v.astype(bf16)
        out[pl.ds(y, CHUNK), :] = rounded
        write(missing, y, v - rounded.astype(f32))
    for y in starts(rows):
        out[pl.ds(rows + y, CHUNK), :] = (read(far, y) + 2.0 * plane_part(missing, y)).astype(bf16)


def curvature_of(p):
    return 3.0 * p * p - 1.0


def local_step(state, first, phase, row, count, emit):
    layers = len(state)
    rows = phase.shape[1]
    depth = phase.shape[2]
    side_a, side_b = has_partner(count)
    transport = row[0:1, :]
    for d in range(layers):
        for y in starts(rows):
            lap = plane_part(state[d], y)
            if d > 0:
                lap = lap + read(state[d - 1], y)
            if d < layers - 1:
                lap = lap + read(state[d + 1], y)
            write(first[d], y, lap)
    for d in range(layers):
        at = stored(d, layers)
        for y in starts(rows):
            v = read(state[d], y)
            second = plane_part(first[d], y)
            second = second + (read(first[d - 1], y) if d > 0 else side_a * v)
            second = second + (read(first[d + 1], y) if d < layers - 1 else side_b * v)
            p = phase[at, pl.ds(y, CHUNK), :].astype(f32)
            moved = read(state[d], y, 1) - read(state[d], y, -1)
            stepped = (
                v
                + mobility_step * curvature_of(p) * read(first[d], y)
                - stiffness_step * second
                + transport * moved
            )
            emit(d, y, v, stepped)


def padded(rows, depth, layers=None):
    lead = () if layers is None else (layers,)
    return pltpu.VMEM((*lead, rows + 2 * PAD, depth), f32)


def layers_of(ref):
    return [(ref, (d,)) for d in range(ref.shape[0])]


def first_message(adjoint, targets, owners, cells, rates, out, held, near, far, missing, digits, owner, cell, sems):
    layers, rows, depth = adjoint.shape
    n = targets.shape[0]
    pairs = [(adjoint.at[stored(d, layers)], ref.at[pl.ds(PAD, rows)]) for d, ref in ((0, near), (1, far))]
    pairs += [(targets, out.at[pl.ds(2 * rows, n)]), (owners, owner), (cells, cell), (rates, held)]
    copies = copy_all(pairs, sems)
    digits[...] = jnp.zeros(digits.shape, f32)
    for c in copies[3:]:
        c.wait()
    digits[0:1, 0:n] = owner[...].astype(f32)
    digits[1:2, 0:n] = (cell[...] >> 8).astype(f32)
    digits[2:3, 0:n] = (cell[...] & 255).astype(f32)
    out[pl.ds(2 * rows + n, 16), :] = digits[...].astype(bf16)
    for c in copies[:3]:
        c.wait()
    write_message((near, ()), (far, ()), (missing, ()), out, rows)


def make_first_message(adjoint, targets, owners, cells, rates):
    layers, rows, depth = adjoint.shape
    extra = targets.shape[0] + 16
    row = pltpu.VMEM(owners.shape, jnp.int32)
    return call(
        first_message,
        (jax.ShapeDtypeStruct((2 * rows + extra, depth), bf16), jax.ShapeDtypeStruct(rates.shape, f32)),
        (VMEM, VMEM),
        [ANY] * 5,
        [padded(rows, depth)] * 3 + [pltpu.VMEM((16, depth), f32), row, row, pltpu.SemaphoreType.DMA((6,))],
        cost(LONG),
    )(*[pltpu.with_memory_space_constraint(v, pltpu.HBM) for v in (adjoint, targets, owners, cells, rates)])


def transport_row(inflow, depth):
    lane = lax.broadcasted_iota(jnp.int32, (8, depth), 1)
    height = (lane.astype(f32) + 0.5) / depth
    return (transport_step * inflow) * (4.0 * height * (1.0 - height))


def first_local(
    count, adjoint, phase, rates, choice, mask, after, out, message, row, masked, near_walls, state, first, missing, sems
):
    layers, rows, depth = adjoint.shape
    copies = copy_all(
        [(adjoint.at[stored(d, layers)], state.at[d, pl.ds(PAD, rows)]) for d in range(layers)], sems
    )
    row[...] = transport_row(rates[0, choice[0]], depth)
    masked[...] = wall_weight * mask[...].astype(f32)
    for d in range(layers):
        clear_margins((state, (d,)))
        clear_margins((first, (d,)))
    for c in copies:
        c.wait()
    own = layers_of(state)
    write_message(own[-1], own[-2], (missing, ()), message, rows)

    def emit(d, y, v, stepped):
        out[d, pl.ds(y, CHUNK), :] = stepped

    local_step(own, layers_of(first), phase, row, count, emit)
    four = (0, 1, depth - 1, depth - 2)
    two = (0, depth - 1)
    at = stored(layers - 1, layers)
    for y in range(0, rows, 128):
        span = pl.ds(y, 128)
        high, low = split(out[layers - 1, span, :], 2)
        high2, low2 = split(out[layers - 2, span, :], 2)
        picked = pick_rows(high, four, 0, 16) + pick_rows(low, four, 4, 16) + pick_rows(phase[at, span, :], four, 12, 16)
        picked = picked + pick_rows(high2, two, 8, 16) + pick_rows(low2, two, 10, 16)
        message[pl.ds(2 * rows + y // 8, 16), :] = picked.astype(bf16)
        steps = range(y, y + 128, CHUNK)
        near = jnp.concatenate([read(own[-1], k) for k in steps])
        both = jnp.concatenate([read(own[-2], k) + 2.0 * plane_part(own[-1], k) for k in steps])
        near_walls[:, span] = pick_exact(near, four, 0) + pick_exact(both, four, 4)


def make_first_local(adjoint, phase, rates, choice, mask, after, count):
    layers, rows, depth = adjoint.shape
    return call(
        lambda *refs: first_local(count, *refs),
        (
            jax.ShapeDtypeStruct(adjoint.shape, f32),
            jax.ShapeDtypeStruct((2 * rows + rows // 8, depth), bf16),
            jax.ShapeDtypeStruct((8, depth), f32),
            jax.ShapeDtypeStruct(mask.shape, f32),
            jax.ShapeDtypeStruct((8, rows), f32),
        ),
        (VMEM,) * 5,
        [ANY, VMEM, SMEM, SMEM, VMEM, ANY],
        [padded(rows, depth, layers)] * 2 + [padded(rows, depth), pltpu.SemaphoreType.DMA((layers,))],
        cost(LONG),
    )(adjoint, phase, rates, choice, mask, after)


def add_halo(message, edge, inner, halo, phase, at, rows, put_edge, put_inner):
    clear_margins(halo)
    for y in starts(rows):
        near = message[pl.ds(y, CHUNK), :].astype(f32)
        write(halo, y, near)
        put_inner(y, inner(y) - stiffness_step * near)
    for y in starts(rows):
        near = read(halo, y)
        far = message[pl.ds(rows + y, CHUNK), :].astype(f32)
        curvature = curvature_of(phase[at, pl.ds(y, CHUNK), :].astype(f32))
        both = far + 2.0 * plane_part(halo, y)
        put_edge(y, edge(y) + mobility_step * curvature * near - stiffness_step * both)


def pick_rows(v, heights, first_row, rows=8):
    depth = v.shape[1]
    row = lax.broadcasted_iota(jnp.int32, (rows, depth), 0) - first_row
    lane = lax.broadcasted_iota(jnp.int32, (rows, depth), 1)
    pick = jnp.zeros((rows, depth), f32)
    for i, z in enumerate(heights):
        pick = pick + jnp.where((row == i) & (lane == z), 1.0, 0.0)
    return lax.dot_general(pick.astype(bf16), v, (((1,), (1,)), ((), ())), preferred_element_type=f32)


def split(v, parts):
    out = []
    for _ in range(parts):
        high = v.astype(bf16)
        out.append(high)
        v = v - high.astype(f32)
    return out


def pick_exact(v, heights, first_row):
    return sum(pick_rows(part, heights, first_row) for part in split(v, 3))


def wall_rows(v, first_row):
    heights = (0, v.shape[1] - 1)
    return pick_rows(v, heights, first_row) if v.dtype == bf16 else pick_exact(v, heights, first_row)


def join_halo(side, message, pre, phase, out, halo):
    layers, rows, depth = pre.shape
    one, two = (0, 1) if side == 0 else (layers - 1, layers - 2)
    edge, inner = layers_of(out)
    clear_margins(edge)
    clear_margins(inner)
    add_halo(
        message,
        lambda y: pre[one, pl.ds(y, CHUNK), :],
        lambda y: pre[two, pl.ds(y, CHUNK), :],
        (halo, ()),
        phase,
        stored(one, layers),
        rows,
        lambda y, v: write(edge, y, v),
        lambda y, v: write(inner, y, v),
    )


def wall_parts(half, y):
    edge, inner = layers_of(half)
    parts = 0.0
    for i in range(2):
        span = range(y + 128 * i, y + 128 * (i + 1), CHUNK)
        both = jnp.concatenate([read(inner, k) + 2.0 * plane_part(edge, k) for k in span])
        near = jnp.concatenate([read(edge, k) for k in span])
        parts = parts + wall_rows(near, 4 * i) + wall_rows(both, 4 * i + 2)
    return parts


def put_walls(half, out, start):
    rows = half.shape[1] - 2 * PAD
    for y in range(0, rows, 256):
        parts = wall_parts(half, y)
        high = parts.astype(bf16).astype(f32)
        out[pl.ds(start + y // 16, 16), :] = jnp.concatenate([high, parts - high]).astype(bf16)


def middle_a(message, pre, phase, first, out, sent, early, block, halo, missing):
    rows, n = pre.shape[1], block.shape[0] // 2
    join_halo(0, message, pre, phase, out, halo)
    write_message(*layers_of(out), (missing, ()), sent, rows)
    put_walls(out, early, 0)
    block[pl.ds(0, n), :] = first[pl.ds(2 * rows, n), :]
    block[pl.ds(n, n), :] = message[pl.ds(2 * rows, n), :]


def make_middle_a(message, pre, phase, first):
    layers, rows, depth = pre.shape
    extra = first.shape[0] - 2 * rows
    return call(
        middle_a,
        (
            jax.ShapeDtypeStruct((2, rows + 2 * PAD, depth), f32),
            jax.ShapeDtypeStruct((2 * rows, depth), bf16),
            jax.ShapeDtypeStruct((rows // 16, depth), bf16),
            jax.ShapeDtypeStruct((2 * extra, depth), bf16),
        ),
        (VMEM,) * 4,
        [VMEM] * 4,
        [padded(rows, depth)] * 2,
        cost(LONG),
    )(message, pre, phase, first)


def partner_walls(message, near_walls, rows, present):
    sent = [message[pl.ds(2 * rows + y // 8, 16), :].astype(f32) for y in range(0, rows, 128)]
    sent = jnp.concatenate(sent, axis=1)
    here = near_walls[0:4, :]
    near = sent[0:4] + sent[4:8] + mobility_step * curvature_of(sent[12:16]) * here
    near = near - stiffness_step * near_walls[4:8, :]
    far = sent[8:10] + sent[10:12]
    lane = lax.broadcasted_iota(jnp.int32, (1, rows), 1)
    out = []
    for wall in range(2):
        v = near[2 * wall : 2 * wall + 1]
        along = jnp.where(lane == 0, 0.0, pltpu.roll(v, 1, 1)) + jnp.where(lane == rows - 1, 0.0, pltpu.roll(v, rows - 1, 1))
        plane = along + near[2 * wall + 1 : 2 * wall + 2] - 6.0 * v
        both = far[wall : wall + 1] - stiffness_step * here[2 * wall : 2 * wall + 1] + 2.0 * plane
        out.append((present * v, present * both))
    return [out[0][0], out[1][0], out[0][1], out[1][1]]


def middle_b(count, message, pre, phase, near_walls, after, out, sent, walls, halo, missing):
    rows = pre.shape[1]
    join_halo(1, message, pre, phase, out, halo)
    write_message(*layers_of(out), (missing, ()), sent, rows)
    walls[...] = jnp.zeros(walls.shape, f32)
    for i, v in enumerate(partner_walls(message, near_walls, rows, has_partner(count)[1])):
        walls[i : i + 1, :] = v


def make_middle_b(message, pre, phase, near_walls, after, count):
    layers, rows, depth = pre.shape
    return call(
        lambda *refs: middle_b(count, *refs),
        (
            jax.ShapeDtypeStruct((2, rows + 2 * PAD, depth), f32),
            jax.ShapeDtypeStruct((2 * rows, depth), bf16),
            jax.ShapeDtypeStruct((8, rows), f32),
        ),
        (VMEM,) * 3,
        [VMEM] * 4 + [ANY],
        [padded(rows, depth)] * 2,
        cost(6 * 10**8),
    )(message, pre, phase, near_walls, after)


def join(one, two, after, out):
    n = one.shape[0]
    out[pl.ds(0, n), :] = one[...]
    out[pl.ds(n, n), :] = two[...]


def make_join(one, two, after, flops):
    return call(
        join,
        jax.ShapeDtypeStruct((2 * one.shape[0], one.shape[1]), bf16),
        VMEM,
        [VMEM, VMEM, ANY],
        [],
        cost(flops),
    )(one, two, after)


def second_local(count, side_a, side_b, phase, row, out, wall, phase_wall, first):
    layers, rows, depth = out.shape
    own = layers_of(side_a) + layers_of(side_b)[::-1]
    for d in range(layers):
        clear_margins((first, (d,)))
    held = []

    def emit(d, y, v, stepped):
        out[d, pl.ds(y, CHUNK), :] = stepped
        held.append(v + stepped)
        if len(held) * CHUNK == 128:
            start = y + CHUNK - 128
            wall[d, :, pl.ds(start, 128)] = wall_rows(jnp.concatenate(held), 0)
            phase_wall[d, :, pl.ds(start, 128)] = wall_rows(phase[stored(d, layers), pl.ds(start, 128), :], 0)
            held.clear()

    local_step(own, layers_of(first), phase, row, count, emit)


def make_second_local(side_a, side_b, phase, row, count):
    layers, rows, depth = phase.shape
    return call(
        lambda *refs: second_local(count, *refs),
        (
            jax.ShapeDtypeStruct((layers, rows, depth), f32),
            jax.ShapeDtypeStruct((layers, 8, rows), f32),
            jax.ShapeDtypeStruct((layers, 8, rows), f32),
        ),
        (VMEM,) * 3,
        [VMEM] * 4,
        [padded(rows, depth, layers)],
        cost(13 * 10**8),
    )(side_a, side_b, phase, row)


def injection(n, phase, pre, *refs):
    sources, (out, index, rhs) = refs[:-3], refs[-3:]
    layers, rows, depth = out.shape
    position = lax.axis_index("slab").astype(f32)
    rhs[:, :depth] = jnp.ones((rhs.shape[0], depth), bf16)
    at = 0
    for source in sources:
        for first in range(0, source.shape[0], n + 16):
            rhs[pl.ds(at, n), depth:] = source[pl.ds(first, n), :]
            digits = source[pl.ds(first + n, 16), :].astype(f32)
            cell = jnp.where(digits[0:1] == position, digits[1:2] * 256.0 + digits[2:3], -1.0)
            index[0:1, pl.ds(at, n)] = cell[:, :n].astype(jnp.int32)
            at += n
    for d in range(layers):
        at = stored(d, layers)
        for y in range(0, rows, 128):
            cell = lax.broadcasted_iota(jnp.int32, (128, index.shape[1]), 0) + (at * rows + y)
            here = jnp.where(cell == index[0:1, :], 1.0, 0.0).astype(bf16)
            added = jnp.dot(here, rhs[...], preferred_element_type=f32)
            p = phase[at, pl.ds(y, 128), :].astype(f32)
            out[d, pl.ds(y, 128), :] = pre[d, pl.ds(y, 128), :] + (added[:, :depth] * p - added[:, depth:])


def make_injection(phase, n, pre, sources):
    layers, rows, depth = phase.shape
    total = sum(r.shape[0] // (n + 16) * n for r in sources)
    return call(
        lambda *refs: injection(n, *refs),
        jax.ShapeDtypeStruct((layers, rows, depth), f32),
        VMEM,
        [VMEM, VMEM] + [VMEM] * len(sources),
        [pltpu.VMEM((8, total), jnp.int32), pltpu.VMEM((total, 2 * depth), bf16)],
        cost(1),
    )(phase, pre, *sources)


def unpack_walls(message, out):
    for y in range(0, out.shape[1], 256):
        both = message[pl.ds(y // 16, 16), :].astype(f32)
        both = both[:8] + both[8:]
        for i in range(2):
            out[:4, pl.ds(y + 128 * i, 128)] = both[4 * i : 4 * i + 4]


def wall_kernel(wall, phase_wall, early_a, from_b, mask, after, out, from_a):
    layers = wall.shape[0]
    unpack_walls(early_a, from_a)
    odd = is_odd()
    terms = []
    for d in range(layers):
        p = phase_wall[d, :2, :]
        w = wall[d, :2, :]
        for halo, off in ((from_a, d), (from_b, layers - 1 - d)):
            if off == 0:
                w = w + mobility_step * curvature_of(p) * halo[:2] - stiffness_step * halo[2:4]
            elif off == 1:
                w = w - stiffness_step * halo[:2]
        terms.append((1.0 - p * p) * w)
    for l in range(layers):
        out[:, l, :] = mask[:, l, :] * jnp.where(odd, terms[l], terms[layers - 1 - l])


def make_walls(wall, phase_wall, early_a, from_b, mask, after):
    return call(
        wall_kernel,
        jax.ShapeDtypeStruct(mask.shape, f32),
        VMEM,
        [VMEM] * 5 + [ANY],
        [pltpu.VMEM(wall.shape[1:], f32)],
        cost(3 * 10**8),
    )(wall, phase_wall, early_a, from_b, mask, after)


def layers_at_a(message, phase, state, out, halo):
    layers = state.shape[0]

    def put(d):
        def store(y, v):
            out[d, pl.ds(y, CHUNK), :] = v

        return store

    def get(d):
        return lambda y: state[d, pl.ds(y, CHUNK), :]

    add_halo(message, get(0), get(1), (halo, ()), phase, stored(0, layers), phase.shape[1], put(0), put(1))


def make_layers_at_a(message, phase, state):
    layers, rows, depth = phase.shape
    return call(
        layers_at_a,
        jax.ShapeDtypeStruct((2, rows, depth), f32),
        VMEM,
        [VMEM] * 3,
        [padded(rows, depth)],
        cost(15 * 10**8),
    )(message, phase, state)


def final(at_a, message_b, state, phase, *refs):
    walls, (out, total, planes, summed, halo, sems) = refs[:-6], refs[-6:]
    layers, rows, depth = state.shape
    half = rows // 4
    copies = []

    def send(source, target):
        c = pltpu.make_async_copy(source, target, sems.at[len(copies)])
        c.start()
        copies.append(c)

    for d in range(2):
        send(at_a.at[d], out.at[stored(d, layers)])
    if len(walls) == 4:
        summed[...] = (walls[0][...] + walls[3][...]) + (walls[1][...] + walls[2][...])
    else:
        summed[...] = walls[0][...]
    send(summed, total)

    def put(i):
        def store(y, v):
            planes[i, pl.ds(y, CHUNK), :] = v
            if (y + CHUNK) % half == 0:
                span = pl.ds(y + CHUNK - half, half)
                send(planes.at[i, span], out.at[stored(layers - 1 - i, layers), span])

        return store

    def get(d):
        return lambda y: state[d, pl.ds(y, CHUNK), :]

    one, two = layers - 1, layers - 2
    add_halo(message_b, get(one), get(two), (halo, ()), phase, stored(one, layers), rows, put(0), put(1))
    for c in copies:
        c.wait()


def make_final(at_a, message_b, state, phase, walls):
    layers, rows, depth = state.shape
    return call(
        final,
        (jax.ShapeDtypeStruct(state.shape, f32), jax.ShapeDtypeStruct(walls[0].shape, f32)),
        (ANY, ANY),
        [VMEM] * (4 + len(walls)),
        [
            pltpu.VMEM((2, rows, depth), f32),
            pltpu.VMEM(walls[0].shape, f32),
            padded(rows, depth),
            pltpu.SemaphoreType.DMA((11,)),
        ],
        cost(1),
    )(at_a, message_b, state, phase, *walls)


def on_device(adjoint, phase, targets, owners, target_cell, rate_index, inflow_rates, wall_mask):
    state, phase, targets = adjoint[0], phase[0], targets[0]
    owners = owners.reshape(target_cell.shape)
    count = lax.axis_size("slab")
    pairs = (
        [(i, i ^ 1) for i in range(count) if i ^ 1 < count],
        [(i, i + 1) for i in range(1, count - 1, 2)] + [(i + 1, i) for i in range(1, count - 1, 2)],
    )

    def send(v, side):
        return lax.ppermute(v, "slab", pairs[side])

    rows, n = state.shape[1], targets.shape[0]
    few = count == 8
    first, rates = make_first_message(state, targets, owners, target_cell, inflow_rates[None])
    from_a = send(first, 0)
    pre, message, row, mask, near_walls = make_first_local(state, phase, rates, rate_index, wall_mask, first, count)
    from_b = send(message, 1)
    half_a, message, early, pair = make_middle_a(from_a, pre, phase, first)
    early = send(early, 0)
    later_a = send(message, 0)
    four = far = pair
    if few:
        four = make_join(pair, lax.ppermute(pair, "slab", [(i, i ^ 4) for i in range(count)]), pair, 15 * 10**8)
        far = lax.ppermute(four, "slab", [(i, i ^ 2) for i in range(count)])
    half_b, message, walls_b = make_middle_b(from_b, pre, phase, near_walls, four, count)
    later_b = send(message, 1)
    pre, wall, phase_wall = make_second_local(half_a, half_b, phase, row, count)
    block = make_join(four, far, wall, 1)
    if not few:
        block = lax.all_gather(first[2 * state.shape[1] :], "slab", axis=0, tiled=True)
    part = make_walls(wall, phase_wall, early, walls_b, mask, block)
    if lax.axis_size("cond") == 4:
        walls = [part] + [lax.ppermute(part, "cond", [(i, i ^ k) for i in range(4)]) for k in (3, 2, 1)]
    else:
        walls = [lax.psum(part, "cond")]
    state = make_injection(phase, n, pre, [block])
    at_a = make_layers_at_a(later_a, phase, state)
    out, wall_gradient = make_final(at_a, later_b, state, phase, walls)
    return out[None], wall_gradient


def solution(mesh):
    in_specs = (
        P("cond", "slab", None, None),
        P("cond", "slab", None, None),
        P("cond", "slab", None),
        P("cond", "slab", None),
        P("cond", "slab"),
        P("cond"),
        P(),
        P(None, "slab", None),
    )
    out_specs = (P("cond", "slab", None, None), P(None, "slab", None))
    return jax.shard_map(
        on_device, mesh=mesh, in_specs=in_specs, out_specs=out_specs, check_vma=False
    )
```

```python
import jax
import jax.numpy as jnp
from jax import lax
from jax.experimental import pallas as pl
from jax.experimental.pallas import tpu as pltpu
from jax.sharding import PartitionSpec as P

mobility_step = 0.02
stiffness_step = 0.01
transport_step = 0.125
wall_weight = 0.25

f32 = jnp.float32
bf16 = jnp.bfloat16
CHUNK = 128
LONG = 10**10
PAD = 8
ANY = pl.BlockSpec(memory_space=pl.ANY)
HBM = pl.BlockSpec(memory_space=pltpu.HBM)
VMEM = pl.BlockSpec(memory_space=pltpu.VMEM)
SMEM = pl.BlockSpec(memory_space=pltpu.SMEM)


def cost(flops):
    return pl.CostEstimate(flops=flops, bytes_accessed=1, transcendentals=0)


def call(kernel, outs, out_specs, in_specs, scratch, estimate, aliases=None, limit=12):
    return pl.pallas_call(
        kernel,
        out_shape=outs,
        out_specs=out_specs,
        in_specs=in_specs,
        scratch_shapes=scratch,
        input_output_aliases=aliases or {},
        cost_estimate=estimate,
        compiler_params=pltpu.CompilerParams(vmem_limit_bytes=limit * 1024 * 1024),
    )


def starts(rows):
    return range(0, rows, CHUNK)


def read(layer, y, shift=0):
    ref, lead = layer
    return ref[(*lead, pl.ds(PAD + y + shift, CHUNK), slice(None))]


def write(layer, y, v):
    ref, lead = layer
    ref[(*lead, pl.ds(PAD + y, CHUNK), slice(None))] = v


def z_sum(v):
    depth = v.shape[1]
    lane = lax.broadcasted_iota(jnp.int32, v.shape, 1)
    below = jnp.where(lane == 0, 0.0, pltpu.roll(v, 1, 1))
    above = jnp.where(lane == depth - 1, 0.0, pltpu.roll(v, depth - 1, 1))
    return below + above


def plane_part(layer, y):
    v = read(layer, y)
    return read(layer, y, 1) + read(layer, y, -1) + z_sum(v) - 6.0 * v


def clear_margins(layer):
    ref, lead = layer
    zero = jnp.zeros((PAD, ref.shape[-1]), f32)
    ref[(*lead, pl.ds(0, PAD), slice(None))] = zero
    ref[(*lead, pl.ds(ref.shape[-2] - PAD, PAD), slice(None))] = zero


def is_odd():
    return lax.rem(lax.axis_index("slab"), 2) == 1


def stored(d, layers):
    return jnp.where(is_odd(), d, layers - 1 - d)


def has_partner(count):
    position = lax.axis_index("slab")
    above = position < count - 1
    below = position > 0
    odd = is_odd()
    flags = jnp.where(odd, below, above), jnp.where(odd, above, below)
    return [jnp.where(f, 1.0, 0.0).astype(f32) for f in flags]


def copy_all(pairs, sems):
    copies = [pltpu.make_async_copy(s, d, sems.at[i]) for i, (s, d) in enumerate(pairs)]
    for c in copies:
        c.start()
    return copies


def write_message(near, far, missing, out, rows):
    clear_margins(missing)
    for y in starts(rows):
        v = read(near, y)
        rounded = v.astype(bf16)
        out[pl.ds(y, CHUNK), :] = rounded
        write(missing, y, v - rounded.astype(f32))
    for y in starts(rows):
        out[pl.ds(rows + y, CHUNK), :] = (read(far, y) + 2.0 * plane_part(missing, y)).astype(bf16)


def curvature_of(p):
    return 3.0 * p * p - 1.0


def local_step(state, first, phase, row, count, emit):
    layers = len(state)
    rows = phase.shape[1]
    depth = phase.shape[2]
    side_a, side_b = has_partner(count)
    transport = row[0:1, :]
    for d in range(layers):
        for y in starts(rows):
            lap = plane_part(state[d], y)
            if d > 0:
                lap = lap + read(state[d - 1], y)
            if d < layers - 1:
                lap = lap + read(state[d + 1], y)
            write(first[d], y, lap)
    for d in range(layers):
        at = stored(d, layers)
        for y in starts(rows):
            v = read(state[d], y)
            second = plane_part(first[d], y)
            second = second + (read(first[d - 1], y) if d > 0 else side_a * v)
            second = second + (read(first[d + 1], y) if d < layers - 1 else side_b * v)
            p = phase[at, pl.ds(y, CHUNK), :].astype(f32)
            moved = read(state[d], y, 1) - read(state[d], y, -1)
            stepped = (
                v
                + mobility_step * curvature_of(p) * read(first[d], y)
                - stiffness_step * second
                + transport * moved
            )
            emit(d, y, v, stepped)


def padded(rows, depth, layers=None):
    lead = () if layers is None else (layers,)
    return pltpu.VMEM((*lead, rows + 2 * PAD, depth), f32)


def layers_of(ref):
    return [(ref, (d,)) for d in range(ref.shape[0])]


def first_message(adjoint, targets, owners, cells, rates, out, held, near, far, missing, digits, owner, cell, sems):
    layers, rows, depth = adjoint.shape
    n = targets.shape[0]
    pairs = [(adjoint.at[stored(d, layers)], ref.at[pl.ds(PAD, rows)]) for d, ref in ((0, near), (1, far))]
    pairs += [(targets, out.at[pl.ds(2 * rows, n)]), (owners, owner), (cells, cell), (rates, held)]
    copies = copy_all(pairs, sems)
    digits[...] = jnp.zeros(digits.shape, f32)
    for c in copies[3:]:
        c.wait()
    digits[0:1, 0:n] = owner[...].astype(f32)
    digits[1:2, 0:n] = (cell[...] >> 8).astype(f32)
    digits[2:3, 0:n] = (cell[...] & 255).astype(f32)
    out[pl.ds(2 * rows + n, 16), :] = digits[...].astype(bf16)
    for c in copies[:3]:
        c.wait()
    write_message((near, ()), (far, ()), (missing, ()), out, rows)


def make_first_message(adjoint, targets, owners, cells, rates):
    layers, rows, depth = adjoint.shape
    extra = targets.shape[0] + 16
    row = pltpu.VMEM(owners.shape, jnp.int32)
    return call(
        first_message,
        (jax.ShapeDtypeStruct((2 * rows + extra, depth), bf16), jax.ShapeDtypeStruct(rates.shape, f32)),
        (VMEM, VMEM),
        [ANY] * 5,
        [padded(rows, depth)] * 3 + [pltpu.VMEM((16, depth), f32), row, row, pltpu.SemaphoreType.DMA((6,))],
        cost(LONG),
    )(*[pltpu.with_memory_space_constraint(v, pltpu.HBM) for v in (adjoint, targets, owners, cells, rates)])


def transport_row(inflow, depth):
    lane = lax.broadcasted_iota(jnp.int32, (8, depth), 1)
    height = (lane.astype(f32) + 0.5) / depth
    return (transport_step * inflow) * (4.0 * height * (1.0 - height))


def first_local(
    count, adjoint, phase, rates, choice, mask, after, out, message, row, masked, near_walls, state, first, missing, sems
):
    layers, rows, depth = adjoint.shape
    copies = copy_all(
        [(adjoint.at[stored(d, layers)], state.at[d, pl.ds(PAD, rows)]) for d in range(layers)], sems
    )
    row[...] = transport_row(rates[0, choice[0]], depth)
    masked[...] = wall_weight * mask[...].astype(f32)
    for d in range(layers):
        clear_margins((state, (d,)))
        clear_margins((first, (d,)))
    for c in copies:
        c.wait()
    own = layers_of(state)
    write_message(own[-1], own[-2], (missing, ()), message, rows)

    def emit(d, y, v, stepped):
        out[d, pl.ds(y, CHUNK), :] = stepped

    local_step(own, layers_of(first), phase, row, count, emit)
    four = (0, 1, depth - 1, depth - 2)
    two = (0, depth - 1)
    at = stored(layers - 1, layers)
    for y in range(0, rows, 128):
        span = pl.ds(y, 128)
        high, low = split(out[layers - 1, span, :], 2)
        high2, low2 = split(out[layers - 2, span, :], 2)
        picked = pick_rows(high, four, 0, 16) + pick_rows(low, four, 4, 16) + pick_rows(phase[at, span, :], four, 12, 16)
        picked = picked + pick_rows(high2, two, 8, 16) + pick_rows(low2, two, 10, 16)
        message[pl.ds(2 * rows + y // 8, 16), :] = picked.astype(bf16)
        steps = range(y, y + 128, CHUNK)
        near = jnp.concatenate([read(own[-1], k) for k in steps])
        both = jnp.concatenate([read(own[-2], k) + 2.0 * plane_part(own[-1], k) for k in steps])
        near_walls[:, span] = pick_exact(near, four, 0) + pick_exact(both, four, 4)


def make_first_local(adjoint, phase, rates, choice, mask, after, count):
    layers, rows, depth = adjoint.shape
    return call(
        lambda *refs: first_local(count, *refs),
        (
            jax.ShapeDtypeStruct(adjoint.shape, f32),
            jax.ShapeDtypeStruct((2 * rows + rows // 8, depth), bf16),
            jax.ShapeDtypeStruct((8, depth), f32),
            jax.ShapeDtypeStruct(mask.shape, f32),
            jax.ShapeDtypeStruct((8, rows), f32),
        ),
        (VMEM,) * 5,
        [ANY, VMEM, SMEM, SMEM, VMEM, ANY],
        [padded(rows, depth, layers)] * 2 + [padded(rows, depth), pltpu.SemaphoreType.DMA((layers,))],
        cost(LONG),
    )(adjoint, phase, rates, choice, mask, after)


def add_halo(message, edge, inner, halo, phase, at, rows, put_edge, put_inner):
    clear_margins(halo)
    for y in starts(rows):
        near = message[pl.ds(y, CHUNK), :].astype(f32)
        write(halo, y, near)
        put_inner(y, inner(y) - stiffness_step * near)
    for y in starts(rows):
        near = read(halo, y)
        far = message[pl.ds(rows + y, CHUNK), :].astype(f32)
        curvature = curvature_of(phase[at, pl.ds(y, CHUNK), :].astype(f32))
        both = far + 2.0 * plane_part(halo, y)
        put_edge(y, edge(y) + mobility_step * curvature * near - stiffness_step * both)


def pick_rows(v, heights, first_row, rows=8):
    depth = v.shape[1]
    row = lax.broadcasted_iota(jnp.int32, (rows, depth), 0) - first_row
    lane = lax.broadcasted_iota(jnp.int32, (rows, depth), 1)
    pick = jnp.zeros((rows, depth), f32)
    for i, z in enumerate(heights):
        pick = pick + jnp.where((row == i) & (lane == z), 1.0, 0.0)
    return lax.dot_general(pick.astype(bf16), v, (((1,), (1,)), ((), ())), preferred_element_type=f32)


def split(v, parts):
    out = []
    for _ in range(parts):
        high = v.astype(bf16)
        out.append(high)
        v = v - high.astype(f32)
    return out


def pick_exact(v, heights, first_row):
    return sum(pick_rows(part, heights, first_row) for part in split(v, 3))


def wall_rows(v, first_row):
    heights = (0, v.shape[1] - 1)
    return pick_rows(v, heights, first_row) if v.dtype == bf16 else pick_exact(v, heights, first_row)


def join_halo(side, message, pre, phase, out, halo):
    layers, rows, depth = pre.shape
    one, two = (0, 1) if side == 0 else (layers - 1, layers - 2)
    edge, inner = layers_of(out)
    clear_margins(edge)
    clear_margins(inner)
    add_halo(
        message,
        lambda y: pre[one, pl.ds(y, CHUNK), :],
        lambda y: pre[two, pl.ds(y, CHUNK), :],
        (halo, ()),
        phase,
        stored(one, layers),
        rows,
        lambda y, v: write(edge, y, v),
        lambda y, v: write(inner, y, v),
    )


def wall_parts(half, y):
    edge, inner = layers_of(half)
    parts = 0.0
    for i in range(2):
        span = range(y + 128 * i, y + 128 * (i + 1), CHUNK)
        both = jnp.concatenate([read(inner, k) + 2.0 * plane_part(edge, k) for k in span])
        near = jnp.concatenate([read(edge, k) for k in span])
        parts = parts + wall_rows(near, 4 * i) + wall_rows(both, 4 * i + 2)
    return parts


def put_walls(half, out, start):
    rows = half.shape[1] - 2 * PAD
    for y in range(0, rows, 256):
        parts = wall_parts(half, y)
        high = parts.astype(bf16).astype(f32)
        out[pl.ds(start + y // 16, 16), :] = jnp.concatenate([high, parts - high]).astype(bf16)


def middle_a(message, pre, phase, first, out, sent, early, block, halo, missing):
    rows, n = pre.shape[1], block.shape[0] // 2
    join_halo(0, message, pre, phase, out, halo)
    write_message(*layers_of(out), (missing, ()), sent, rows)
    put_walls(out, early, 0)
    block[pl.ds(0, n), :] = first[pl.ds(2 * rows, n), :]
    block[pl.ds(n, n), :] = message[pl.ds(2 * rows, n), :]


def make_middle_a(message, pre, phase, first):
    layers, rows, depth = pre.shape
    extra = first.shape[0] - 2 * rows
    return call(
        middle_a,
        (
            jax.ShapeDtypeStruct((2, rows + 2 * PAD, depth), f32),
            jax.ShapeDtypeStruct((2 * rows, depth), bf16),
            jax.ShapeDtypeStruct((rows // 16, depth), bf16),
            jax.ShapeDtypeStruct((2 * extra, depth), bf16),
        ),
        (VMEM,) * 4,
        [VMEM] * 4,
        [padded(rows, depth)] * 2,
        cost(LONG),
    )(message, pre, phase, first)


def partner_walls(message, near_walls, rows, present):
    sent = [message[pl.ds(2 * rows + y // 8, 16), :].astype(f32) for y in range(0, rows, 128)]
    sent = jnp.concatenate(sent, axis=1)
    here = near_walls[0:4, :]
    near = sent[0:4] + sent[4:8] + mobility_step * curvature_of(sent[12:16]) * here
    near = near - stiffness_step * near_walls[4:8, :]
    far = sent[8:10] + sent[10:12]
    lane = lax.broadcasted_iota(jnp.int32, (1, rows), 1)
    out = []
    for wall in range(2):
        v = near[2 * wall : 2 * wall + 1]
        along = jnp.where(lane == 0, 0.0, pltpu.roll(v, 1, 1)) + jnp.where(lane == rows - 1, 0.0, pltpu.roll(v, rows - 1, 1))
        plane = along + near[2 * wall + 1 : 2 * wall + 2] - 6.0 * v
        both = far[wall : wall + 1] - stiffness_step * here[2 * wall : 2 * wall + 1] + 2.0 * plane
        out.append((present * v, present * both))
    return [out[0][0], out[1][0], out[0][1], out[1][1]]


def middle_b(count, message, pre, phase, near_walls, after, out, sent, walls, halo, missing):
    rows = pre.shape[1]
    join_halo(1, message, pre, phase, out, halo)
    write_message(*layers_of(out), (missing, ()), sent, rows)
    walls[...] = jnp.zeros(walls.shape, f32)
    for i, v in enumerate(partner_walls(message, near_walls, rows, has_partner(count)[1])):
        walls[i : i + 1, :] = v


def make_middle_b(message, pre, phase, near_walls, after, count):
    layers, rows, depth = pre.shape
    return call(
        lambda *refs: middle_b(count, *refs),
        (
            jax.ShapeDtypeStruct((2, rows + 2 * PAD, depth), f32),
            jax.ShapeDtypeStruct((2 * rows, depth), bf16),
            jax.ShapeDtypeStruct((8, rows), f32),
        ),
        (VMEM,) * 3,
        [VMEM] * 4 + [ANY],
        [padded(rows, depth)] * 2,
        cost(6 * 10**8),
    )(message, pre, phase, near_walls, after)


def join(one, two, after, out):
    n = one.shape[0]
    out[pl.ds(0, n), :] = one[...]
    out[pl.ds(n, n), :] = two[...]


def make_join(one, two, after, flops):
    return call(
        join,
        jax.ShapeDtypeStruct((2 * one.shape[0], one.shape[1]), bf16),
        VMEM,
        [VMEM, VMEM, ANY],
        [],
        cost(flops),
    )(one, two, after)


def second_local(count, side_a, side_b, phase, row, out, wall, phase_wall, first):
    layers, rows, depth = out.shape
    own = layers_of(side_a) + layers_of(side_b)[::-1]
    for d in range(layers):
        clear_margins((first, (d,)))
    held = []

    def emit(d, y, v, stepped):
        out[d, pl.ds(y, CHUNK), :] = stepped
        held.append(v + stepped)
        if len(held) * CHUNK == 128:
            start = y + CHUNK - 128
            wall[d, :, pl.ds(start, 128)] = wall_rows(jnp.concatenate(held), 0)
            phase_wall[d, :, pl.ds(start, 128)] = wall_rows(phase[stored(d, layers), pl.ds(start, 128), :], 0)
            held.clear()

    local_step(own, layers_of(first), phase, row, count, emit)


def make_second_local(side_a, side_b, phase, row, count):
    layers, rows, depth = phase.shape
    return call(
        lambda *refs: second_local(count, *refs),
        (
            jax.ShapeDtypeStruct((layers, rows, depth), f32),
            jax.ShapeDtypeStruct((layers, 8, rows), f32),
            jax.ShapeDtypeStruct((layers, 8, rows), f32),
        ),
        (VMEM,) * 3,
        [VMEM] * 4,
        [padded(rows, depth, layers)],
        cost(13 * 10**8),
    )(side_a, side_b, phase, row)


def injection(n, phase, pre, *refs):
    sources, (out, index, rhs) = refs[:-3], refs[-3:]
    layers, rows, depth = out.shape
    position = lax.axis_index("slab").astype(f32)
    rhs[:, :depth] = jnp.ones((rhs.shape[0], depth), bf16)
    at = 0
    for source in sources:
        for first in range(0, source.shape[0], n + 16):
            rhs[pl.ds(at, n), depth:] = source[pl.ds(first, n), :]
            digits = source[pl.ds(first + n, 16), :].astype(f32)
            cell = jnp.where(digits[0:1] == position, digits[1:2] * 256.0 + digits[2:3], -1.0)
            index[0:1, pl.ds(at, n)] = cell[:, :n].astype(jnp.int32)
            at += n
    for d in range(layers):
        at = stored(d, layers)
        for y in range(0, rows, 128):
            cell = lax.broadcasted_iota(jnp.int32, (128, index.shape[1]), 0) + (at * rows + y)
            here = jnp.where(cell == index[0:1, :], 1.0, 0.0).astype(bf16)
            added = jnp.dot(here, rhs[...], preferred_element_type=f32)
            p = phase[at, pl.ds(y, 128), :].astype(f32)
            out[d, pl.ds(y, 128), :] = pre[d, pl.ds(y, 128), :] + (added[:, :depth] * p - added[:, depth:])


def make_injection(phase, n, pre, sources):
    layers, rows, depth = phase.shape
    total = sum(r.shape[0] // (n + 16) * n for r in sources)
    return call(
        lambda *refs: injection(n, *refs),
        jax.ShapeDtypeStruct((layers, rows, depth), f32),
        VMEM,
        [VMEM, VMEM] + [VMEM] * len(sources),
        [pltpu.VMEM((8, total), jnp.int32), pltpu.VMEM((total, 2 * depth), bf16)],
        cost(1),
    )(phase, pre, *sources)


def unpack_walls(message, out):
    for y in range(0, out.shape[1], 256):
        both = message[pl.ds(y // 16, 16), :].astype(f32)
        both = both[:8] + both[8:]
        for i in range(2):
            out[:4, pl.ds(y + 128 * i, 128)] = both[4 * i : 4 * i + 4]


def wall_kernel(wall, phase_wall, early_a, from_b, mask, after, out, from_a):
    layers = wall.shape[0]
    unpack_walls(early_a, from_a)
    odd = is_odd()
    terms = []
    for d in range(layers):
        p = phase_wall[d, :2, :]
        w = wall[d, :2, :]
        for halo, off in ((from_a, d), (from_b, layers - 1 - d)):
            if off == 0:
                w = w + mobility_step * curvature_of(p) * halo[:2] - stiffness_step * halo[2:4]
            elif off == 1:
                w = w - stiffness_step * halo[:2]
        terms.append((1.0 - p * p) * w)
    for l in range(layers):
        out[:, l, :] = mask[:, l, :] * jnp.where(odd, terms[l], terms[layers - 1 - l])


def make_walls(wall, phase_wall, early_a, from_b, mask, after):
    return call(
        wall_kernel,
        jax.ShapeDtypeStruct(mask.shape, f32),
        VMEM,
        [VMEM] * 5 + [ANY],
        [pltpu.VMEM(wall.shape[1:], f32)],
        cost(3 * 10**8),
    )(wall, phase_wall, early_a, from_b, mask, after)


def layers_at_a(message, phase, state, out, halo):
    layers = state.shape[0]

    def put(d):
        def store(y, v):
            out[d, pl.ds(y, CHUNK), :] = v

        return store

    def get(d):
        return lambda y: state[d, pl.ds(y, CHUNK), :]

    add_halo(message, get(0), get(1), (halo, ()), phase, stored(0, layers), phase.shape[1], put(0), put(1))


def make_layers_at_a(message, phase, state):
    layers, rows, depth = phase.shape
    return call(
        layers_at_a,
        jax.ShapeDtypeStruct((2, rows, depth), f32),
        VMEM,
        [VMEM] * 3,
        [padded(rows, depth)],
        cost(15 * 10**8),
    )(message, phase, state)


def final(at_a, message_b, state, phase, *refs):
    walls, (out, total, planes, summed, halo, sems) = refs[:-6], refs[-6:]
    layers, rows, depth = state.shape
    half = rows // 2
    copies = []

    def send(source, target):
        c = pltpu.make_async_copy(source, target, sems.at[len(copies)])
        c.start()
        copies.append(c)

    for d in range(2):
        send(at_a.at[d], out.at[stored(d, layers)])
    if len(walls) == 4:
        summed[...] = (walls[0][...] + walls[3][...]) + (walls[1][...] + walls[2][...])
    else:
        summed[...] = walls[0][...]
    send(summed, total)

    def put(i):
        def store(y, v):
            planes[i, pl.ds(y, CHUNK), :] = v
            if (y + CHUNK) % half == 0:
                span = pl.ds(y + CHUNK - half, half)
                send(planes.at[i, span], out.at[stored(layers - 1 - i, layers), span])

        return store

    def get(d):
        return lambda y: state[d, pl.ds(y, CHUNK), :]

    one, two = layers - 1, layers - 2
    add_halo(message_b, get(one), get(two), (halo, ()), phase, stored(one, layers), rows, put(0), put(1))
    for c in copies:
        c.wait()


def make_final(at_a, message_b, state, phase, walls):
    layers, rows, depth = state.shape
    return call(
        final,
        (jax.ShapeDtypeStruct(state.shape, f32), jax.ShapeDtypeStruct(walls[0].shape, f32)),
        (ANY, ANY),
        [VMEM] * (4 + len(walls)),
        [
            pltpu.VMEM((2, rows, depth), f32),
            pltpu.VMEM(walls[0].shape, f32),
            padded(rows, depth),
            pltpu.SemaphoreType.DMA((7,)),
        ],
        cost(1),
    )(at_a, message_b, state, phase, *walls)


def on_device(adjoint, phase, targets, owners, target_cell, rate_index, inflow_rates, wall_mask):
    state, phase, targets = adjoint[0], phase[0], targets[0]
    owners = owners.reshape(target_cell.shape)
    count = lax.axis_size("slab")
    pairs = (
        [(i, i ^ 1) for i in range(count) if i ^ 1 < count],
        [(i, i + 1) for i in range(1, count - 1, 2)] + [(i + 1, i) for i in range(1, count - 1, 2)],
    )

    def send(v, side):
        return lax.ppermute(v, "slab", pairs[side])

    rows, n = state.shape[1], targets.shape[0]
    few = count == 8
    first, rates = make_first_message(state, targets, owners, target_cell, inflow_rates[None])
    from_a = send(first, 0)
    pre, message, row, mask, near_walls = make_first_local(state, phase, rates, rate_index, wall_mask, first, count)
    from_b = send(message, 1)
    half_a, message, early, pair = make_middle_a(from_a, pre, phase, first)
    early = send(early, 0)
    later_a = send(message, 0)
    four = far = pair
    if few:
        four = make_join(pair, lax.ppermute(pair, "slab", [(i, i ^ 4) for i in range(count)]), pair, 15 * 10**8)
        far = lax.ppermute(four, "slab", [(i, i ^ 2) for i in range(count)])
    half_b, message, walls_b = make_middle_b(from_b, pre, phase, near_walls, four, count)
    later_b = send(message, 1)
    pre, wall, phase_wall = make_second_local(half_a, half_b, phase, row, count)
    block = make_join(four, far, wall, 1)
    if not few:
        block = lax.all_gather(first[2 * state.shape[1] :], "slab", axis=0, tiled=True)
    part = make_walls(wall, phase_wall, early, walls_b, mask, block)
    if lax.axis_size("cond") == 4:
        walls = [part] + [lax.ppermute(part, "cond", [(i, i ^ k) for i in range(4)]) for k in (3, 2, 1)]
    else:
        walls = [lax.psum(part, "cond")]
    state = make_injection(phase, n, pre, [block])
    at_a = make_layers_at_a(later_a, phase, state)
    out, wall_gradient = make_final(at_a, later_b, state, phase, walls)
    return out[None], wall_gradient


def solution(mesh):
    in_specs = (
        P("cond", "slab", None, None),
        P("cond", "slab", None, None),
        P("cond", "slab", None),
        P("cond", "slab", None),
        P("cond", "slab"),
        P("cond"),
        P(),
        P(None, "slab", None),
    )
    out_specs = (P("cond", "slab", None, None), P(None, "slab", None))
    return jax.shard_map(
        on_device, mesh=mesh, in_specs=in_specs, out_specs=out_specs, check_vma=False
    )
```
